256 devices in a mesh: mp: 8 (over z), fsdp: 32 (over y, x, core).
Axes of the slice: x: 4, y: 4, z: 8, core: 2. Of those that a mesh axis runs over, the one named last changes fastest.
Arguments:
- wide_momentum: float32 [2, 8192, 8192], P(None, 'mp', 'fsdp'), may hold values from -6 to 6
- wide_grad: bfloat16 [2, 8192, 8192], P(None, 'mp', 'fsdp'), may hold values from -6 to 6
- wide_basis: float32 [2, 8192, 256], P(None, 'fsdp'), may hold values from -0.0625 to 0.0625
- narrow_momentum: float32 [2, 1024, 8192], P(None, 'mp', 'fsdp'), may hold values from -6 to 6
- narrow_grad: bfloat16 [2, 1024, 8192], P(None, 'mp', 'fsdp'), may hold values from -6 to 6
- narrow_basis: float32 [2, 8192, 256], P(None, 'fsdp'), may hold values from -0.0625 to 0.0625
Outputs:
- wide_momentum_out: float32 [2, 8192, 8192], P(None, 'mp', 'fsdp')
- wide_basis_out: float32 [2, 8192, 256], P(None, 'fsdp')
- wide_update: bfloat16 [2, 8192, 8192], P(None, 'mp', 'fsdp')
- narrow_momentum_out: float32 [2, 1024, 8192], P(None, 'mp', 'fsdp')
- narrow_basis_out: float32 [2, 8192, 256], P(None, 'fsdp')
- narrow_update: bfloat16 [2, 1024, 8192], P(None, 'mp', 'fsdp')
The draws below stay inside these ranges and needn't reach their ends.
All inputs are finite; a program needn't handle non-finite values.
Results may differ from the reference program's by a relative error of at most 0.0015.
Values sent between devices are 32-bit elements; how exact they have to be, the bound alone decides.
A program may use at most 64 MiB of HBM per device.

```python
import jax
import jax.numpy as jnp
from jax import lax

D = 8192
KVW = 1024
RANK = 256


def steps_of(key, shape, pieces, least, largest):
    factor_of, own = 1.0, jax.random.fold_in(key, 6)
    for position, parts in pieces:
        heights = jnp.exp(jax.random.uniform(jax.random.fold_in(own, position), (parts,), jnp.float32, least / len(pieces), largest / len(pieces)))
        factor_of = factor_of * jnp.repeat(heights, shape[position] // parts).reshape([-1 if axis == position else 1 for axis in range(len(shape))])
    return factor_of


def bell_draw(rng, extent, width, limit, split=(), held_as=jnp.bfloat16):
    values = width * jax.random.normal(rng, extent, jnp.float32)
    if split:
        values = values * steps_of(rng, extent, split, -0.22, 0.18)
    return jnp.clip(values, -limit, limit).astype(held_as)


def setup_inputs(seed: int = 0) -> dict:
    streams_of = jax.random.split(jax.random.key(seed), 7)
    wide_momentum = bell_draw(streams_of[0], (2, D, D), 1.0, 6.0, ((1, 8), (2, 32)), jnp.float32)
    wide_grad = bell_draw(streams_of[1], (2, D, D), 1.0, 6.0, ((1, 8), (2, 32)))
    wide_basis = bell_draw(streams_of[2], (2, D, RANK), D ** -0.5, 0.0625, ((1, 32),), jnp.float32)
    narrow_momentum = bell_draw(streams_of[3], (2, KVW, D), 1.0, 6.0, ((1, 8), (2, 32)), jnp.float32)
    narrow_grad = bell_draw(streams_of[4], (2, KVW, D), 1.0, 6.0, ((1, 8), (2, 32)))
    narrow_basis = bell_draw(streams_of[5], (2, D, RANK), D ** -0.5, 0.0625, ((1, 32),), jnp.float32)
    return {"wide_momentum": wide_momentum, "wide_grad": wide_grad, "wide_basis": wide_basis, "narrow_momentum": narrow_momentum, "narrow_grad": narrow_grad, "narrow_basis": narrow_basis}


EXACT_ARITHMETIC = lax.Precision.HIGHEST

def right_inverse(lower, mapped_lines):
    solved = jax.vmap(lambda tri, rhs: jax.scipy.linalg.solve_triangular(tri, rhs, lower=True))(lower, jnp.swapaxes(mapped_lines, 1, 2))
    return jnp.swapaxes(solved, 1, 2)

def dion_step(momentum, grad, right_factor, update_scale):
    velocity_store = momentum + grad.astype(jnp.float32)
    unscaled_update = jnp.einsum('klc,kcq->klq', velocity_store, right_factor, precision=EXACT_ARITHMETIC)
    gram_matrix = jnp.einsum('xik,xih->xkh', unscaled_update, unscaled_update, precision=EXACT_ARITHMETIC)
    lower = jnp.linalg.cholesky(gram_matrix)
    unit_basis_lines = right_inverse(lower, unscaled_update)
    triangular_root = jnp.einsum('jms,jmu->jsu', velocity_store, unit_basis_lines, precision=EXACT_ARITHMETIC)
    inner_product_table = lax.optimization_barrier(jnp.sum(triangular_root * triangular_root, axis=1))
    next_right_factor = triangular_root * lax.rsqrt(inner_product_table + 1e-06)[:, None, :]
    next_momentum = velocity_store - 0.05 * jnp.einsum('ocd,old->ocl', unit_basis_lines, triangular_root, precision=EXACT_ARITHMETIC)
    weight_update = (update_scale * jnp.einsum('ocd,old->ocl', unit_basis_lines, next_right_factor, precision=EXACT_ARITHMETIC)).astype(jnp.bfloat16)
    return (next_momentum, next_right_factor, weight_update)

def reference(wide_momentum, wide_grad, wide_basis, narrow_momentum, narrow_grad, narrow_basis):
    wide_scale = (D * D / RANK) ** 0.5
    narrow_scale = (KVW * D / RANK) ** 0.5
    wide_mom, wide_new, wide_upd = dion_step(wide_momentum, wide_grad, wide_basis, wide_scale)
    narrow_mom, narrow_new, narrow_upd = dion_step(narrow_momentum, narrow_grad, narrow_basis, narrow_scale)
    return (wide_mom, wide_new, wide_upd, narrow_mom, narrow_new, narrow_upd)
```

```python
import functools

import jax
import jax.numpy as jnp
from jax import lax
from jax.experimental import pallas as pl
from jax.experimental.pallas import tpu as pltpu
from jax.sharding import PartitionSpec as P

D = 8192
KVW = 1024
RANK = 256
WIDE = 1024
NARROW = 128
COLS = 256
HALF = WIDE + NARROW
F32 = jnp.float32
BF16 = jnp.bfloat16
MESH = pl.DeviceIdType.MESH
EXACT = lax.Precision.HIGHEST

NN = (((1,), (0,)), ((), ()))
NT = (((1,), (1,)), ((), ()))
TN = (((0,), (0,)), ((), ()))


def exact_dot(a, b, dims=NN):
    return lax.dot_general(a, b, dims, precision=EXACT, preferred_element_type=F32)


def split(a):
    high = a.astype(BF16)
    return high, (a - high.astype(F32)).astype(BF16)


def bf16_dot(a, b, dims=NN):
    return lax.dot_general(a, b, dims, preferred_element_type=F32)


class Links:
    def __init__(self, send, recv):
        self.send, self.recv = send, recv
        self.count = 0
        self.started = []

    def start(self, src, dst, device):
        i = self.count
        self.count += 1
        copy = pltpu.make_async_remote_copy(
            src_ref=src,
            dst_ref=dst,
            send_sem=self.send.at[i],
            recv_sem=self.recv.at[i],
            device_id=device,
            device_id_type=MESH,
        )
        copy.start()
        self.started.append(copy)
        return copy

    def finish(self):
        for copy in self.started:
            copy.wait_send()


def ring_reduce(links, buf, out, h, base, chunk, cut, q, right, left, land):
    after, before = (q + 1) % 4, (q + 3) % 4

    def rows(c, lo, n):
        return pl.ds(pl.multiple_of(base + c * chunk + lo, 8), n)

    far = (q + 2) % 4
    a = links.start(buf.at[h, rows(far, 0, cut)], land.at[0, pl.ds(0, cut)], right)
    b = links.start(
        buf.at[h, rows(far, cut, chunk - cut)], land.at[1, pl.ds(0, chunk - cut)], left
    )
    yield
    a.wait_recv()
    buf[h, rows(after, 0, cut), :] += land[0, 0:cut, :]
    a = links.start(buf.at[h, rows(after, 0, chunk)], land.at[2, pl.ds(0, chunk)], right)
    b.wait_recv()
    buf[h, rows(before, cut, chunk - cut), :] += land[1, 0 : chunk - cut, :]
    b = links.start(buf.at[h, rows(before, 0, chunk)], land.at[3, pl.ds(0, chunk)], left)
    yield
    a.wait_recv()
    b.wait_recv()
    out[h, rows(q, 0, chunk), :] = (
        buf[h, rows(q, 0, chunk), :] + land[2, 0:chunk, :] + land[3, 0:chunk, :]
    )


def ring_gather(links, buf, h, base, chunk, cut, q, right, left):
    after, before = (q + 1) % 4, (q + 3) % 4

    def part(c, lo, n):
        return buf.at[h, pl.ds(pl.multiple_of(base + c * chunk + lo, 8), n)]

    own = part(q, 0, chunk)
    a = links.start(own, own, right)
    b = links.start(own, own, left)
    yield
    a.wait_recv()
    piece = part(before, 0, cut)
    a = links.start(piece, piece, right)
    b.wait_recv()
    piece = part(after, cut, chunk - cut)
    b = links.start(piece, piece, left)
    yield
    a.wait_recv()
    b.wait_recv()


def z_reduce_gather(links, buf, out, land, q, right, left):
    def chunk(ref, c):
        return ref.at[c % 8]

    def part(ref, c, lo):
        return ref.at[c % 8, pl.ds(lo, 64)]

    a = links.start(part(buf, q + 4, 0), land.at[0, 0, pl.ds(0, 64)], right)
    b = links.start(part(buf, q + 4, 64), land.at[1, 0, pl.ds(64, 64)], left)
    yield
    a.wait_recv()
    buf[(q + 3) % 8, 0:64, :] += land[0, 0, 0:64, :]
    a = links.start(chunk(buf, q + 3), land.at[0, 1], right)
    b.wait_recv()
    buf[(q + 5) % 8, 64:128, :] += land[1, 0, 64:128, :]
    b = links.start(chunk(buf, q + 5), land.at[1, 1], left)
    yield
    for s in (2, 3):
        a.wait_recv()
        buf[(q + 4 - s) % 8] += land[0, s - 1]
        a = links.start(chunk(buf, q + 4 - s), land.at[0, s], right)
        b.wait_recv()
        buf[(q + 4 + s) % 8] += land[1, s - 1]
        b = links.start(chunk(buf, q + 4 + s), land.at[1, s], left)
        yield
    a.wait_recv()
    b.wait_recv()
    out[q] = buf[q] + land[0, 3] + land[1, 3]
    a = links.start(chunk(out, q), chunk(out, q), right)
    b = links.start(chunk(out, q), chunk(out, q), left)
    yield
    for s in (1, 2):
        a.wait_recv()
        a = links.start(chunk(out, q + 8 - s), chunk(out, q + 8 - s), right)
        b.wait_recv()
        b = links.start(chunk(out, q + s), chunk(out, q + s), left)
        yield
    a.wait_recv()
    a = links.start(part(out, q + 5, 0), part(out, q + 5, 0), right)
    b.wait_recv()
    b = links.start(part(out, q + 3, 64), part(out, q + 3, 64), left)
    yield
    a.wait_recv()
    b.wait_recv()


def together(*stages):
    done = object()
    live = list(stages)
    while live:
        live = [s for s in live if next(s, done) is not done]


def block_inverse(e):
    lane = lax.broadcasted_iota(jnp.int32, (8, 128), 1)
    sub = lax.broadcasted_iota(jnp.int32, (8, 128), 0)
    group = (lane // 64) * 64

    def pick(tile, index):
        return jnp.take_along_axis(tile, group + index, axis=1)

    e = list(e)
    for g in range(4):
        cols = [[pick(e[i], 8 * g + t) for i in range(g, 4)] for t in range(8)]
        for t in range(8):
            inv = 1.0 / cols[t][0][t : t + 1, :]
            for n, i in enumerate(range(g, 4)):
                f = cols[t][n] * inv
                if n == 0:
                    f = jnp.where(sub > t, f, 0.0)
                e[i] = e[i] - f * e[g][t : t + 1, :]
                for s in range(t + 1, 8):
                    cols[s][n] = cols[s][n] - f * cols[s][0][t : t + 1, :]
    return [tile * lax.rsqrt(pick(tile, 8 * i + sub)) for i, tile in enumerate(e)]


def factor_block(a_ref, k):
    lane = lax.broadcasted_iota(jnp.int32, (32, 128), 1)
    row = lax.broadcasted_iota(jnp.int32, (32, 128), 0)
    eye = jnp.where(lane % 32 == row, 1.0, 0.0)
    d0 = a_ref[0, 0:32, 0:128]
    d1 = pltpu.roll(a_ref[1, 0:32, 0:128], 64, 1)
    e = jnp.where(
        lane < 32, d0, jnp.where((lane >= 64) & (lane < 96), d1, eye)
    )
    e = jnp.concatenate(block_inverse([e[8 * i : 8 * i + 8] for i in range(4)]), axis=0)
    col = lax.broadcasted_iota(jnp.int32, (32, 256), 1)
    wide_row = lax.broadcasted_iota(jnp.int32, (32, 256), 0)
    wide_eye = jnp.where(col == wide_row, 1.0, 0.0)
    for m in range(2):
        t = pltpu.roll(e, 96 - 64 * m, 1)[:, 0:32]
        panel = exact_dot(t, jnp.where(col < 32, wide_eye, a_ref[m, 0:32, :]))
        u = jnp.where((col >= 32) & (col < 256 - 32 * k), panel, 0.0)
        change = exact_dot(u, panel, TN)
        rest = lax.broadcasted_iota(jnp.int32, (224, 256), 1)
        rest = jnp.where(rest < 32, 0.0, a_ref[m, 32:256, :]) - change[32:256, :]
        a_ref[m, 0:224, :] = pltpu.roll(rest, 224, 1)
        a_ref[m, 224:256, :] = pltpu.roll(panel, 224, 1)


def main_kernel(
    wm, wg, wb, nm, ng, nb,
    ow, on, fac, sq,
    buf, part, full, swap, land_a, land_b, gram, slices, zland, gathered,
    wpart, wfull, wland, inverse, sq_a, sq_x, sq_y,
    send, recv,
):
    z = lax.axis_index("mp")
    f = lax.axis_index("fsdp")
    c = f % 2
    x = (f // 2) % 4
    y = f // 8

    def plane(xx, yy, cc):
        return {"fsdp": ((yy % 4) * 4 + xx % 4) * 2 + cc}

    sibling = plane(x, y, 1 - c)
    xs = [plane(x + d, y, c) for d in (1, 2, 3)]
    ys = [plane(x, y + d, c) for d in (1, 2, 3)]
    zs = [{"mp": (z + d) % 8} for d in range(1, 8)]

    barrier = pltpu.get_barrier_semaphore()
    partners = [sibling] + xs + ys + zs
    for device in partners:
        pl.semaphore_signal(barrier, inc=1, device_id=device, device_id_type=MESH)
    pl.semaphore_wait(barrier, len(partners))

    links = Links(send, recv)

    def raw_half(cc):
        base = cc * HALF

        def tile(r, n, moment, grad, basis):
            b = moment + grad.astype(F32)
            rows = pl.ds(pl.multiple_of(base + r, 8), n)
            buf[rows, :] = b
            raw = exact_dot(b, basis)
            part[0, rows, :] = raw[:, 0:128]
            part[1, rows, :] = raw[:, 128:256]

        @pl.loop(0, WIDE // 256)
        def _(i):
            rows = pl.ds(pl.multiple_of(i * 256, 256), 256)
            tile(i * 256, 256, wm[cc, rows, :], wg[cc, rows, :], wb[cc])

        tile(WIDE, NARROW, nm[cc], ng[cc], nb[cc])

    raw_half(1 - c)
    other = pl.ds(pl.multiple_of((1 - c) * HALF, 8), HALF)
    mine = pl.ds(pl.multiple_of(c * HALF, 8), HALF)
    exchange = links.start(part.at[:, other], swap, sibling)
    raw_half(c)
    exchange.wait_recv()
    part[:, mine, :] += swap[...]

    x_ring = dict(q=x, right=xs[0], left=xs[2])
    y_ring = dict(q=y, right=ys[0], left=ys[2])
    base = c * HALF
    big, small = HALF // 4, HALF // 16

    def reduce_both(h, first, second, land):
        yield from ring_reduce(
            links, part, part, h, base, big, 144, land=land.at[0], **first
        )
        yield from ring_reduce(
            links, part, full, h, base + first["q"] * big, small, 40, land=land.at[1], **second
        )

    def gather_both(buffer, h, start, sizes, cuts, first, second):
        yield from ring_gather(
            links, buffer, h, start + first["q"] * sizes[0], sizes[1], cuts[1], **second
        )
        yield from ring_gather(links, buffer, h, start, sizes[0], cuts[0], **first)

    together(reduce_both(0, x_ring, y_ring, land_a), reduce_both(1, y_ring, x_ring, land_b))
    together(
        gather_both(full, 0, base, (big, small), (144, 40), x_ring, y_ring),
        gather_both(full, 1, base, (big, small), (144, 40), y_ring, x_ring),
    )
    exchange = links.start(full.at[:, mine], full.at[:, mine], sibling)

    def raw_rows(start, n):
        rows = pl.ds(pl.multiple_of(start, 8), n)
        return jnp.concatenate([full[0, rows, :], full[1, rows, :]], axis=1)

    for kind, (start, n) in enumerate(((0, WIDE), (WIDE, NARROW))):
        raw = raw_rows(base + start, n)
        gram[kind] = exact_dot(raw, raw, TN)
    places = (x * 4 + y, y * 4 + x)
    for t in range(8):
        h, m, r = t // 4, (t // 2) % 2, t % 2
        rows = pl.ds(pl.multiple_of(places[h] * 16 + r * 8, 8), 8)
        slices[t] = gram[m, rows, h * 128 : h * 128 + 128]
    gram_sends = [
        links.start(slices.at[(z + d) % 8], zland.at[d - 1], zs[d - 1]) for d in range(1, 8)
    ]

    exchange.wait_recv()
    for m in range(4):
        start, n = ((0, WIDE), (HALF, WIDE), (WIDE, NARROW), (HALF + WIDE, NARROW))[m]
        w = exact_dot(buf[start : start + n, :], raw_rows(start, n), TN)
        for k in range(8):
            wpart[k, m * 32 : m * 32 + 32, :] = w[k * 32 : k * 32 + 32, :]
    w_sum = z_reduce_gather(links, wpart, wfull, wland, z, zs[0], zs[6])
    next(w_sum)

    for copy in gram_sends:
        copy.wait_recv()
    total = slices[z]
    for d in range(7):
        total = total + zland[d]
    place = places[0] + (z // 4) * (places[1] - places[0])
    own = gathered.at[z // 4, pl.ds(pl.multiple_of(place * 32 + (z % 4) * 8, 8), 8)]
    own[...] = total
    gram_sends = [links.start(own, own, zs[d]) for d in range(7)]
    next(w_sum)
    for copy in gram_sends:
        copy.wait_recv()
    together(
        gather_both(gathered, 0, 0, (128, 32), (64, 16), x_ring, y_ring),
        gather_both(gathered, 1, 0, (128, 32), (64, 16), y_ring, x_ring),
    )
    for h in range(2):
        for p in range(16):
            for m in range(2):
                gram[m, p * 16 : p * 16 + 16, h * 128 : h * 128 + 128] = gathered[
                    h, p * 32 + m * 16 : p * 32 + m * 16 + 16, :
                ]

    for k in range(0, 8, 2):
        lax.fori_loop(k, k + 2, lambda i, _: factor_block(gram, i), None)
        next(w_sum, None)
    inverse[c] = gram[...]
    exchange = links.start(inverse.at[c], inverse.at[c], sibling)
    for _ in w_sum:
        pass
    exchange.wait_recv()

    for m in range(4):
        w = jnp.concatenate([wfull[k, m * 32 : m * 32 + 32, :] for k in range(8)], axis=0)
        factor = exact_dot(w, inverse[m % 2, m // 2], NT)
        fac[m] = factor
        squares = jnp.sum(factor * factor, axis=0, keepdims=True)
        for h in range(2):
            row = 2 * m + h
            sq[row : row + 1, :] = squares[:, h * 128 : h * 128 + 128]
    sq_a[0] = sq[...]
    exchange = links.start(sq_a.at[0], sq_a.at[1], sibling)

    def ortho_half(cc):
        start = cc * HALF
        for m, (lo, n) in enumerate(((0, WIDE), (WIDE, NARROW))):
            o = exact_dot(raw_rows(start + lo, n), inverse[cc, m], NT)
            if m == 0:
                ow[cc] = o
            else:
                on[cc] = o

    exchange.wait_recv()
    sq_x[0] = sq_a[0] + sq_a[1]
    sends = [links.start(sq_x.at[0], sq_x.at[d + 1], xs[d]) for d in range(3)]
    ortho_half(0)
    for copy in sends:
        copy.wait_recv()
    sq_y[0] = sq_x[0] + sq_x[1] + sq_x[2] + sq_x[3]
    sends = [links.start(sq_y.at[0], sq_y.at[d + 1], ys[d]) for d in range(3)]
    ortho_half(1)
    for copy in sends:
        copy.wait_recv()
    sq[...] = sq_y[0] + sq_y[1] + sq_y[2] + sq_y[3]
    links.finish()


def last_kernel(wm, wg, nm, ng, ow, on, fac, sq, wmo, wbo, wup, nmo, nbo, nup):
    for kind, (moment, grad, ortho, m_out, b_out, update, rows) in enumerate(
        ((wm, wg, ow, wmo, wbo, wup, D), (nm, ng, on, nmo, nbo, nup, KVW))
    ):
        factor = fac[kind, 0]
        basis = factor * lax.rsqrt(sq[kind, 0] + 1e-6)
        b_out[0] = basis
        o_high, o_low = split(ortho[0])
        b_high, b_low = split(basis)
        m_out[0] = (
            moment[0]
            + grad[0].astype(F32)
            - 0.05 * bf16_dot(o_high, factor.astype(BF16), NT)
        )
        product = bf16_dot(o_high, b_high, NT) + (
            bf16_dot(o_high, b_low, NT) + bf16_dot(o_low, b_high, NT)
        )
        update[0] = ((rows * D / RANK) ** 0.5 * product).astype(BF16)


def local(wide_momentum, wide_grad, wide_basis, narrow_momentum, narrow_grad, narrow_basis):
    vmem = pl.BlockSpec(memory_space=pltpu.VMEM)
    copies = 128
    ow, on, fac, sq = pl.pallas_call(
        main_kernel,
        out_shape=(
            jax.ShapeDtypeStruct((2, WIDE, RANK), F32),
            jax.ShapeDtypeStruct((2, NARROW, RANK), F32),
            jax.ShapeDtypeStruct((4, COLS, RANK), F32),
            jax.ShapeDtypeStruct((8, 128), F32),
        ),
        in_specs=[vmem] * 6,
        out_specs=[vmem] * 4,
        scratch_shapes=[
            pltpu.VMEM((2 * HALF, COLS), F32),
            pltpu.VMEM((2, 2 * HALF, 128), F32),
            pltpu.VMEM((2, 2 * HALF, 128), F32),
            pltpu.VMEM((2, HALF, 128), F32),
            pltpu.VMEM((2, 4, HALF // 4, 128), F32),
            pltpu.VMEM((2, 4, HALF // 4, 128), F32),
            pltpu.VMEM((2, RANK, RANK), F32),
            pltpu.VMEM((8, 8, 128), F32),
            pltpu.VMEM((7, 8, 128), F32),
            pltpu.VMEM((2, 512, 128), F32),
            pltpu.VMEM((8, 128, RANK), F32),
            pltpu.VMEM((8, 128, RANK), F32),
            pltpu.VMEM((2, 4, 128, RANK), F32),
            pltpu.VMEM((2, 2, RANK, RANK), F32),
            pltpu.VMEM((2, 8, 128), F32),
            pltpu.VMEM((4, 8, 128), F32),
            pltpu.VMEM((4, 8, 128), F32),
            pltpu.SemaphoreType.DMA((copies,)),
            pltpu.SemaphoreType.DMA((copies,)),
        ],
        compiler_params=pltpu.CompilerParams(
            collective_id=0, has_side_effects=True, vmem_limit_bytes=48 * 2**20
        ),
    )(wide_momentum, wide_grad, wide_basis, narrow_momentum, narrow_grad, narrow_basis)

    def rows(n):
        return pl.BlockSpec((1, n, COLS), lambda m, i: (m, i, 0))

    def whole(*lead):
        return pl.BlockSpec(lead, lambda m, i: (0, m, 0, 0))

    basis_out = pl.BlockSpec((1, COLS, RANK), lambda m, i: (m, 0, 0))
    steps = 4
    w, n = WIDE // steps, NARROW // steps
    return pl.pallas_call(
        last_kernel,
        grid=(2, steps),
        out_shape=(
            jax.ShapeDtypeStruct((2, WIDE, COLS), F32),
            jax.ShapeDtypeStruct((2, COLS, RANK), F32),
            jax.ShapeDtypeStruct((2, WIDE, COLS), BF16),
            jax.ShapeDtypeStruct((2, NARROW, COLS), F32),
            jax.ShapeDtypeStruct((2, COLS, RANK), F32),
            jax.ShapeDtypeStruct((2, NARROW, COLS), BF16),
        ),
        in_specs=[
            rows(w), rows(w), rows(n), rows(n), rows(w), rows(n),
            whole(2, 1, COLS, RANK), whole(2, 1, 1, RANK),
        ],
        out_specs=[rows(w), basis_out, rows(w), rows(n), basis_out, rows(n)],
        compiler_params=pltpu.CompilerParams(vmem_limit_bytes=32 * 2**20),
    )(
        wide_momentum, wide_grad, narrow_momentum, narrow_grad, ow, on,
        fac.reshape(2, 2, COLS, RANK), sq.reshape(2, 2, 1, RANK),
    )


def solution(mesh):
    return jax.shard_map(
        local,
        mesh=mesh,
        in_specs=(
            P(None, "mp", "fsdp"),
            P(None, "mp", "fsdp"),
            P(None, "fsdp", None),
            P(None, "mp", "fsdp"),
            P(None, "mp", "fsdp"),
            P(None, "fsdp", None),
        ),
        out_specs=(
            P(None, "mp", "fsdp"),
            P(None, "fsdp", None),
            P(None, "mp", "fsdp"),
            P(None, "mp", "fsdp"),
            P(None, "fsdp", None),
            P(None, "mp", "fsdp"),
        ),
        check_vma=False,
    )
```

```python
import jax
import jax.numpy as jnp
from jax import lax
from jax.experimental import pallas as pl
from jax.experimental.pallas import tpu as pltpu
from jax.sharding import PartitionSpec as P

D = 8192
KVW = 1024
RANK = 256
WIDE = 1024
NARROW = 128
COLS = 256
HALF = WIDE + NARROW
F32 = jnp.float32
BF16 = jnp.bfloat16
MESH = pl.DeviceIdType.MESH
EXACT = lax.Precision.HIGHEST

NN = (((1,), (0,)), ((), ()))
NT = (((1,), (1,)), ((), ()))
TN = (((0,), (0,)), ((), ()))


def exact_dot(a, b, dims=NN):
    return lax.dot_general(a, b, dims, precision=EXACT, preferred_element_type=F32)


def split(a):
    high = a.astype(BF16)
    return high, (a - high.astype(F32)).astype(BF16)


def bf16_dot(a, b, dims=NN):
    return lax.dot_general(a, b, dims, preferred_element_type=F32)


class Links:
    def __init__(self, send, recv):
        self.send, self.recv = send, recv
        self.count = 0
        self.started = []

    def start(self, src, dst, device):
        i = self.count
        self.count += 1
        copy = pltpu.make_async_remote_copy(
            src_ref=src,
            dst_ref=dst,
            send_sem=self.send.at[i],
            recv_sem=self.recv.at[i],
            device_id=device,
            device_id_type=MESH,
        )
        copy.start()
        self.started.append(copy)
        return copy

    def finish(self):
        for copy in self.started:
            copy.wait_send()


def ring_reduce(links, buf, out, h, base, chunk, cut, q, right, left, land):
    after, before = (q + 1) % 4, (q + 3) % 4

    def rows(c, lo, n):
        return pl.ds(pl.multiple_of(base + c * chunk + lo, 8), n)

    far = (q + 2) % 4
    a = links.start(buf.at[h, rows(far, 0, cut)], land.at[0, pl.ds(0, cut)], right)
    b = links.start(
        buf.at[h, rows(far, cut, chunk - cut)], land.at[1, pl.ds(0, chunk - cut)], left
    )
    yield
    a.wait_recv()
    buf[h, rows(after, 0, cut), :] += land[0, 0:cut, :]
    a = links.start(buf.at[h, rows(after, 0, chunk)], land.at[2, pl.ds(0, chunk)], right)
    b.wait_recv()
    buf[h, rows(before, cut, chunk - cut), :] += land[1, 0 : chunk - cut, :]
    b = links.start(buf.at[h, rows(before, 0, chunk)], land.at[3, pl.ds(0, chunk)], left)
    yield
    a.wait_recv()
    b.wait_recv()
    out[h, rows(q, 0, chunk), :] = (
        buf[h, rows(q, 0, chunk), :] + land[2, 0:chunk, :] + land[3, 0:chunk, :]
    )


def ring_gather(links, buf, h, base, chunk, cut, q, right, left):
    after, before = (q + 1) % 4, (q + 3) % 4

    def part(c, lo, n):
        return buf.at[h, pl.ds(pl.multiple_of(base + c * chunk + lo, 8), n)]

    own = part(q, 0, chunk)
    a = links.start(own, own, right)
    b = links.start(own, own, left)
    yield
    a.wait_recv()
    piece = part(before, 0, cut)
    a = links.start(piece, piece, right)
    b.wait_recv()
    piece = part(after, cut, chunk - cut)
    b = links.start(piece, piece, left)
    yield
    a.wait_recv()
    b.wait_recv()


def z_reduce_gather(links, buf, out, land, lo, n, q, right, left):
    half = n // 2

    def part(ref, i, start, size):
        return ref.at[i, pl.ds(lo + start, size)]

    def chunk(ref, i):
        return part(ref, i % 8, 0, n)

    def add(i, slot, start, size):
        rows = slice(lo + start, lo + start + size)
        buf[i % 8, rows, :] += land[slot[0], slot[1], rows, :]

    a = links.start(
        part(buf, (q + 4) % 8, 0, half), part(land.at[0], 0, 0, half), right
    )
    b = links.start(
        part(buf, (q + 4) % 8, half, half), part(land.at[1], 0, half, half), left
    )
    yield
    for s in (1, 2, 3):
        size = half if s == 1 else n
        a.wait_recv()
        add(q + 4 - s, (0, s - 1), 0, size)
        a = links.start(chunk(buf, q + 4 - s), part(land.at[0], s, 0, n), right)
        b.wait_recv()
        add(q + 4 + s, (1, s - 1), n - size, size)
        b = links.start(chunk(buf, q + 4 + s), part(land.at[1], s, 0, n), left)
        yield
    a.wait_recv()
    b.wait_recv()
    rows = slice(lo, lo + n)
    out[q, rows, :] = buf[q, rows, :] + land[0, 3, rows, :] + land[1, 3, rows, :]
    a = links.start(chunk(out, q), chunk(out, q), right)
    b = links.start(chunk(out, q), chunk(out, q), left)
    yield
    for s in (1, 2):
        a.wait_recv()
        a = links.start(chunk(out, q + 8 - s), chunk(out, q + 8 - s), right)
        b.wait_recv()
        b = links.start(chunk(out, q + s), chunk(out, q + s), left)
        yield
    a.wait_recv()
    piece = part(out, (q + 5) % 8, 0, half)
    a = links.start(piece, piece, right)
    b.wait_recv()
    piece = part(out, (q + 3) % 8, half, half)
    b = links.start(piece, piece, left)
    yield
    a.wait_recv()
    b.wait_recv()


def together(*stages):
    done = object()
    live = list(stages)
    while live:
        live = [s for s in live if next(s, done) is not done]


def block_inverse(e):
    lane = lax.broadcasted_iota(jnp.int32, (8, 128), 1)
    sub = lax.broadcasted_iota(jnp.int32, (8, 128), 0)
    group = (lane // 64) * 64

    def pick(tile, index):
        return jnp.take_along_axis(tile, group + index, axis=1)

    e = list(e)
    for g in range(4):
        cols = [[pick(e[i], 8 * g + t) for i in range(g, 4)] for t in range(8)]
        for t in range(8):
            pivot = cols[t][0][t : t + 1, :]
            inv = pl.reciprocal(pivot, approx=True)
            inv = inv * (2.0 - pivot * inv)
            for n, i in enumerate(range(g, 4)):
                f = cols[t][n] * inv
                if n == 0:
                    f = jnp.where(sub > t, f, 0.0)
                e[i] = e[i] - f * e[g][t : t + 1, :]
                for s in range(t + 1, 8):
                    cols[s][n] = cols[s][n] - f * cols[s][0][t : t + 1, :]
    return [tile * lax.rsqrt(pick(tile, 8 * i + sub)) for i, tile in enumerate(e)]


def factor_block(a_ref, k):
    at = 32 * k
    base = at // 128 * 128
    off = at - base
    lane = lax.broadcasted_iota(jnp.int32, (32, 128), 1)
    row = lax.broadcasted_iota(jnp.int32, (32, 128), 0)
    eye = jnp.where(lane % 32 == row, 1.0, 0.0)

    def turned(v, by):
        return pltpu.roll(v, by % 128, 1) if by % 128 else v

    d0, d1 = (a_ref[m, at : at + 32, base : base + 128] for m in range(2))
    d0, d1 = turned(d0, -off), turned(d1, 64 - off)
    e = jnp.where(lane < 32, d0, jnp.where((lane >= 64) & (lane < 96), d1, eye))
    e = jnp.concatenate(block_inverse([e[8 * i : 8 * i + 8] for i in range(4)]), axis=0)
    col = lax.broadcasted_iota(jnp.int32, (32, 256), 1)
    wide_row = lax.broadcasted_iota(jnp.int32, (32, 256), 0)
    inside = (col >= at) & (col < at + 32)
    wide_eye = jnp.where(col - at == wide_row, 1.0, 0.0)
    below = at + 32
    low = below // 128 * 128
    for m in range(2):
        t = turned(e, 96 - 64 * m)[:, 0:32]
        panel = exact_dot(t, jnp.where(inside, wide_eye, a_ref[m, at : at + 32, :]))
        a_ref[m, at : at + 32, :] = panel
        if below < 256:
            change = exact_dot(panel[:, low:256], panel, TN)
            under = lax.broadcasted_iota(jnp.int32, (256 - below, 256), 1)
            rest = jnp.where(
                (under >= at) & (under < below), 0.0, a_ref[m, below:256, :]
            )
            a_ref[m, below:256, :] = rest - change[below - low :, :]


def main_kernel(
    wm_in, wg_in, wb_in, nm_in, ng_in, nb_in,
    ow_out, on_out, fac_out, sq_out,
    ow, on, fac, sq,
    wm, wg, wb, nm, ng, nb,
    bh, bl, vh, vl, part, full, swap, land, gram, slices, zland, gathered,
    wpart, wfull, wland, inverse, sq_x, sq_y,
    load, store, send, recv,
):
    z = lax.axis_index("mp")
    f = lax.axis_index("fsdp")
    c = f % 2
    x = (f // 2) % 4
    y = f // 8

    loads = []
    for i, cc in enumerate((1 - c, c)):
        pairs = ((wb_in, wb), (wg_in, wg), (wm_in, wm), (nb_in, nb), (ng_in, ng), (nm_in, nm))
        for n, (src, dst) in enumerate(pairs):
            copy = pltpu.make_async_copy(src.at[cc], dst.at[cc], load.at[6 * i + n])
            copy.start()
            loads.append(copy)

    def plane(xx, yy, cc):
        return {"fsdp": ((yy % 4) * 4 + xx % 4) * 2 + cc}

    sibling = plane(x, y, 1 - c)
    xs = [plane(x + d, y, c) for d in (1, 2, 3)]
    xos = [plane(x + d, y, 1 - c) for d in (1, 2, 3)]
    ys = [plane(x, y + d, c) for d in (1, 2, 3)]
    zs = [{"mp": (z + d) % 8} for d in range(1, 8)]

    barrier = pltpu.get_barrier_semaphore()
    partners = [sibling] + xs + xos + ys + zs
    for device in partners:
        pl.semaphore_signal(barrier, inc=1, device_id=device, device_id_type=MESH)

    links = Links(send, recv)
    sets = ((0, 640), (640, 512))
    wide_b = WIDE - 640

    def split_basis(cc):
        for kind, basis in enumerate((wb, nb)):
            high, low = split(basis[cc])
            vh[cc, kind] = high
            vl[cc, kind] = low

    def raw_rows_of(cc, kind, r, n, moment, grad):
        rows = pl.ds(pl.multiple_of(cc * HALF + r, 16), n)
        high, low = split(moment + grad.astype(F32))
        bh[rows, :] = high
        bl[rows, :] = low
        v_high = vh[cc, kind]
        raw = bf16_dot(high, v_high) + (bf16_dot(high, vl[cc, kind]) + bf16_dot(low, v_high))
        part[0, rows, :] = raw[:, 0:128]
        part[1, rows, :] = raw[:, 128:256]

    def raw_set(cc, i):
        lo, n = ((0, 640), (640, wide_b))[i]
        step = 128

        @pl.loop(0, n // step)
        def _(j):
            rows = pl.ds(pl.multiple_of(lo + j * step, step), step)
            raw_rows_of(cc, 0, lo + j * step, step, wm[cc, rows, :], wg[cc, rows, :])

        if i == 1:
            raw_rows_of(cc, 1, WIDE, NARROW, nm[cc], ng[cc])

    def half_rows(cc, start, n):
        return pl.ds(pl.multiple_of(cc * HALF + start, 8), n)

    for copy in loads[0:6]:
        copy.wait()
    split_basis(1 - c)
    raw_set(1 - c, 0)
    pl.semaphore_wait(barrier, len(partners))
    exchanges = []
    for i, (start, n) in enumerate(sets):
        if i == 1:
            raw_set(1 - c, 1)
        exchanges.append(
            links.start(
                part.at[:, half_rows(1 - c, start, n)], swap.at[:, pl.ds(start, n)], sibling
            )
        )
    for copy in loads[6:12]:
        copy.wait()
    split_basis(c)

    x_ring = dict(q=x, right=xs[0], left=xs[2])
    y_ring = dict(q=y, right=ys[0], left=ys[2])
    base = c * HALF

    def gather_both(buffer, h, start, sizes, cuts, first, second):
        yield from ring_gather(
            links, buffer, h, start + first["q"] * sizes[0], sizes[1], cuts[1], **second
        )
        yield from ring_gather(links, buffer, h, start, sizes[0], cuts[0], **first)

    shares = []

    def whole_sum(i, h):
        start, n = sets[i]
        big, small = n // 4, n // 16
        cuts = (big // 2, (small // 16) * 8)
        first, second = (x_ring, y_ring) if h == 0 else (y_ring, x_ring)
        yield from ring_reduce(
            links, part, part, h, base + start, big, cuts[0], land=land.at[i, h, 0], **first
        )
        yield from ring_reduce(
            links, part, full, h, base + start + first["q"] * big, small, cuts[1],
            land=land.at[i, h, 1], **second
        )
        yield from gather_both(full, h, base + start, (big, small), cuts, first, second)
        done = full.at[h, half_rows(c, start, n)]
        shares.append(links.start(done, done, sibling))

    stages = []
    for i, (start, n) in enumerate(sets):
        raw_set(c, i)
        exchanges[i].wait_recv()
        rows = half_rows(c, start, n)
        part[:, rows, :] += swap[:, start : start + n, :]
        for h in range(2):
            stage = whole_sum(i, h)
            next(stage)
            stages.append(stage)
    together(*stages)

    def raw_rows(start, n):
        rows = pl.ds(pl.multiple_of(start, 8), n)
        return jnp.concatenate([full[0, rows, :], full[1, rows, :]], axis=1)

    for kind, (start, n) in enumerate(((0, WIDE), (WIDE, NARROW))):
        raw = raw_rows(base + start, n)
        gram[kind] = exact_dot(raw, raw, TN)
    places = (x * 4 + y, y * 4 + x)
    for t in range(8):
        h, m, r = t // 4, (t // 2) % 2, t % 2
        rows = pl.ds(pl.multiple_of(places[h] * 16 + r * 8, 8), 8)
        slices[t] = gram[m, rows, h * 128 : h * 128 + 128]
    gram_sends = [
        links.start(slices.at[(z + d) % 8], zland.at[d - 1], zs[d - 1]) for d in range(1, 8)
    ]

    def w_of(m):
        start, n = ((0, WIDE), (HALF, WIDE), (WIDE, NARROW), (HALF + WIDE, NARROW))[m]
        high, low = split(raw_rows(start, n))
        b_high = bh[start : start + n, :]
        w = bf16_dot(b_high, high, TN) + (
            bf16_dot(b_high, low, TN) + bf16_dot(bl[start : start + n, :], high, TN)
        )
        for k in range(8):
            wpart[k, m * 32 : m * 32 + 32, :] = w[k * 32 : k * 32 + 32, :]

    def z_chain(i):
        return z_reduce_gather(links, wpart, wfull, wland, 64 * i, 64, z, zs[0], zs[6])

    for copy in shares:
        copy.wait_recv()
    w_of(0)
    w_of(1)
    chains = [z_chain(0)]
    next(chains[0])

    def z_step():
        for chain in chains:
            next(chain, None)

    for copy in gram_sends:
        copy.wait_recv()
    total = slices[z]
    for d in range(7):
        total = total + zland[d]
    place = places[0] + (z // 4) * (places[1] - places[0])
    own = gathered.at[z // 4, pl.ds(pl.multiple_of(place * 32 + (z % 4) * 8, 8), 8)]
    own[...] = total
    gram_sends = [links.start(own, own, zs[d]) for d in range(7)]
    w_of(2)
    w_of(3)
    z_step()
    chains.append(z_chain(1))
    next(chains[1])
    for copy in gram_sends:
        copy.wait_recv()
    stages = [
        gather_both(gathered, 0, 0, (128, 32), (64, 16), x_ring, y_ring),
        gather_both(gathered, 1, 0, (128, 32), (64, 16), y_ring, x_ring),
    ]
    for i in range(5):
        for stage in stages:
            next(stage, None)
        if i in (1, 3):
            z_step()
    for h in range(2):
        for p in range(16):
            for m in range(2):
                gram[m, p * 16 : p * 16 + 16, h * 128 : h * 128 + 128] = gathered[
                    h, p * 32 + m * 16 : p * 32 + m * 16 + 16, :
                ]

    for k in range(8):
        factor_block(gram, k)
        z_step()
    full_row = lax.broadcasted_iota(jnp.int32, (256, 256), 0)
    full_col = lax.broadcasted_iota(jnp.int32, (256, 256), 1)
    for m in range(2):
        inverse[c, m] = jnp.where(full_row >= full_col, gram[m], 0.0)
    exchange = links.start(inverse.at[c], inverse.at[c], sibling)
    for chain in chains:
        for _ in chain:
            pass

    def times_inverse(a, cc, kind):
        i_high, i_low = split(inverse[cc, kind])
        high, low = split(a)
        return bf16_dot(high, i_high, NT) + (
            bf16_dot(high, i_low, NT) + bf16_dot(low, i_high, NT)
        )

    def factor_of(cc, kind):
        rows = pl.ds(pl.multiple_of(kind * 64 + cc * 32, 32), 32)
        w = jnp.concatenate([wfull[k, rows, :] for k in range(8)], axis=0)
        factor = times_inverse(w, cc, kind)
        fac[2 * kind + cc] = factor
        squares = jnp.sum(factor * factor, axis=0, keepdims=True)
        return [squares[:, 0:128], squares[:, 128:256]]

    stores = []

    def put(src, dst):
        copy = pltpu.make_async_copy(src, dst, store.at[len(stores)])
        copy.start()
        stores.append(copy)

    def ortho_half(cc):
        start = cc * HALF
        ow[cc] = times_inverse(raw_rows(start, WIDE), cc, 0)
        put(ow.at[cc], ow_out.at[cc])
        on[cc] = times_inverse(raw_rows(start + WIDE, NARROW), cc, 1)
        put(on.at[cc], on_out.at[cc])

    for kind in range(2):
        for h, squares in enumerate(factor_of(c, kind)):
            row = pl.ds(pl.multiple_of((2 * kind + c) * 2, 2) + h, 1)
            sq[row, :] = squares
    exchange.wait_recv()
    for kind in range(2):
        for h, squares in enumerate(factor_of(1 - c, kind)):
            row = pl.ds(pl.multiple_of((2 * kind + 1 - c) * 2, 2) + h, 1)
            sq[row, :] = squares
    put(fac, fac_out)
    sq_x[0] = sq[...]
    sends = [
        links.start(sq_x.at[0], sq_x.at[d + 1], device)
        for d, device in enumerate([sibling] + xs + xos)
    ]
    ortho_half(c)
    for copy in sends:
        copy.wait_recv()
    total = sq_x[0]
    for d in range(7):
        total = total + sq_x[d + 1]
    sq_y[0] = total
    sends = [links.start(sq_y.at[0], sq_y.at[d + 1], ys[d]) for d in range(3)]
    ortho_half(1 - c)
    for copy in sends:
        copy.wait_recv()
    sq[...] = sq_y[0] + sq_y[1] + sq_y[2] + sq_y[3]
    put(sq, sq_out)
    links.finish()
    for copy in stores:
        copy.wait()


def last_kernel(
    wm, wg, nm, ng, ow, on, fac, sq, wmo, wbo, wup, nmo, nbo, nup, f_t, b_high, b_low
):
    kinds = ((wm, wg, ow, wmo, wbo, wup, D), (nm, ng, on, nmo, nbo, nup, KVW))

    @pl.when(pl.program_id(1) == 0)
    def _():
        for kind in range(2):
            factor = fac[kind, 0]
            basis = factor * lax.rsqrt(sq[kind, 0] + 1e-6)
            kinds[kind][4][0] = basis
            f_t[kind] = factor.astype(BF16).T
            b_high[kind], b_low[kind] = split(basis.T)

    for kind, (moment, grad, ortho, m_out, _, update, rows) in enumerate(kinds):
        o_high, o_low = split(ortho[0])
        m_out[0] = moment[0] + grad[0].astype(F32) - 0.05 * bf16_dot(o_high, f_t[kind])
        product = bf16_dot(o_high, b_high[kind]) + (
            bf16_dot(o_high, b_low[kind]) + bf16_dot(o_low, b_high[kind])
        )
        update[0] = ((rows * D / RANK) ** 0.5 * product).astype(BF16)


def local(wide_momentum, wide_grad, wide_basis, narrow_momentum, narrow_grad, narrow_basis):
    hbm = pl.BlockSpec(memory_space=pltpu.HBM)
    copies = 144
    ow, on, fac, sq = pl.pallas_call(
        main_kernel,
        out_shape=(
            jax.ShapeDtypeStruct((2, WIDE, RANK), F32),
            jax.ShapeDtypeStruct((2, NARROW, RANK), F32),
            jax.ShapeDtypeStruct((4, COLS, RANK), F32),
            jax.ShapeDtypeStruct((8, 128), F32),
        ),
        in_specs=[hbm] * 6,
        out_specs=[hbm] * 4,
        scratch_shapes=[
            pltpu.VMEM((2, WIDE, RANK), F32),
            pltpu.VMEM((2, NARROW, RANK), F32),
            pltpu.VMEM((4, COLS, RANK), F32),
            pltpu.VMEM((8, 128), F32),
            pltpu.VMEM((2, WIDE, COLS), F32),
            pltpu.VMEM((2, WIDE, COLS), BF16),
            pltpu.VMEM((2, COLS, RANK), F32),
            pltpu.VMEM((2, NARROW, COLS), F32),
            pltpu.VMEM((2, NARROW, COLS), BF16),
            pltpu.VMEM((2, COLS, RANK), F32),
            pltpu.VMEM((2 * HALF, COLS), BF16),
            pltpu.VMEM((2 * HALF, COLS), BF16),
            pltpu.VMEM((2, 2, COLS, RANK), BF16),
            pltpu.VMEM((2, 2, COLS, RANK), BF16),
            pltpu.VMEM((2, 2 * HALF, 128), F32),
            pltpu.VMEM((2, 2 * HALF, 128), F32),
            pltpu.VMEM((2, HALF, 128), F32),
            pltpu.VMEM((2, 2, 2, 4, 160, 128), F32),
            pltpu.VMEM((2, RANK, RANK), F32),
            pltpu.VMEM((8, 8, 128), F32),
            pltpu.VMEM((7, 8, 128), F32),
            pltpu.VMEM((2, 512, 128), F32),
            pltpu.VMEM((8, 128, RANK), F32),
            pltpu.VMEM((8, 128, RANK), F32),
            pltpu.VMEM((2, 4, 128, RANK), F32),
            pltpu.VMEM((2, 2, RANK, RANK), F32),
            pltpu.VMEM((8, 8, 128), F32),
            pltpu.VMEM((4, 8, 128), F32),
            pltpu.SemaphoreType.DMA((12,)),
            pltpu.SemaphoreType.DMA((6,)),
            pltpu.SemaphoreType.DMA((copies,)),
            pltpu.SemaphoreType.DMA((copies,)),
        ],
        compiler_params=pltpu.CompilerParams(
            collective_id=0, has_side_effects=True, vmem_limit_bytes=60 * 2**20
        ),
    )(wide_momentum, wide_grad, wide_basis, narrow_momentum, narrow_grad, narrow_basis)

    def rows(n):
        return pl.BlockSpec((1, n, COLS), lambda m, i: (m, i, 0))

    def whole(*lead):
        return pl.BlockSpec(lead, lambda m, i: (0, m, 0, 0))

    basis_out = pl.BlockSpec((1, COLS, RANK), lambda m, i: (m, 0, 0))
    steps = 2
    w, n = WIDE // steps, NARROW // steps
    return pl.pallas_call(
        last_kernel,
        grid=(2, steps),
        out_shape=(
            jax.ShapeDtypeStruct((2, WIDE, COLS), F32),
            jax.ShapeDtypeStruct((2, COLS, RANK), F32),
            jax.ShapeDtypeStruct((2, WIDE, COLS), BF16),
            jax.ShapeDtypeStruct((2, NARROW, COLS), F32),
            jax.ShapeDtypeStruct((2, COLS, RANK), F32),
            jax.ShapeDtypeStruct((2, NARROW, COLS), BF16),
        ),
        in_specs=[
            rows(w), rows(w), rows(n), rows(n), rows(w), rows(n),
            whole(2, 1, COLS, RANK), whole(2, 1, 1, RANK),
        ],
        out_specs=[rows(w), basis_out, rows(w), rows(n), basis_out, rows(n)],
        scratch_shapes=[pltpu.VMEM((2, RANK, COLS), BF16)] * 3,
        compiler_params=pltpu.CompilerParams(vmem_limit_bytes=60 * 2**20),
    )(
        wide_momentum, wide_grad, narrow_momentum, narrow_grad, ow, on,
        fac.reshape(2, 2, COLS, RANK), sq.reshape(2, 2, 1, RANK),
    )


def solution(mesh):
    return jax.shard_map(
        local,
        mesh=mesh,
        in_specs=(
            P(None, "mp", "fsdp"),
            P(None, "mp", "fsdp"),
            P(None, "fsdp", None),
            P(None, "mp", "fsdp"),
            P(None, "mp", "fsdp"),
            P(None, "fsdp", None),
        ),
        out_specs=(
            P(None, "mp", "fsdp"),
            P(None, "fsdp", None),
            P(None, "mp", "fsdp"),
            P(None, "mp", "fsdp"),
            P(None, "fsdp", None),
            P(None, "mp", "fsdp"),
        ),
        check_vma=False,
    )
```

```python
import jax
import jax.numpy as jnp
from jax import lax
from jax.experimental import pallas as pl
from jax.experimental.pallas import tpu as pltpu
from jax.sharding import PartitionSpec as P

D = 8192
KVW = 1024
RANK = 256
WIDE = 1024
NARROW = 128
COLS = 256
HALF = WIDE + NARROW
F32 = jnp.float32
BF16 = jnp.bfloat16
MESH = pl.DeviceIdType.MESH
EXACT = lax.Precision.HIGHEST

NN = (((1,), (0,)), ((), ()))
NT = (((1,), (1,)), ((), ()))
TN = (((0,), (0,)), ((), ()))


def exact_dot(a, b, dims=NN):
    return lax.dot_general(a, b, dims, precision=EXACT, preferred_element_type=F32)


def split(a):
    high = a.astype(BF16)
    return high, (a - high.astype(F32)).astype(BF16)


def bf16_dot(a, b, dims=NN):
    return lax.dot_general(a, b, dims, preferred_element_type=F32)


class Links:
    def __init__(self, send, recv):
        self.send, self.recv = send, recv
        self.count = 0
        self.started = []

    def start(self, src, dst, device):
        i = self.count
        self.count += 1
        copy = pltpu.make_async_remote_copy(
            src_ref=src,
            dst_ref=dst,
            send_sem=self.send.at[i],
            recv_sem=self.recv.at[i],
            device_id=device,
            device_id_type=MESH,
        )
        copy.start()
        self.started.append(copy)
        return copy

    def finish(self, most=None):
        n = len(self.started) if most is None else most
        for copy in self.started[:n]:
            copy.wait_send()
        self.started = self.started[n:]


def ring_reduce(links, buf, out, h, base, chunk, cut, q, peers, land):
    after, before = (q + 1) % 4, (q + 3) % 4
    right, left = peers[0], peers[2]

    def rows(c, lo, n):
        return pl.ds(pl.multiple_of(base + c * chunk + lo, 8), n)

    far = (q + 2) % 4
    a = links.start(buf.at[h, rows(far, 0, cut)], land.at[0, pl.ds(0, cut)], right)
    b = links.start(
        buf.at[h, rows(far, cut, chunk - cut)], land.at[1, pl.ds(0, chunk - cut)], left
    )
    yield
    a.wait_recv()
    buf[h, rows(after, 0, cut), :] += land[0, 0:cut, :]
    a = links.start(buf.at[h, rows(after, 0, chunk)], land.at[2, pl.ds(0, chunk)], right)
    b.wait_recv()
    buf[h, rows(before, cut, chunk - cut), :] += land[1, 0 : chunk - cut, :]
    b = links.start(buf.at[h, rows(before, 0, chunk)], land.at[3, pl.ds(0, chunk)], left)
    yield
    a.wait_recv()
    b.wait_recv()
    out[h, rows(q, 0, chunk), :] = (
        buf[h, rows(q, 0, chunk), :] + land[2, 0:chunk, :] + land[3, 0:chunk, :]
    )


def ring_gather(links, buf, h, base, chunk, cut, q, peers):
    after, before = (q + 1) % 4, (q + 3) % 4
    right, left = peers[0], peers[2]

    def part(c, lo, n):
        return buf.at[h, pl.ds(pl.multiple_of(base + c * chunk + lo, 8), n)]

    own = part(q, 0, chunk)
    a = links.start(own, own, right)
    b = links.start(own, own, left)
    yield
    a.wait_recv()
    piece = part(before, 0, cut)
    a = links.start(piece, piece, right)
    b.wait_recv()
    piece = part(after, cut, chunk - cut)
    b = links.start(piece, piece, left)
    yield
    a.wait_recv()
    b.wait_recv()


def direct_reduce(links, buf, out, h, base, chunk, q, peers, land):
    def rows(c):
        return pl.ds(pl.multiple_of(base + c * chunk, 8), chunk)

    copies = [
        links.start(buf.at[h, rows((q + d) % 4)], land.at[d, pl.ds(0, chunk)], peers[d - 1])
        for d in (2, 1, 3)
    ]
    yield
    for copy in copies:
        copy.wait_recv()
    total = buf[h, rows(q), :]
    for d in (1, 2, 3):
        total = total + land[d, 0:chunk, :]
    out[h, rows(q), :] = total


def direct_gather(links, buf, h, base, chunk, q, peers):
    own = buf.at[h, pl.ds(pl.multiple_of(base + q * chunk, 8), chunk)]
    copies = [links.start(own, own, peers[d - 1]) for d in (2, 1, 3)]
    yield
    for copy in copies:
        copy.wait_recv()


def z_reduce_gather(links, buf, out, land, lo, n, q, right, left):
    half = n // 2

    def part(ref, i, start, size):
        return ref.at[i, pl.ds(lo + start, size)]

    def chunk(ref, i):
        return part(ref, i % 8, 0, n)

    def add(i, slot, start, size):
        rows = slice(lo + start, lo + start + size)
        buf[i % 8, rows, :] += land[slot[0], slot[1], rows, :]

    a = links.start(
        part(buf, (q + 4) % 8, 0, half), part(land.at[0], 0, 0, half), right
    )
    b = links.start(
        part(buf, (q + 4) % 8, half, half), part(land.at[1], 0, half, half), left
    )
    yield
    for s in (1, 2, 3):
        size = half if s == 1 else n
        a.wait_recv()
        add(q + 4 - s, (0, s - 1), 0, size)
        a = links.start(chunk(buf, q + 4 - s), part(land.at[0], s, 0, n), right)
        b.wait_recv()
        add(q + 4 + s, (1, s - 1), n - size, size)
        b = links.start(chunk(buf, q + 4 + s), part(land.at[1], s, 0, n), left)
        yield
    a.wait_recv()
    b.wait_recv()
    rows = slice(lo, lo + n)
    out[q, rows, :] = buf[q, rows, :] + land[0, 3, rows, :] + land[1, 3, rows, :]
    a = links.start(chunk(out, q), chunk(out, q), right)
    b = links.start(chunk(out, q), chunk(out, q), left)
    yield
    for s in (1, 2):
        a.wait_recv()
        a = links.start(chunk(out, q + 8 - s), chunk(out, q + 8 - s), right)
        b.wait_recv()
        b = links.start(chunk(out, q + s), chunk(out, q + s), left)
        yield
    a.wait_recv()
    piece = part(out, (q + 5) % 8, 0, half)
    a = links.start(piece, piece, right)
    b.wait_recv()
    piece = part(out, (q + 3) % 8, half, half)
    b = links.start(piece, piece, left)
    yield
    a.wait_recv()
    b.wait_recv()


def together(first, second, after):
    done = object()
    ended = False
    while first or second:
        first = [s for s in first if next(s, done) is not done]
        if not first and not ended:
            after()
            ended = True
        second = [s for s in second if next(s, done) is not done]


def block_inverse(e):
    lane = lax.broadcasted_iota(jnp.int32, (8, 128), 1)
    sub = lax.broadcasted_iota(jnp.int32, (8, 128), 0)
    group = (lane // 64) * 64

    def pick(tile, index):
        return jnp.take_along_axis(tile, group + index, axis=1)

    e = list(e)
    for g in range(4):
        cols = [[pick(e[i], 8 * g + t) for i in range(g, 4)] for t in range(8)]
        for t in range(8):
            pivot = cols[t][0][t : t + 1, :]
            inv = pl.reciprocal(pivot, approx=True)
            inv = inv * (2.0 - pivot * inv)
            for n, i in enumerate(range(g, 4)):
                f = cols[t][n] * inv
                if n == 0:
                    f = jnp.where(sub > t, f, 0.0)
                e[i] = e[i] - f * e[g][t : t + 1, :]
                for s in range(t + 1, 8):
                    cols[s][n] = cols[s][n] - f * cols[s][0][t : t + 1, :]
    return [tile * lax.rsqrt(pick(tile, 8 * i + sub)) for i, tile in enumerate(e)]


def factor_block(a_ref, k):
    at = 32 * k
    base = at // 128 * 128
    off = at - base
    lane = lax.broadcasted_iota(jnp.int32, (32, 128), 1)
    row = lax.broadcasted_iota(jnp.int32, (32, 128), 0)
    eye = jnp.where(lane % 32 == row, 1.0, 0.0)

    def turned(v, by):
        return pltpu.roll(v, by % 128, 1) if by % 128 else v

    d0, d1 = (a_ref[m, at : at + 32, base : base + 128] for m in range(2))
    d0, d1 = turned(d0, -off), turned(d1, 64 - off)
    e = jnp.where(lane < 32, d0, jnp.where((lane >= 64) & (lane < 96), d1, eye))
    e = jnp.concatenate(block_inverse([e[8 * i : 8 * i + 8] for i in range(4)]), axis=0)
    col = lax.broadcasted_iota(jnp.int32, (32, 256), 1)
    wide_row = lax.broadcasted_iota(jnp.int32, (32, 256), 0)
    inside = (col >= at) & (col < at + 32)
    wide_eye = jnp.where(col - at == wide_row, 1.0, 0.0)
    below = at + 32
    low = below // 128 * 128
    for m in range(2):
        t = turned(e, 96 - 64 * m)[:, 0:32]
        panel = exact_dot(t, jnp.where(inside, wide_eye, a_ref[m, at : at + 32, :]))
        a_ref[m, at : at + 32, :] = panel
        if below < 256:
            change = exact_dot(panel[:, low:256], panel, TN)
            under = lax.broadcasted_iota(jnp.int32, (256 - below, 256), 1)
            rest = jnp.where(
                (under >= at) & (under < below), 0.0, a_ref[m, below:256, :]
            )
            a_ref[m, below:256, :] = rest - change[below - low :, :]


def main_kernel(
    bw, bn, wb, nb,
    ow, on, fac, sq,
    bh, bl, vh, vl, part, full, swap, land, gram, slices, zland, gathered,
    wpart, wfull, wland, inverse, sq_x, sq_y,
    send, recv,
):
    z = lax.axis_index("mp")
    f = lax.axis_index("fsdp")
    c = f % 2
    x = (f // 2) % 4
    y = f // 8

    def plane(xx, yy, cc):
        return {"fsdp": ((yy % 4) * 4 + xx % 4) * 2 + cc}

    sibling = plane(x, y, 1 - c)
    xs = [plane(x + d, y, c) for d in (1, 2, 3)]
    xos = [plane(x + d, y, 1 - c) for d in (1, 2, 3)]
    ys = [plane(x, y + d, c) for d in (1, 2, 3)]
    zs = [{"mp": (z + d) % 8} for d in range(1, 8)]

    barrier = pltpu.get_barrier_semaphore()
    partners = [sibling] + xs + xos + ys + zs
    for device in partners:
        pl.semaphore_signal(barrier, inc=1, device_id=device, device_id_type=MESH)

    links = Links(send, recv)
    sets = ((0, 640), (640, 512))
    wide_b = WIDE - 640

    def split_basis(cc):
        for kind, basis in enumerate((wb, nb)):
            high, low = split(basis[cc])
            vh[cc, kind] = high
            vl[cc, kind] = low

    def raw_rows_of(cc, kind, r, n, buffer):
        rows = pl.ds(pl.multiple_of(cc * HALF + r, 16), n)
        high, low = split(buffer)
        bh[rows, :] = high
        bl[rows, :] = low
        v_high = vh[cc, kind]
        raw = bf16_dot(high, v_high) + (bf16_dot(high, vl[cc, kind]) + bf16_dot(low, v_high))
        part[0, rows, :] = raw[:, 0:128]
        part[1, rows, :] = raw[:, 128:256]

    def raw_set(cc, i):
        lo, n = ((0, 640), (640, wide_b))[i]
        step = 128

        @pl.loop(0, n // step)
        def _(j):
            rows = pl.ds(pl.multiple_of(lo + j * step, step), step)
            raw_rows_of(cc, 0, lo + j * step, step, bw[cc, rows, :])

        if i == 1:
            raw_rows_of(cc, 1, WIDE, NARROW, bn[cc])

    def half_rows(cc, start, n):
        return pl.ds(pl.multiple_of(cc * HALF + start, 8), n)

    split_basis(1 - c)
    raw_set(1 - c, 0)
    pl.semaphore_wait(barrier, len(partners))
    exchanges = []
    for i, (start, n) in enumerate(sets):
        if i == 1:
            raw_set(1 - c, 1)
        exchanges.append(
            links.start(
                part.at[:, half_rows(1 - c, start, n)], swap.at[:, pl.ds(start, n)], sibling
            )
        )
    split_basis(c)

    x_ring = dict(q=x, peers=xs)
    y_ring = dict(q=y, peers=ys)
    base = c * HALF

    def gather_both(buffer, h, start, sizes, first, second):
        yield from direct_gather(
            links, buffer, h, start + first["q"] * sizes[0], sizes[1], **second
        )
        yield from ring_gather(links, buffer, h, start, sizes[0], sizes[0] // 2, **first)

    shares = []

    def whole_sum(i, h):
        start, n = sets[i]
        big, small = n // 4, n // 16
        first, second = (x_ring, y_ring) if h == 0 else (y_ring, x_ring)
        yield from ring_reduce(
            links, part, part, h, base + start, big, big // 2, land=land.at[i, h, 0], **first
        )
        yield from direct_reduce(
            links, part, full, h, base + start + first["q"] * big, small,
            land=land.at[i, h, 1], **second
        )
        yield from gather_both(full, h, base + start, (big, small), first, second)
        done = full.at[h, half_rows(c, start, n)]
        shares.append(links.start(done, done, sibling))

    stages = []
    for i, (start, n) in enumerate(sets):
        raw_set(c, i)
        exchanges[i].wait_recv()
        rows = half_rows(c, start, n)
        part[:, rows, :] += swap[:, start : start + n, :]
        for h in range(2):
            stage = whole_sum(i, h)
            next(stage)
            stages.append(stage)

    def raw_rows(start, n):
        rows = pl.ds(pl.multiple_of(start, 8), n)
        return jnp.concatenate([full[0, rows, :], full[1, rows, :]], axis=1)

    def own_gram(start, n):
        raw = raw_rows(base + start, n)
        return exact_dot(raw, raw, TN)

    together(stages[0:2], stages[2:4], after=lambda: gram.__setitem__(0, own_gram(0, 640)))
    gram[0] += own_gram(640, wide_b)
    gram[1] = own_gram(WIDE, NARROW)

    places = (x * 4 + y, y * 4 + x)
    for t in range(8):
        h, m, r = t // 4, (t // 2) % 2, t % 2
        rows = pl.ds(pl.multiple_of(places[h] * 16 + r * 8, 8), 8)
        slices[t] = gram[m, rows, h * 128 : h * 128 + 128]
    gram_sends = [
        links.start(slices.at[(z + d) % 8], zland.at[d - 1], zs[d - 1]) for d in range(1, 8)
    ]

    def w_of(m):
        start, n = ((0, WIDE), (HALF, WIDE), (WIDE, NARROW), (HALF + WIDE, NARROW))[m]
        high, low = split(raw_rows(start, n))
        b_high = bh[start : start + n, :]
        w = bf16_dot(b_high, high, TN) + (
            bf16_dot(b_high, low, TN) + bf16_dot(bl[start : start + n, :], high, TN)
        )
        for k in range(8):
            wpart[k, m * 32 : m * 32 + 32, :] = w[k * 32 : k * 32 + 32, :]

    def z_chain(i):
        return z_reduce_gather(links, wpart, wfull, wland, 64 * i, 64, z, zs[0], zs[6])

    for copy in shares:
        copy.wait_recv()
    w_of(0)
    w_of(1)
    chains = [z_chain(0)]
    next(chains[0])

    def z_step():
        for chain in chains:
            next(chain, None)

    for copy in gram_sends:
        copy.wait_recv()
    total = slices[z]
    for d in range(7):
        total = total + zland[d]
    place = places[0] + (z // 4) * (places[1] - places[0])
    own = gathered.at[z // 4, pl.ds(pl.multiple_of(place * 32 + (z % 4) * 8, 8), 8)]
    own[...] = total
    gram_sends = [links.start(own, own, zs[d]) for d in range(7)]
    w_of(2)
    w_of(3)
    z_step()
    chains.append(z_chain(1))
    next(chains[1])
    for copy in gram_sends:
        copy.wait_recv()
    stages = [
        gather_both(gathered, 0, 0, (128, 32), x_ring, y_ring),
        gather_both(gathered, 1, 0, (128, 32), y_ring, x_ring),
    ]
    for i in range(4):
        for stage in stages:
            next(stage, None)
        if i < 3:
            links.finish(36)
        if i in (1, 2):
            z_step()
    for h in range(2):
        for p in range(16):
            for m in range(2):
                gram[m, p * 16 : p * 16 + 16, h * 128 : h * 128 + 128] = gathered[
                    h, p * 32 + m * 16 : p * 32 + m * 16 + 16, :
                ]

    for k in range(8):
        factor_block(gram, k)
        z_step()
    full_row = lax.broadcasted_iota(jnp.int32, (256, 256), 0)
    full_col = lax.broadcasted_iota(jnp.int32, (256, 256), 1)
    for m in range(2):
        inverse[c, m] = jnp.where(full_row >= full_col, gram[m], 0.0)
    exchange = links.start(inverse.at[c], inverse.at[c], sibling)
    for chain in chains:
        for _ in chain:
            pass

    def times_inverse(a, cc, kind):
        i_high, i_low = split(inverse[cc, kind])
        high, low = split(a)
        return bf16_dot(high, i_high, NT) + (
            bf16_dot(high, i_low, NT) + bf16_dot(low, i_high, NT)
        )

    def factor_of(cc, kind):
        rows = pl.ds(pl.multiple_of(kind * 64 + cc * 32, 32), 32)
        w = jnp.concatenate([wfull[k, rows, :] for k in range(8)], axis=0)
        factor = times_inverse(w, cc, kind)
        fac[2 * kind + cc] = factor
        squares = jnp.sum(factor * factor, axis=0, keepdims=True)
        return [squares[:, 0:128], squares[:, 128:256]]

    def ortho_half(cc):
        start = cc * HALF
        ow[cc] = times_inverse(raw_rows(start, WIDE), cc, 0)
        on[cc] = times_inverse(raw_rows(start + WIDE, NARROW), cc, 1)

    for kind in range(2):
        for h, squares in enumerate(factor_of(c, kind)):
            row = pl.ds(pl.multiple_of((2 * kind + c) * 2, 2) + h, 1)
            sq[row, :] = squares
    exchange.wait_recv()
    for kind in range(2):
        for h, squares in enumerate(factor_of(1 - c, kind)):
            row = pl.ds(pl.multiple_of((2 * kind + 1 - c) * 2, 2) + h, 1)
            sq[row, :] = squares
    sq_x[0] = sq[...]
    sends = [
        links.start(sq_x.at[0], sq_x.at[d + 1], device)
        for d, device in enumerate([sibling] + xs + xos)
    ]
    ortho_half(c)
    for copy in sends:
        copy.wait_recv()
    total = sq_x[0]
    for d in range(7):
        total = total + sq_x[d + 1]
    sq_y[0] = total
    sends = [links.start(sq_y.at[0], sq_y.at[d + 1], ys[d]) for d in range(3)]
    ortho_half(1 - c)
    for copy in sends:
        copy.wait_recv()
    sq[...] = sq_y[0] + sq_y[1] + sq_y[2] + sq_y[3]
    links.finish()


def last_kernel(
    bw, bn, ow, on, fac, sq, wmo, wbo, wup, nmo, nbo, nup, f_t, b_high, b_low
):
    kinds = ((bw, ow, wmo, wbo, wup, D), (bn, on, nmo, nbo, nup, KVW))

    @pl.when(pl.program_id(1) == 0)
    def _():
        for kind in range(2):
            factor = fac[kind, 0]
            basis = factor * lax.rsqrt(sq[kind, 0] + 1e-6)
            kinds[kind][3][0] = basis
            f_t[kind] = factor.astype(BF16).T
            b_high[kind], b_low[kind] = split(basis.T)

    for kind, (buffer, ortho, m_out, _, update, rows) in enumerate(kinds):
        o_high, o_low = split(ortho[0])
        m_out[0] = buffer[0] - 0.05 * bf16_dot(o_high, f_t[kind])
        product = bf16_dot(o_high, b_high[kind]) + (
            bf16_dot(o_high, b_low[kind]) + bf16_dot(o_low, b_high[kind])
        )
        update[0] = ((rows * D / RANK) ** 0.5 * product).astype(BF16)


def local(wide_momentum, wide_grad, wide_basis, narrow_momentum, narrow_grad, narrow_basis):
    vmem = pl.BlockSpec(memory_space=pltpu.VMEM)
    bw = wide_momentum + wide_grad.astype(F32)
    bn = narrow_momentum + narrow_grad.astype(F32)
    copies = 144
    ow, on, fac, sq = pl.pallas_call(
        main_kernel,
        out_shape=(
            jax.ShapeDtypeStruct((2, WIDE, RANK), F32),
            jax.ShapeDtypeStruct((2, NARROW, RANK), F32),
            jax.ShapeDtypeStruct((4, COLS, RANK), F32),
            jax.ShapeDtypeStruct((8, 128), F32),
        ),
        in_specs=[vmem] * 4,
        out_specs=[vmem] * 4,
        scratch_shapes=[
            pltpu.VMEM((2 * HALF, COLS), BF16),
            pltpu.VMEM((2 * HALF, COLS), BF16),
            pltpu.VMEM((2, 2, COLS, RANK), BF16),
            pltpu.VMEM((2, 2, COLS, RANK), BF16),
            pltpu.VMEM((2, 2 * HALF, 128), F32),
            pltpu.VMEM((2, 2 * HALF, 128), F32),
            pltpu.VMEM((2, HALF, 128), F32),
            pltpu.VMEM((2, 2, 2, 4, 160, 128), F32),
            pltpu.VMEM((2, RANK, RANK), F32),
            pltpu.VMEM((8, 8, 128), F32),
            pltpu.VMEM((7, 8, 128), F32),
            pltpu.VMEM((2, 512, 128), F32),
            pltpu.VMEM((8, 128, RANK), F32),
            pltpu.VMEM((8, 128, RANK), F32),
            pltpu.VMEM((2, 4, 128, RANK), F32),
            pltpu.VMEM((2, 2, RANK, RANK), F32),
            pltpu.VMEM((8, 8, 128), F32),
            pltpu.VMEM((4, 8, 128), F32),
            pltpu.SemaphoreType.DMA((copies,)),
            pltpu.SemaphoreType.DMA((copies,)),
        ],
        compiler_params=pltpu.CompilerParams(
            collective_id=0, has_side_effects=True, vmem_limit_bytes=36 * 2**20
        ),
    )(bw, bn, wide_basis, narrow_basis)

    def rows(n):
        return pl.BlockSpec((1, n, COLS), lambda m, i: (m, i, 0))

    def whole(*lead):
        return pl.BlockSpec(lead, lambda m, i: (0, m, 0, 0))

    basis_out = pl.BlockSpec((1, COLS, RANK), lambda m, i: (m, 0, 0))
    steps = 2
    w, n = WIDE // steps, NARROW // steps
    return pl.pallas_call(
        last_kernel,
        grid=(2, steps),
        out_shape=(
            jax.ShapeDtypeStruct((2, WIDE, COLS), F32),
            jax.ShapeDtypeStruct((2, COLS, RANK), F32),
            jax.ShapeDtypeStruct((2, WIDE, COLS), BF16),
            jax.ShapeDtypeStruct((2, NARROW, COLS), F32),
            jax.ShapeDtypeStruct((2, COLS, RANK), F32),
            jax.ShapeDtypeStruct((2, NARROW, COLS), BF16),
        ),
        in_specs=[
            rows(w), rows(n), rows(w), rows(n),
            whole(2, 1, COLS, RANK), whole(2, 1, 1, RANK),
        ],
        out_specs=[rows(w), basis_out, rows(w), rows(n), basis_out, rows(n)],
        scratch_shapes=[pltpu.VMEM((2, RANK, COLS), BF16)] * 3,
        compiler_params=pltpu.CompilerParams(vmem_limit_bytes=24 * 2**20),
    )(
        bw, bn, ow, on,
        fac.reshape(2, 2, COLS, RANK), sq.reshape(2, 2, 1, RANK),
    )


def solution(mesh):
    return jax.shard_map(
        local,
        mesh=mesh,
        in_specs=(
            P(None, "mp", "fsdp"),
            P(None, "mp", "fsdp"),
            P(None, "fsdp", None),
            P(None, "mp", "fsdp"),
            P(None, "mp", "fsdp"),
            P(None, "fsdp", None),
        ),
        out_specs=(
            P(None, "mp", "fsdp"),
            P(None, "fsdp", None),
            P(None, "mp", "fsdp"),
            P(None, "mp", "fsdp"),
            P(None, "fsdp", None),
            P(None, "mp", "fsdp"),
        ),
        check_vma=False,
    )
```

```python
import jax
import jax.numpy as jnp
from jax import lax
from jax.experimental import pallas as pl
from jax.experimental.pallas import tpu as pltpu
from jax.sharding import PartitionSpec as P

D = 8192
KVW = 1024
RANK = 256
WIDE = 1024
NARROW = 128
COLS = 256
HALF = WIDE + NARROW
F32 = jnp.float32
BF16 = jnp.bfloat16
MESH = pl.DeviceIdType.MESH
EXACT = lax.Precision.HIGHEST

NN = (((1,), (0,)), ((), ()))
NT = (((1,), (1,)), ((), ()))
TN = (((0,), (0,)), ((), ()))


def exact_dot(a, b, dims=NN):
    return lax.dot_general(a, b, dims, precision=EXACT, preferred_element_type=F32)


def split(a):
    high = a.astype(BF16)
    return high, (a - high.astype(F32)).astype(BF16)


def bf16_dot(a, b, dims=NN):
    return lax.dot_general(a, b, dims, preferred_element_type=F32)


class Links:
    def __init__(self, send, recv):
        self.send, self.recv = send, recv
        self.count = 0
        self.started = []

    def start(self, src, dst, device):
        i = self.count
        self.count += 1
        copy = pltpu.make_async_remote_copy(
            src_ref=src,
            dst_ref=dst,
            send_sem=self.send.at[i],
            recv_sem=self.recv.at[i],
            device_id=device,
            device_id_type=MESH,
        )
        copy.start()
        self.started.append(copy)
        return copy

    def finish(self, most=None):
        n = len(self.started) if most is None else most
        for copy in self.started[:n]:
            copy.wait_send()
        self.started = self.started[n:]


def ring_reduce(links, buf, out, h, base, chunk, cut, q, peers, land):
    after, before = (q + 1) % 4, (q + 3) % 4
    right, left = peers[0], peers[2]

    def rows(c, lo, n):
        return pl.ds(pl.multiple_of(base + c * chunk + lo, 8), n)

    far = (q + 2) % 4
    a = links.start(buf.at[h, rows(far, 0, cut)], land.at[0, pl.ds(0, cut)], right)
    b = links.start(
        buf.at[h, rows(far, cut, chunk - cut)], land.at[1, pl.ds(0, chunk - cut)], left
    )
    yield
    a.wait_recv()
    buf[h, rows(after, 0, cut), :] += land[0, 0:cut, :]
    a = links.start(buf.at[h, rows(after, 0, chunk)], land.at[2, pl.ds(0, chunk)], right)
    b.wait_recv()
    buf[h, rows(before, cut, chunk - cut), :] += land[1, 0 : chunk - cut, :]
    b = links.start(buf.at[h, rows(before, 0, chunk)], land.at[3, pl.ds(0, chunk)], left)
    yield
    a.wait_recv()
    b.wait_recv()
    out[h, rows(q, 0, chunk), :] = (
        buf[h, rows(q, 0, chunk), :] + land[2, 0:chunk, :] + land[3, 0:chunk, :]
    )


def ring_gather(links, buf, h, base, chunk, cut, q, peers):
    after, before = (q + 1) % 4, (q + 3) % 4
    right, left = peers[0], peers[2]

    def part(c, lo, n):
        return buf.at[h, pl.ds(pl.multiple_of(base + c * chunk + lo, 8), n)]

    own = part(q, 0, chunk)
    a = links.start(own, own, right)
    b = links.start(own, own, left)
    yield
    a.wait_recv()
    piece = part(before, 0, cut)
    a = links.start(piece, piece, right)
    b.wait_recv()
    piece = part(after, cut, chunk - cut)
    b = links.start(piece, piece, left)
    yield
    a.wait_recv()
    b.wait_recv()


def direct_reduce(links, buf, out, h, base, chunk, q, peers, land):
    def rows(c):
        return pl.ds(pl.multiple_of(base + c * chunk, 8), chunk)

    copies = [
        links.start(buf.at[h, rows((q + d) % 4)], land.at[d, pl.ds(0, chunk)], peers[d - 1])
        for d in (2, 1, 3)
    ]
    yield
    for copy in copies:
        copy.wait_recv()
    total = buf[h, rows(q), :]
    for d in (1, 2, 3):
        total = total + land[d, 0:chunk, :]
    out[h, rows(q), :] = total


def direct_gather(links, buf, h, base, chunk, q, peers):
    own = buf.at[h, pl.ds(pl.multiple_of(base + q * chunk, 8), chunk)]
    copies = [links.start(own, own, peers[d - 1]) for d in (2, 1, 3)]
    yield
    for copy in copies:
        copy.wait_recv()


def z_reduce_gather(links, buf, out, land, lo, n, q, right, left):
    half = n // 2

    def part(ref, i, start, size):
        return ref.at[i, pl.ds(lo + start, size)]

    def chunk(ref, i):
        return part(ref, i % 8, 0, n)

    def add(i, slot, start, size):
        rows = slice(lo + start, lo + start + size)
        buf[i % 8, rows, :] += land[slot[0], slot[1], rows, :]

    a = links.start(
        part(buf, (q + 4) % 8, 0, half), part(land.at[0], 0, 0, half), right
    )
    b = links.start(
        part(buf, (q + 4) % 8, half, half), part(land.at[1], 0, half, half), left
    )
    yield
    for s in (1, 2, 3):
        size = half if s == 1 else n
        a.wait_recv()
        add(q + 4 - s, (0, s - 1), 0, size)
        a = links.start(chunk(buf, q + 4 - s), part(land.at[0], s, 0, n), right)
        b.wait_recv()
        add(q + 4 + s, (1, s - 1), n - size, size)
        b = links.start(chunk(buf, q + 4 + s), part(land.at[1], s, 0, n), left)
        yield
    a.wait_recv()
    b.wait_recv()
    rows = slice(lo, lo + n)
    out[q, rows, :] = buf[q, rows, :] + land[0, 3, rows, :] + land[1, 3, rows, :]
    a = links.start(chunk(out, q), chunk(out, q), right)
    b = links.start(chunk(out, q), chunk(out, q), left)
    yield
    for s in (1, 2):
        a.wait_recv()
        a = links.start(chunk(out, q + 8 - s), chunk(out, q + 8 - s), right)
        b.wait_recv()
        b = links.start(chunk(out, q + s), chunk(out, q + s), left)
        yield
    a.wait_recv()
    piece = part(out, (q + 5) % 8, 0, half)
    a = links.start(piece, piece, right)
    b.wait_recv()
    piece = part(out, (q + 3) % 8, half, half)
    b = links.start(piece, piece, left)
    yield
    a.wait_recv()
    b.wait_recv()


def together(first, second, after):
    done = object()
    ended = False
    while first or second:
        first = [s for s in first if next(s, done) is not done]
        if not first and not ended:
            after()
            ended = True
        second = [s for s in second if next(s, done) is not done]


def block_inverse(e):
    lane = lax.broadcasted_iota(jnp.int32, (8, 128), 1)
    sub = lax.broadcasted_iota(jnp.int32, (8, 128), 0)
    group = (lane // 64) * 64

    def pick(tile, index):
        return jnp.take_along_axis(tile, group + index, axis=1)

    e = list(e)
    for g in range(4):
        cols = [[pick(e[i], 8 * g + t) for i in range(g, 4)] for t in range(8)]
        for t in range(8):
            pivot = cols[t][0][t : t + 1, :]
            inv = pl.reciprocal(pivot, approx=True)
            inv = inv * (2.0 - pivot * inv)
            for n, i in enumerate(range(g, 4)):
                f = cols[t][n] * inv
                if n == 0:
                    f = jnp.where(sub > t, f, 0.0)
                e[i] = e[i] - f * e[g][t : t + 1, :]
                for s in range(t + 1, 8):
                    cols[s][n] = cols[s][n] - f * cols[s][0][t : t + 1, :]
    return [tile * lax.rsqrt(pick(tile, 8 * i + sub)) for i, tile in enumerate(e)]


def factor_block(a_ref, k):
    at = 32 * k
    base = at // 128 * 128
    off = at - base
    lane = lax.broadcasted_iota(jnp.int32, (32, 128), 1)
    row = lax.broadcasted_iota(jnp.int32, (32, 128), 0)
    eye = jnp.where(lane % 32 == row, 1.0, 0.0)

    def turned(v, by):
        return pltpu.roll(v, by % 128, 1) if by % 128 else v

    d0, d1 = (a_ref[m, at : at + 32, base : base + 128] for m in range(2))
    d0, d1 = turned(d0, -off), turned(d1, 64 - off)
    e = jnp.where(lane < 32, d0, jnp.where((lane >= 64) & (lane < 96), d1, eye))
    e = jnp.concatenate(block_inverse([e[8 * i : 8 * i + 8] for i in range(4)]), axis=0)
    col = lax.broadcasted_iota(jnp.int32, (32, 256), 1)
    wide_row = lax.broadcasted_iota(jnp.int32, (32, 256), 0)
    inside = (col >= at) & (col < at + 32)
    wide_eye = jnp.where(col - at == wide_row, 1.0, 0.0)
    below = at + 32
    low = below // 128 * 128
    for m in range(2):
        t = turned(e, 96 - 64 * m)[:, 0:32]
        panel = exact_dot(t, jnp.where(inside, wide_eye, a_ref[m, at : at + 32, :]))
        a_ref[m, at : at + 32, :] = panel
        if below < 256:
            change = exact_dot(panel[:, low:256], panel, TN)
            under = lax.broadcasted_iota(jnp.int32, (256 - below, 256), 1)
            rest = jnp.where(
                (under >= at) & (under < below), 0.0, a_ref[m, below:256, :]
            )
            a_ref[m, below:256, :] = rest - change[below - low :, :]


def main_kernel(
    bw, bn, wb, nb,
    ow, on, fac, sq,
    bh, bl, vh, vl, part, full, swap, land, gram, cross, w_first, slices, zland, gathered,
    wpart, wfull, wland, inverse, sq_x, sq_y,
    send, recv,
):
    z = lax.axis_index("mp")
    f = lax.axis_index("fsdp")
    c = f % 2
    x = (f // 2) % 4
    y = f // 8

    def plane(xx, yy, cc):
        return {"fsdp": ((yy % 4) * 4 + xx % 4) * 2 + cc}

    sibling = plane(x, y, 1 - c)
    xs = [plane(x + d, y, c) for d in (1, 2, 3)]
    xos = [plane(x + d, y, 1 - c) for d in (1, 2, 3)]
    ys = [plane(x, y + d, c) for d in (1, 2, 3)]
    zs = [{"mp": (z + d) % 8} for d in range(1, 8)]

    barrier = pltpu.get_barrier_semaphore()
    partners = [sibling] + xs + xos + ys + zs
    for device in partners:
        pl.semaphore_signal(barrier, inc=1, device_id=device, device_id_type=MESH)

    links = Links(send, recv)
    sets = ((0, 640), (640, 512))
    wide_b = WIDE - 640

    def split_basis(cc):
        for kind, basis in enumerate((wb, nb)):
            high, low = split(basis[cc])
            vh[cc, kind] = high
            vl[cc, kind] = low

    def raw_rows_of(cc, kind, r, n, buffer):
        rows = pl.ds(pl.multiple_of(cc * HALF + r, 16), n)
        high, low = split(buffer)
        bh[rows, :] = high
        bl[rows, :] = low
        v_high = vh[cc, kind]
        raw = bf16_dot(high, v_high) + (bf16_dot(high, vl[cc, kind]) + bf16_dot(low, v_high))
        part[0, rows, :] = raw[:, 0:128]
        part[1, rows, :] = raw[:, 128:256]

    def raw_set(cc, i):
        lo, n = ((0, 640), (640, wide_b))[i]
        raw_rows_of(cc, 0, lo, n, bw[cc, lo : lo + n, :])

        if i == 1:
            raw_rows_of(cc, 1, WIDE, NARROW, bn[cc])

    def half_rows(cc, start, n):
        return pl.ds(pl.multiple_of(cc * HALF + start, 8), n)

    split_basis(1 - c)
    raw_set(1 - c, 0)
    pl.semaphore_wait(barrier, len(partners))
    exchanges = []
    for i, (start, n) in enumerate(sets):
        if i == 1:
            raw_set(1 - c, 1)
        exchanges.append(
            links.start(
                part.at[:, half_rows(1 - c, start, n)], swap.at[:, pl.ds(start, n)], sibling
            )
        )
    split_basis(c)

    x_ring = dict(q=x, peers=xs)
    y_ring = dict(q=y, peers=ys)
    base = c * HALF

    def gather_both(buffer, h, start, sizes, first, second):
        yield from direct_gather(
            links, buffer, h, start + first["q"] * sizes[0], sizes[1], **second
        )
        yield from ring_gather(links, buffer, h, start, sizes[0], sizes[0] // 2, **first)

    shares = []

    def whole_sum(i, h):
        start, n = sets[i]
        big, small = n // 4, n // 16
        first, second = (x_ring, y_ring) if h == 0 else (y_ring, x_ring)
        yield from ring_reduce(
            links, part, part, h, base + start, big, big // 2, land=land.at[i, h, 0], **first
        )
        yield from direct_reduce(
            links, part, full, h, base + start + first["q"] * big, small,
            land=land.at[i, h, 1], **second
        )
        yield from gather_both(full, h, base + start, (big, small), first, second)
        done = full.at[h, half_rows(c, start, n)]
        shares.append(links.start(done, done, sibling))

    stages = []
    for i, (start, n) in enumerate(sets):
        raw_set(c, i)
        exchanges[i].wait_recv()
        rows = half_rows(c, start, n)
        part[:, rows, :] += swap[:, start : start + n, :]
        for h in range(2):
            stage = whole_sum(i, h)
            next(stage)
            stages.append(stage)

    def raw_rows(start, n):
        rows = pl.ds(pl.multiple_of(start, 8), n)
        return jnp.concatenate([full[0, rows, :], full[1, rows, :]], axis=1)

    def own_gram(start, n):
        raw = raw_rows(base + start, n)
        high = raw.astype(BF16)
        middle, low = split(raw - high.astype(F32))
        cross[...] = bf16_dot(high, middle, TN) + bf16_dot(high, low, TN)
        mirrored = cross[...] + cross[...].T
        return bf16_dot(high, high, TN) + (mirrored + bf16_dot(middle, middle, TN))

    def w_of(cc, start, n):
        start = cc * HALF + start
        rows = pl.ds(pl.multiple_of(start, 16), n)
        high, low = split(raw_rows(start, n))
        b_high = bh[rows, :]
        return bf16_dot(b_high, high, TN) + (
            bf16_dot(b_high, low, TN) + bf16_dot(bl[rows, :], high, TN)
        )

    def first_set():
        gram[0] = own_gram(0, 640)
        w_first[...] = w_of(c, 0, 640)

    together(stages[0:2], stages[2:4], after=first_set)
    gram[0] += own_gram(640, wide_b)
    gram[1] = own_gram(WIDE, NARROW)

    places = (x * 4 + y, y * 4 + x)
    for t in range(8):
        h, m, r = t // 4, (t // 2) % 2, t % 2
        rows = pl.ds(pl.multiple_of(places[h] * 16 + r * 8, 8), 8)
        slices[t] = gram[m, rows, h * 128 : h * 128 + 128]
    gram_sends = [
        links.start(slices.at[(z + d) % 8], zland.at[d - 1], zs[d - 1]) for d in range(1, 8)
    ]

    def put_w(i, kind, w):
        row = i * 64 + kind * 32
        for k in range(8):
            wpart[k, row : row + 32, :] = w[k * 32 : k * 32 + 32, :]

    def z_chain(i):
        return z_reduce_gather(links, wpart, wfull, wland, 64 * i, 64, z, zs[0], zs[6])

    put_w(0, 0, w_first[...] + w_of(c, 640, wide_b))
    put_w(0, 1, w_of(c, WIDE, NARROW))
    chains = [z_chain(0)]
    next(chains[0])

    def z_step():
        for chain in chains:
            next(chain, None)

    for copy in gram_sends:
        copy.wait_recv()
    total = slices[z]
    for d in range(7):
        total = total + zland[d]
    place = places[0] + (z // 4) * (places[1] - places[0])
    own = gathered.at[z // 4, pl.ds(pl.multiple_of(place * 32 + (z % 4) * 8, 8), 8)]
    own[...] = total
    gram_sends = [links.start(own, own, zs[d]) for d in range(7)]
    for copy in shares:
        copy.wait_recv()
    put_w(1, 0, w_of(1 - c, 0, WIDE))
    put_w(1, 1, w_of(1 - c, WIDE, NARROW))
    z_step()
    chains.append(z_chain(1))
    next(chains[1])
    for copy in gram_sends:
        copy.wait_recv()
    stages = [
        gather_both(gathered, 0, 0, (128, 32), x_ring, y_ring),
        gather_both(gathered, 1, 0, (128, 32), y_ring, x_ring),
    ]
    for i in range(4):
        for stage in stages:
            next(stage, None)
        if i < 3:
            links.finish(36)
        z_step()
    for h in range(2):
        for p in range(16):
            for m in range(2):
                gram[m, p * 16 : p * 16 + 16, h * 128 : h * 128 + 128] = gathered[
                    h, p * 32 + m * 16 : p * 32 + m * 16 + 16, :
                ]

    for k in range(8):
        factor_block(gram, k)
        if k % 2:
            z_step()
    full_row = lax.broadcasted_iota(jnp.int32, (256, 256), 0)
    full_col = lax.broadcasted_iota(jnp.int32, (256, 256), 1)
    for m in range(2):
        inverse[c, m] = jnp.where(full_row >= full_col, gram[m], 0.0)
    exchange = links.start(inverse.at[c], inverse.at[c], sibling)
    for chain in chains:
        for _ in chain:
            pass

    def times_inverse(a, cc, kind):
        i_high, i_low = split(inverse[cc, kind])
        high, low = split(a)
        return bf16_dot(high, i_high, NT) + (
            bf16_dot(high, i_low, NT) + bf16_dot(low, i_high, NT)
        )

    def factor_of(i, cc, kind):
        row = i * 64 + kind * 32
        w = jnp.concatenate([wfull[k, row : row + 32, :] for k in range(8)], axis=0)
        factor = times_inverse(w, cc, kind)
        fac[2 * kind + cc] = factor
        squares = jnp.sum(factor * factor, axis=0, keepdims=True)
        return [squares[:, 0:128], squares[:, 128:256]]

    def ortho_half(cc):
        start = cc * HALF
        ow[cc] = times_inverse(raw_rows(start, WIDE), cc, 0)
        on[cc] = times_inverse(raw_rows(start + WIDE, NARROW), cc, 1)

    for kind in range(2):
        for h, squares in enumerate(factor_of(0, c, kind)):
            row = pl.ds(pl.multiple_of((2 * kind + c) * 2, 2) + h, 1)
            sq[row, :] = squares
    exchange.wait_recv()
    for kind in range(2):
        for h, squares in enumerate(factor_of(1, 1 - c, kind)):
            row = pl.ds(pl.multiple_of((2 * kind + 1 - c) * 2, 2) + h, 1)
            sq[row, :] = squares
    sq_x[0] = sq[...]
    sends = [
        links.start(sq_x.at[0], sq_x.at[d + 1], device)
        for d, device in enumerate([sibling] + xs + xos)
    ]
    ortho_half(c)
    for copy in sends:
        copy.wait_recv()
    total = sq_x[0]
    for d in range(7):
        total = total + sq_x[d + 1]
    sq_y[0] = total
    sends = [links.start(sq_y.at[0], sq_y.at[d + 1], ys[d]) for d in range(3)]
    ortho_half(1 - c)
    for copy in sends:
        copy.wait_recv()
    sq[...] = sq_y[0] + sq_y[1] + sq_y[2] + sq_y[3]
    links.finish()


def last_kernel(
    bw, bn, ow, on, fac, sq, wmo, wbo, wup, nmo, nbo, nup, f_t, b_high, b_low
):
    kinds = ((bw, ow, wmo, wbo, wup, D), (bn, on, nmo, nbo, nup, KVW))

    @pl.when(pl.program_id(1) == 0)
    def _():
        for kind in range(2):
            factor = fac[kind, 0]
            basis = factor * lax.rsqrt(sq[kind, 0] + 1e-6)
            kinds[kind][3][0] = basis
            f_t[kind] = factor.astype(BF16).T
            b_high[kind], b_low[kind] = split(basis.T)

    for kind, (buffer, ortho, m_out, _, update, rows) in enumerate(kinds):
        o_high, o_low = split(ortho[0])
        m_out[0] = buffer[0] - 0.05 * bf16_dot(o_high, f_t[kind])
        product = bf16_dot(o_high, b_high[kind]) + (
            bf16_dot(o_high, b_low[kind]) + bf16_dot(o_low, b_high[kind])
        )
        update[0] = ((rows * D / RANK) ** 0.5 * product).astype(BF16)


def local(wide_momentum, wide_grad, wide_basis, narrow_momentum, narrow_grad, narrow_basis):
    vmem = pl.BlockSpec(memory_space=pltpu.VMEM)
    bw = wide_momentum + wide_grad.astype(F32)
    bn = narrow_momentum + narrow_grad.astype(F32)
    copies = 144
    ow, on, fac, sq = pl.pallas_call(
        main_kernel,
        out_shape=(
            jax.ShapeDtypeStruct((2, WIDE, RANK), F32),
            jax.ShapeDtypeStruct((2, NARROW, RANK), F32),
            jax.ShapeDtypeStruct((4, COLS, RANK), F32),
            jax.ShapeDtypeStruct((8, 128), F32),
        ),
        in_specs=[vmem] * 4,
        out_specs=[vmem] * 4,
        scratch_shapes=[
            pltpu.VMEM((2 * HALF, COLS), BF16),
            pltpu.VMEM((2 * HALF, COLS), BF16),
            pltpu.VMEM((2, 2, COLS, RANK), BF16),
            pltpu.VMEM((2, 2, COLS, RANK), BF16),
            pltpu.VMEM((2, 2 * HALF, 128), F32),
            pltpu.VMEM((2, 2 * HALF, 128), F32),
            pltpu.VMEM((2, HALF, 128), F32),
            pltpu.VMEM((2, 2, 2, 4, 160, 128), F32),
            pltpu.VMEM((2, RANK, RANK), F32),
            pltpu.VMEM((RANK, RANK), F32),
            pltpu.VMEM((COLS, RANK), F32),
            pltpu.VMEM((8, 8, 128), F32),
            pltpu.VMEM((7, 8, 128), F32),
            pltpu.VMEM((2, 512, 128), F32),
            pltpu.VMEM((8, 128, RANK), F32),
            pltpu.VMEM((8, 128, RANK), F32),
            pltpu.VMEM((2, 4, 128, RANK), F32),
            pltpu.VMEM((2, 2, RANK, RANK), F32),
            pltpu.VMEM((8, 8, 128), F32),
            pltpu.VMEM((4, 8, 128), F32),
            pltpu.SemaphoreType.DMA((copies,)),
            pltpu.SemaphoreType.DMA((copies,)),
        ],
        compiler_params=pltpu.CompilerParams(
            collective_id=0, has_side_effects=True, vmem_limit_bytes=36 * 2**20
        ),
    )(bw, bn, wide_basis, narrow_basis)

    def rows(n):
        return pl.BlockSpec((1, n, COLS), lambda m, i: (m, i, 0))

    def whole(*lead):
        return pl.BlockSpec(lead, lambda m, i: (0, m, 0, 0))

    basis_out = pl.BlockSpec((1, COLS, RANK), lambda m, i: (m, 0, 0))
    steps = 2
    w, n = WIDE // steps, NARROW // steps
    return pl.pallas_call(
        last_kernel,
        grid=(2, steps),
        out_shape=(
            jax.ShapeDtypeStruct((2, WIDE, COLS), F32),
            jax.ShapeDtypeStruct((2, COLS, RANK), F32),
            jax.ShapeDtypeStruct((2, WIDE, COLS), BF16),
            jax.ShapeDtypeStruct((2, NARROW, COLS), F32),
            jax.ShapeDtypeStruct((2, COLS, RANK), F32),
            jax.ShapeDtypeStruct((2, NARROW, COLS), BF16),
        ),
        in_specs=[
            rows(w), rows(n), rows(w), rows(n),
            whole(2, 1, COLS, RANK), whole(2, 1, 1, RANK),
        ],
        out_specs=[rows(w), basis_out, rows(w), rows(n), basis_out, rows(n)],
        scratch_shapes=[pltpu.VMEM((2, RANK, COLS), BF16)] * 3,
        compiler_params=pltpu.CompilerParams(vmem_limit_bytes=24 * 2**20),
    )(
        bw, bn, ow, on,
        fac.reshape(2, 2, COLS, RANK), sq.reshape(2, 2, 1, RANK),
    )


def solution(mesh):
    return jax.shard_map(
        local,
        mesh=mesh,
        in_specs=(
            P(None, "mp", "fsdp"),
            P(None, "mp", "fsdp"),
            P(None, "fsdp", None),
            P(None, "mp", "fsdp"),
            P(None, "mp", "fsdp"),
            P(None, "fsdp", None),
        ),
        out_specs=(
            P(None, "mp", "fsdp"),
            P(None, "fsdp", None),
            P(None, "mp", "fsdp"),
            P(None, "mp", "fsdp"),
            P(None, "fsdp", None),
            P(None, "mp", "fsdp"),
        ),
        check_vma=False,
    )
```

```python
import jax
import jax.numpy as jnp
from jax import lax
from jax.experimental import pallas as pl
from jax.experimental.pallas import tpu as pltpu
from jax.sharding import PartitionSpec as P

D = 8192
KVW = 1024
RANK = 256
WIDE = 1024
NARROW = 128
COLS = 256
HALF = WIDE + NARROW
F32 = jnp.float32
BF16 = jnp.bfloat16
MESH = pl.DeviceIdType.MESH
EXACT = lax.Precision.HIGHEST

NN = (((1,), (0,)), ((), ()))
NT = (((1,), (1,)), ((), ()))
TN = (((0,), (0,)), ((), ()))


def exact_dot(a, b, dims=NN):
    return lax.dot_general(a, b, dims, precision=EXACT, preferred_element_type=F32)


def split(a):
    high = a.astype(BF16)
    return high, (a - high.astype(F32)).astype(BF16)


def bf16_dot(a, b, dims=NN):
    return lax.dot_general(a, b, dims, preferred_element_type=F32)


class Links:
    def __init__(self, send, recv):
        self.send, self.recv = send, recv
        self.count = 0
        self.started = []

    def start(self, src, dst, device):
        i = self.count
        self.count += 1
        copy = pltpu.make_async_remote_copy(
            src_ref=src,
            dst_ref=dst,
            send_sem=self.send.at[i],
            recv_sem=self.recv.at[i],
            device_id=device,
            device_id_type=MESH,
        )
        copy.start()
        self.started.append(copy)
        return copy

    def finish(self, most=None):
        n = len(self.started) if most is None else most
        for copy in self.started[:n]:
            copy.wait_send()
        self.started = self.started[n:]


def ring_reduce(links, buf, out, h, base, chunk, cut, q, peers, land):
    after, before = (q + 1) % 4, (q + 3) % 4
    right, left = peers[0], peers[2]

    def rows(c, lo, n):
        return pl.ds(pl.multiple_of(base + c * chunk + lo, 8), n)

    far = (q + 2) % 4
    a = links.start(buf.at[h, rows(far, 0, cut)], land.at[0, pl.ds(0, cut)], right)
    b = links.start(
        buf.at[h, rows(far, cut, chunk - cut)], land.at[1, pl.ds(0, chunk - cut)], left
    )
    yield
    a.wait_recv()
    buf[h, rows(after, 0, cut), :] += land[0, 0:cut, :]
    a = links.start(buf.at[h, rows(after, 0, chunk)], land.at[2, pl.ds(0, chunk)], right)
    b.wait_recv()
    buf[h, rows(before, cut, chunk - cut), :] += land[1, 0 : chunk - cut, :]
    b = links.start(buf.at[h, rows(before, 0, chunk)], land.at[3, pl.ds(0, chunk)], left)
    yield
    a.wait_recv()
    b.wait_recv()
    out[h, rows(q, 0, chunk), :] = (
        buf[h, rows(q, 0, chunk), :] + land[2, 0:chunk, :] + land[3, 0:chunk, :]
    )


def ring_gather(links, buf, h, base, chunk, cut, q, peers):
    after, before = (q + 1) % 4, (q + 3) % 4
    right, left = peers[0], peers[2]

    def part(c, lo, n):
        return buf.at[h, pl.ds(pl.multiple_of(base + c * chunk + lo, 8), n)]

    own = part(q, 0, chunk)
    a = links.start(own, own, right)
    b = links.start(own, own, left)
    yield
    a.wait_recv()
    piece = part(before, 0, cut)
    a = links.start(piece, piece, right)
    b.wait_recv()
    piece = part(after, cut, chunk - cut)
    b = links.start(piece, piece, left)
    yield
    a.wait_recv()
    b.wait_recv()


def direct_reduce(links, buf, out, h, base, chunk, q, peers, land):
    def rows(c):
        return pl.ds(pl.multiple_of(base + c * chunk, 8), chunk)

    copies = [
        links.start(buf.at[h, rows((q + d) % 4)], land.at[d, pl.ds(0, chunk)], peers[d - 1])
        for d in (2, 1, 3)
    ]
    yield
    for copy in copies:
        copy.wait_recv()
    total = buf[h, rows(q), :]
    for d in (1, 2, 3):
        total = total + land[d, 0:chunk, :]
    out[h, rows(q), :] = total


def direct_gather(links, buf, h, base, chunk, q, peers):
    own = buf.at[h, pl.ds(pl.multiple_of(base + q * chunk, 8), chunk)]
    copies = [links.start(own, own, peers[d - 1]) for d in (2, 1, 3)]
    yield
    for copy in copies:
        copy.wait_recv()


def z_reduce_gather(links, buf, out, land, lo, n, q, right, left):
    half = n // 2

    def part(ref, i, start, size):
        return ref.at[i, pl.ds(lo + start, size)]

    def chunk(ref, i):
        return part(ref, i % 8, 0, n)

    def add(i, slot, start, size):
        rows = slice(lo + start, lo + start + size)
        buf[i % 8, rows, :] += land[slot[0], slot[1], rows, :]

    a = links.start(
        part(buf, (q + 4) % 8, 0, half), part(land.at[0], 0, 0, half), right
    )
    b = links.start(
        part(buf, (q + 4) % 8, half, half), part(land.at[1], 0, half, half), left
    )
    yield
    for s in (1, 2, 3):
        size = half if s == 1 else n
        a.wait_recv()
        add(q + 4 - s, (0, s - 1), 0, size)
        a = links.start(chunk(buf, q + 4 - s), part(land.at[0], s, 0, n), right)
        b.wait_recv()
        add(q + 4 + s, (1, s - 1), n - size, size)
        b = links.start(chunk(buf, q + 4 + s), part(land.at[1], s, 0, n), left)
        yield
    a.wait_recv()
    b.wait_recv()
    rows = slice(lo, lo + n)
    out[q, rows, :] = buf[q, rows, :] + land[0, 3, rows, :] + land[1, 3, rows, :]
    a = links.start(chunk(out, q), chunk(out, q), right)
    b = links.start(chunk(out, q), chunk(out, q), left)
    yield
    for s in (1, 2):
        a.wait_recv()
        a = links.start(chunk(out, q + 8 - s), chunk(out, q + 8 - s), right)
        b.wait_recv()
        b = links.start(chunk(out, q + s), chunk(out, q + s), left)
        yield
    a.wait_recv()
    piece = part(out, (q + 5) % 8, 0, half)
    a = links.start(piece, piece, right)
    b.wait_recv()
    piece = part(out, (q + 3) % 8, half, half)
    b = links.start(piece, piece, left)
    yield
    a.wait_recv()
    b.wait_recv()


def together(first, second, after):
    done = object()
    ended = False
    while first or second:
        first = [s for s in first if next(s, done) is not done]
        if not first and not ended:
            after()
            ended = True
        second = [s for s in second if next(s, done) is not done]


def block_inverse(e):
    lane = lax.broadcasted_iota(jnp.int32, (8, 128), 1)
    sub = lax.broadcasted_iota(jnp.int32, (8, 128), 0)
    group = (lane // 64) * 64

    def pick(tile, index):
        return jnp.take_along_axis(tile, group + index, axis=1)

    e = list(e)
    for g in range(4):
        cols = [[pick(e[i], 8 * g + t) for i in range(g, 4)] for t in range(8)]
        for t in range(8):
            pivot = cols[t][0][t : t + 1, :]
            inv = pl.reciprocal(pivot, approx=True)
            inv = inv * (2.0 - pivot * inv)
            for n, i in enumerate(range(g, 4)):
                f = cols[t][n] * inv
                if n == 0:
                    f = jnp.where(sub > t, f, 0.0)
                e[i] = e[i] - f * e[g][t : t + 1, :]
                for s in range(t + 1, 8):
                    cols[s][n] = cols[s][n] - f * cols[s][0][t : t + 1, :]
    return [tile * lax.rsqrt(pick(tile, 8 * i + sub)) for i, tile in enumerate(e)]


def invert_factor(a_ref, out, after):
    lane = lax.broadcasted_iota(jnp.int32, (32, 128), 1)
    row = lax.broadcasted_iota(jnp.int32, (32, 128), 0)
    eye = jnp.where(lane % 32 == row, 1.0, 0.0)
    col = lax.broadcasted_iota(jnp.int32, (32, 256), 1)
    wide_row = lax.broadcasted_iota(jnp.int32, (32, 256), 0)

    def turned(v, by):
        return pltpu.roll(v, by % 128, 1) if by % 128 else v

    blocks = [a_ref[m, 0:32, 0:128] for m in range(2)]
    panels = None
    for k in range(8):
        at, below = 32 * k, 32 * k + 32
        base, low = at // 128 * 128, below // 128 * 128
        if k > 0:
            for m in range(2):
                change = exact_dot(panels[m][:, base:256], panels[m], TN)
                under = lax.broadcasted_iota(jnp.int32, (256 - at, 256), 1)
                rest = jnp.where(
                    (under >= at - 32) & (under < at), 0.0, a_ref[m, at:256, :]
                )
                a_ref[m, at:256, :] = rest - change[at - base :, :]
        d0, d1 = turned(blocks[0], base - at), turned(blocks[1], 64 + base - at)
        e = jnp.where(lane < 32, d0, jnp.where((lane >= 64) & (lane < 96), d1, eye))
        e = jnp.concatenate(
            block_inverse([e[8 * i : 8 * i + 8] for i in range(4)]), axis=0
        )
        inside = (col >= at) & (col < below)
        wide_eye = jnp.where(col - at == wide_row, 1.0, 0.0)
        panels, blocks = [], []
        for m in range(2):
            t = turned(e, 96 - 64 * m)[:, 0:32]
            panel = exact_dot(t, jnp.where(inside, wide_eye, a_ref[m, at:below, :]))
            panels.append(panel)
            if below < 256:
                near = panel[:, low : low + 128]
                change = exact_dot(near, near, TN)
                blocks.append(
                    a_ref[m, below : below + 32, low : low + 128]
                    - change[below - low : below - low + 32, :]
                )
            a_ref[m, at:below, :] = panel
            out[m, at:below, :] = jnp.where(col <= at + wide_row, panel, 0.0)
        after(k)


def main_kernel(
    bw, bn, wb, nb,
    ow, on, fac, sq,
    bh, bl, vh, vl, part, full, swap, land, gram, cross, w_first, slices, zland, gathered,
    wpart, wfull, wland, inverse, sq_land,
    send, recv,
):
    z = lax.axis_index("mp")
    f = lax.axis_index("fsdp")
    c = f % 2
    x = (f // 2) % 4
    y = f // 8

    def plane(xx, yy, cc):
        return {"fsdp": ((yy % 4) * 4 + xx % 4) * 2 + cc}

    sibling = plane(x, y, 1 - c)
    xs = [plane(x + d, y, c) for d in (1, 2, 3)]
    others = [(d, {"fsdp": (f + d) % 32}) for d in range(1, 32)]
    ys = [plane(x, y + d, c) for d in (1, 2, 3)]
    zs = [{"mp": (z + d) % 8} for d in range(1, 8)]

    barrier = pltpu.get_barrier_semaphore()
    partners = [device for _, device in others] + zs
    for device in partners:
        pl.semaphore_signal(barrier, inc=1, device_id=device, device_id_type=MESH)

    links = Links(send, recv)
    sets = ((0, 640), (640, 512))
    wide_b = WIDE - 640

    def split_basis(cc):
        for kind, basis in enumerate((wb, nb)):
            high, low = split(basis[cc])
            vh[cc, kind] = high
            vl[cc, kind] = low

    def raw_rows_of(cc, kind, r, n, buffer):
        rows = pl.ds(pl.multiple_of(cc * HALF + r, 16), n)
        high, low = split(buffer)
        bh[rows, :] = high
        bl[rows, :] = low
        v_high = vh[cc, kind]
        raw = bf16_dot(high, v_high) + (bf16_dot(high, vl[cc, kind]) + bf16_dot(low, v_high))
        part[0, rows, :] = raw[:, 0:128]
        part[1, rows, :] = raw[:, 128:256]

    def raw_set(cc, i):
        lo, n = ((0, 640), (640, wide_b))[i]
        raw_rows_of(cc, 0, lo, n, bw[cc, lo : lo + n, :])

        if i == 1:
            raw_rows_of(cc, 1, WIDE, NARROW, bn[cc])

    def half_rows(cc, start, n):
        return pl.ds(pl.multiple_of(cc * HALF + start, 8), n)

    split_basis(1 - c)
    raw_set(1 - c, 0)
    pl.semaphore_wait(barrier, len(partners))
    exchanges = []
    for i, (start, n) in enumerate(sets):
        if i == 1:
            raw_set(1 - c, 1)
        exchanges.append(
            links.start(
                part.at[:, half_rows(1 - c, start, n)], swap.at[:, pl.ds(start, n)], sibling
            )
        )
    split_basis(c)

    x_ring = dict(q=x, peers=xs)
    y_ring = dict(q=y, peers=ys)
    base = c * HALF

    def gather_both(buffer, h, start, sizes, first, second):
        yield from direct_gather(
            links, buffer, h, start + first["q"] * sizes[0], sizes[1], **second
        )
        yield from ring_gather(links, buffer, h, start, sizes[0], sizes[0] // 2, **first)

    shares = []

    def whole_sum(i, h):
        start, n = sets[i]
        big, small = n // 4, n // 16
        first, second = (x_ring, y_ring) if h == 0 else (y_ring, x_ring)
        yield from ring_reduce(
            links, part, part, h, base + start, big, big // 2, land=land.at[i, h, 0], **first
        )
        yield from direct_reduce(
            links, part, full, h, base + start + first["q"] * big, small,
            land=land.at[i, h, 1], **second
        )
        yield from gather_both(full, h, base + start, (big, small), first, second)
        done = full.at[h, half_rows(c, start, n)]
        shares.append(links.start(done, done, sibling))

    stages = []
    for i, (start, n) in enumerate(sets):
        raw_set(c, i)
        exchanges[i].wait_recv()
        rows = half_rows(c, start, n)
        part[:, rows, :] += swap[:, start : start + n, :]
        for h in range(2):
            stage = whole_sum(i, h)
            next(stage)
            stages.append(stage)

    def raw_rows(start, n):
        rows = pl.ds(pl.multiple_of(start, 8), n)
        return jnp.concatenate([full[0, rows, :], full[1, rows, :]], axis=1)

    def own_gram(start, n):
        raw = raw_rows(base + start, n)
        high = raw.astype(BF16)
        middle, low = split(raw - high.astype(F32))
        cross[...] = bf16_dot(high, middle, TN) + bf16_dot(high, low, TN)
        mirrored = cross[...] + cross[...].T
        return bf16_dot(high, high, TN) + (mirrored + bf16_dot(middle, middle, TN))

    def w_of(cc, start, n):
        start = cc * HALF + start
        rows = pl.ds(pl.multiple_of(start, 16), n)
        high, low = split(raw_rows(start, n))
        b_high = bh[rows, :]
        return bf16_dot(b_high, high, TN) + (
            bf16_dot(b_high, low, TN) + bf16_dot(bl[rows, :], high, TN)
        )

    def first_set():
        gram[0] = own_gram(0, 640)
        w_first[...] = w_of(c, 0, 640)

    together(stages[0:2], stages[2:4], after=first_set)
    gram[0] += own_gram(640, wide_b)
    gram[1] = own_gram(WIDE, NARROW)

    places = (x * 4 + y, y * 4 + x)
    for t in range(8):
        h, m, r = t // 4, (t // 2) % 2, t % 2
        rows = pl.ds(pl.multiple_of(places[h] * 16 + r * 8, 8), 8)
        slices[t] = gram[m, rows, h * 128 : h * 128 + 128]
    gram_sends = [
        links.start(slices.at[(z + d) % 8], zland.at[d - 1], zs[d - 1]) for d in range(1, 8)
    ]

    def put_w(i, kind, w):
        row = i * 64 + kind * 32
        for k in range(8):
            wpart[k, row : row + 32, :] = w[k * 32 : k * 32 + 32, :]

    def z_chain(i):
        return z_reduce_gather(links, wpart, wfull, wland, 64 * i, 64, z, zs[0], zs[6])

    put_w(0, 0, w_first[...] + w_of(c, 640, wide_b))
    put_w(0, 1, w_of(c, WIDE, NARROW))
    chains = [z_chain(0)]
    next(chains[0])

    def z_step():
        for chain in chains:
            next(chain, None)

    for copy in gram_sends:
        copy.wait_recv()
    total = slices[z]
    for d in range(7):
        total = total + zland[d]
    place = places[0] + (z // 4) * (places[1] - places[0])
    own = gathered.at[z // 4, pl.ds(pl.multiple_of(place * 32 + (z % 4) * 8, 8), 8)]
    own[...] = total
    gram_sends = [links.start(own, own, zs[d]) for d in range(7)]
    for copy in shares:
        copy.wait_recv()
    put_w(1, 0, w_of(1 - c, 0, WIDE))
    put_w(1, 1, w_of(1 - c, WIDE, NARROW))
    z_step()
    chains.append(z_chain(1))
    next(chains[1])
    for copy in gram_sends:
        copy.wait_recv()
    stages = [
        gather_both(gathered, 0, 0, (128, 32), x_ring, y_ring),
        gather_both(gathered, 1, 0, (128, 32), y_ring, x_ring),
    ]
    for i in range(4):
        for stage in stages:
            next(stage, None)
        if i < 3:
            links.finish(36)
        z_step()
    for h in range(2):
        for p in range(16):
            for m in range(2):
                gram[m, p * 16 : p * 16 + 16, h * 128 : h * 128 + 128] = gathered[
                    h, p * 32 + m * 16 : p * 32 + m * 16 + 16, :
                ]

    exchanges = []

    def after_block(k):
        if k % 2:
            done = inverse.at[c, :, pl.ds(32 * (k - 1), 64)]
            exchanges.append(links.start(done, done, sibling))
            z_step()

    invert_factor(gram, inverse.at[c], after_block)
    for chain in chains:
        for _ in chain:
            pass

    def times_inverse(a, cc, kind):
        i_high, i_low = split(inverse[cc, kind])
        high, low = split(a)
        return bf16_dot(high, i_high, NT) + (
            bf16_dot(high, i_low, NT) + bf16_dot(low, i_high, NT)
        )

    def factor_of(i, cc, kind):
        row = i * 64 + kind * 32
        w = jnp.concatenate([wfull[k, row : row + 32, :] for k in range(8)], axis=0)
        factor = times_inverse(w, cc, kind)
        fac[2 * kind + cc] = factor
        squares = jnp.sum(factor * factor, axis=0, keepdims=True)
        return [squares[:, 0:128], squares[:, 128:256]]

    def ortho_half(cc):
        start = cc * HALF
        ow[cc] = times_inverse(raw_rows(start, WIDE), cc, 0)
        on[cc] = times_inverse(raw_rows(start + WIDE, NARROW), cc, 1)

    for kind in range(2):
        for h, squares in enumerate(factor_of(0, c, kind)):
            row = pl.ds(pl.multiple_of((2 * kind + c) * 2, 2) + h, 1)
            sq[row, :] = squares
    for copy in exchanges:
        copy.wait_recv()
    for kind in range(2):
        for h, squares in enumerate(factor_of(1, 1 - c, kind)):
            row = pl.ds(pl.multiple_of((2 * kind + 1 - c) * 2, 2) + h, 1)
            sq[row, :] = squares
    sq_land[0] = sq[...]
    sends = [links.start(sq_land.at[0], sq_land.at[d], device) for d, device in others]
    ortho_half(c)
    ortho_half(1 - c)
    total = sq_land[0]
    for (d, _), copy in zip(others, sends):
        copy.wait_recv()
        total = total + sq_land[d]
    sq[...] = total
    links.finish()


def last_kernel(
    bw, bn, ow, on, fac, sq, wmo, wbo, wup, nmo, nbo, nup, f_t, b_high, b_low
):
    kinds = ((bw, ow, wmo, wbo, wup, D), (bn, on, nmo, nbo, nup, KVW))

    @pl.when(pl.program_id(1) == 0)
    def _():
        for kind in range(2):
            factor = fac[kind, 0]
            basis = factor * lax.rsqrt(sq[kind, 0] + 1e-6)
            kinds[kind][3][0] = basis
            f_t[kind] = factor.astype(BF16).T
            b_high[kind], b_low[kind] = split(basis.T)

    for kind, (buffer, ortho, m_out, _, update, rows) in enumerate(kinds):
        o_high, o_low = split(ortho[0])
        m_out[0] = buffer[0] - 0.05 * bf16_dot(o_high, f_t[kind])
        product = bf16_dot(o_high, b_high[kind]) + (
            bf16_dot(o_high, b_low[kind]) + bf16_dot(o_low, b_high[kind])
        )
        update[0] = ((rows * D / RANK) ** 0.5 * product).astype(BF16)


def local(wide_momentum, wide_grad, wide_basis, narrow_momentum, narrow_grad, narrow_basis):
    vmem = pl.BlockSpec(memory_space=pltpu.VMEM)
    bw = wide_momentum + wide_grad.astype(F32)
    bn = narrow_momentum + narrow_grad.astype(F32)
    copies = 160
    ow, on, fac, sq = pl.pallas_call(
        main_kernel,
        out_shape=(
            jax.ShapeDtypeStruct((2, WIDE, RANK), F32),
            jax.ShapeDtypeStruct((2, NARROW, RANK), F32),
            jax.ShapeDtypeStruct((4, COLS, RANK), F32),
            jax.ShapeDtypeStruct((8, 128), F32),
        ),
        in_specs=[vmem] * 4,
        out_specs=[vmem] * 4,
        scratch_shapes=[
            pltpu.VMEM((2 * HALF, COLS), BF16),
            pltpu.VMEM((2 * HALF, COLS), BF16),
            pltpu.VMEM((2, 2, COLS, RANK), BF16),
            pltpu.VMEM((2, 2, COLS, RANK), BF16),
            pltpu.VMEM((2, 2 * HALF, 128), F32),
            pltpu.VMEM((2, 2 * HALF, 128), F32),
            pltpu.VMEM((2, HALF, 128), F32),
            pltpu.VMEM((2, 2, 2, 4, 160, 128), F32),
            pltpu.VMEM((2, RANK, RANK), F32),
            pltpu.VMEM((RANK, RANK), F32),
            pltpu.VMEM((COLS, RANK), F32),
            pltpu.VMEM((8, 8, 128), F32),
            pltpu.VMEM((7, 8, 128), F32),
            pltpu.VMEM((2, 512, 128), F32),
            pltpu.VMEM((8, 128, RANK), F32),
            pltpu.VMEM((8, 128, RANK), F32),
            pltpu.VMEM((2, 4, 128, RANK), F32),
            pltpu.VMEM((2, 2, RANK, RANK), F32),
            pltpu.VMEM((32, 8, 128), F32),
            pltpu.SemaphoreType.DMA((copies,)),
            pltpu.SemaphoreType.DMA((copies,)),
        ],
        compiler_params=pltpu.CompilerParams(
            collective_id=0, has_side_effects=True, vmem_limit_bytes=36 * 2**20
        ),
    )(bw, bn, wide_basis, narrow_basis)

    def rows(n):
        return pl.BlockSpec((1, n, COLS), lambda m, i: (m, i, 0))

    def whole(*lead):
        return pl.BlockSpec(lead, lambda m, i: (0, m, 0, 0))

    basis_out = pl.BlockSpec((1, COLS, RANK), lambda m, i: (m, 0, 0))
    steps = 2
    w, n = WIDE // steps, NARROW // steps
    return pl.pallas_call(
        last_kernel,
        grid=(2, steps),
        out_shape=(
            jax.ShapeDtypeStruct((2, WIDE, COLS), F32),
            jax.ShapeDtypeStruct((2, COLS, RANK), F32),
            jax.ShapeDtypeStruct((2, WIDE, COLS), BF16),
            jax.ShapeDtypeStruct((2, NARROW, COLS), F32),
            jax.ShapeDtypeStruct((2, COLS, RANK), F32),
            jax.ShapeDtypeStruct((2, NARROW, COLS), BF16),
        ),
        in_specs=[
            rows(w), rows(n), rows(w), rows(n),
            whole(2, 1, COLS, RANK), whole(2, 1, 1, RANK),
        ],
        out_specs=[rows(w), basis_out, rows(w), rows(n), basis_out, rows(n)],
        scratch_shapes=[pltpu.VMEM((2, RANK, COLS), BF16)] * 3,
        compiler_params=pltpu.CompilerParams(vmem_limit_bytes=24 * 2**20),
    )(
        bw, bn, ow, on,
        fac.reshape(2, 2, COLS, RANK), sq.reshape(2, 2, 1, RANK),
    )


def solution(mesh):
    return jax.shard_map(
        local,
        mesh=mesh,
        in_specs=(
            P(None, "mp", "fsdp"),
            P(None, "mp", "fsdp"),
            P(None, "fsdp", None),
            P(None, "mp", "fsdp"),
            P(None, "mp", "fsdp"),
            P(None, "fsdp", None),
        ),
        out_specs=(
            P(None, "mp", "fsdp"),
            P(None, "fsdp", None),
            P(None, "mp", "fsdp"),
            P(None, "mp", "fsdp"),
            P(None, "fsdp", None),
            P(None, "mp", "fsdp"),
        ),
        check_vma=False,
    )
```

```python
import jax
import jax.numpy as jnp
from jax import lax
from jax.experimental import pallas as pl
from jax.experimental.pallas import tpu as pltpu
from jax.sharding import PartitionSpec as P

D = 8192
KVW = 1024
RANK = 256
WIDE = 1024
NARROW = 128
COLS = 256
HALF = WIDE + NARROW
F32 = jnp.float32
BF16 = jnp.bfloat16
MESH = pl.DeviceIdType.MESH
EXACT = lax.Precision.HIGHEST

NN = (((1,), (0,)), ((), ()))
NT = (((1,), (1,)), ((), ()))
TN = (((0,), (0,)), ((), ()))


def exact_dot(a, b, dims=NN):
    return lax.dot_general(a, b, dims, precision=EXACT, preferred_element_type=F32)


def split(a):
    high = a.astype(BF16)
    return high, (a - high.astype(F32)).astype(BF16)


def bf16_dot(a, b, dims=NN):
    return lax.dot_general(a, b, dims, preferred_element_type=F32)


class Links:
    def __init__(self, send, recv):
        self.send, self.recv = send, recv
        self.count = 0
        self.started = []

    def start(self, src, dst, device):
        i = self.count
        self.count += 1
        copy = pltpu.make_async_remote_copy(
            src_ref=src,
            dst_ref=dst,
            send_sem=self.send.at[i],
            recv_sem=self.recv.at[i],
            device_id=device,
            device_id_type=MESH,
        )
        copy.start()
        self.started.append(copy)
        return copy

    def finish(self, most=None):
        n = len(self.started) if most is None else most
        for copy in self.started[:n]:
            copy.wait_send()
        self.started = self.started[n:]


def ring_reduce(links, buf, out, h, base, chunk, cut, q, peers, land):
    after, before = (q + 1) % 4, (q + 3) % 4
    right, left = peers[0], peers[2]

    def rows(c, lo, n):
        return pl.ds(pl.multiple_of(base + c * chunk + lo, 8), n)

    far = (q + 2) % 4
    a = links.start(buf.at[h, rows(far, 0, cut)], land.at[0, pl.ds(0, cut)], right)
    b = links.start(
        buf.at[h, rows(far, cut, chunk - cut)], land.at[1, pl.ds(0, chunk - cut)], left
    )
    yield
    a.wait_recv()
    buf[h, rows(after, 0, cut), :] += land[0, 0:cut, :]
    a = links.start(buf.at[h, rows(after, 0, chunk)], land.at[2, pl.ds(0, chunk)], right)
    b.wait_recv()
    buf[h, rows(before, cut, chunk - cut), :] += land[1, 0 : chunk - cut, :]
    b = links.start(buf.at[h, rows(before, 0, chunk)], land.at[3, pl.ds(0, chunk)], left)
    yield
    a.wait_recv()
    b.wait_recv()
    out[h, rows(q, 0, chunk), :] = (
        buf[h, rows(q, 0, chunk), :] + land[2, 0:chunk, :] + land[3, 0:chunk, :]
    )


def ring_gather(links, buf, h, base, chunk, cut, q, peers):
    after, before = (q + 1) % 4, (q + 3) % 4
    right, left = peers[0], peers[2]

    def part(c, lo, n):
        return buf.at[h, pl.ds(pl.multiple_of(base + c * chunk + lo, 8), n)]

    own = part(q, 0, chunk)
    a = links.start(own, own, right)
    b = links.start(own, own, left)
    yield
    a.wait_recv()
    piece = part(before, 0, cut)
    a = links.start(piece, piece, right)
    b.wait_recv()
    piece = part(after, cut, chunk - cut)
    b = links.start(piece, piece, left)
    yield
    a.wait_recv()
    b.wait_recv()


def direct_reduce(links, buf, out, h, base, chunk, q, peers, land):
    def rows(c):
        return pl.ds(pl.multiple_of(base + c * chunk, 8), chunk)

    copies = [
        links.start(buf.at[h, rows((q + d) % 4)], land.at[d, pl.ds(0, chunk)], peers[d - 1])
        for d in (2, 1, 3)
    ]
    yield
    for copy in copies:
        copy.wait_recv()
    total = buf[h, rows(q), :]
    for d in (1, 2, 3):
        total = total + land[d, 0:chunk, :]
    out[h, rows(q), :] = total


def direct_gather(links, buf, h, base, chunk, q, peers):
    own = buf.at[h, pl.ds(pl.multiple_of(base + q * chunk, 8), chunk)]
    copies = [links.start(own, own, peers[d - 1]) for d in (2, 1, 3)]
    yield
    for copy in copies:
        copy.wait_recv()


def z_reduce_gather(links, buf, out, land, lo, n, q, right, left):
    half = n // 2

    def part(ref, i, start, size):
        return ref.at[i, pl.ds(lo + start, size)]

    def chunk(ref, i):
        return part(ref, i % 8, 0, n)

    def add(i, slot, start, size):
        rows = slice(lo + start, lo + start + size)
        buf[i % 8, rows, :] += land[slot[0], slot[1], rows, :]

    a = links.start(
        part(buf, (q + 4) % 8, 0, half), part(land.at[0], 0, 0, half), right
    )
    b = links.start(
        part(buf, (q + 4) % 8, half, half), part(land.at[1], 0, half, half), left
    )
    yield
    for s in (1, 2, 3):
        size = half if s == 1 else n
        a.wait_recv()
        add(q + 4 - s, (0, s - 1), 0, size)
        a = links.start(chunk(buf, q + 4 - s), part(land.at[0], s, 0, n), right)
        b.wait_recv()
        add(q + 4 + s, (1, s - 1), n - size, size)
        b = links.start(chunk(buf, q + 4 + s), part(land.at[1], s, 0, n), left)
        yield
    a.wait_recv()
    b.wait_recv()
    rows = slice(lo, lo + n)
    out[q, rows, :] = buf[q, rows, :] + land[0, 3, rows, :] + land[1, 3, rows, :]
    a = links.start(chunk(out, q), chunk(out, q), right)
    b = links.start(chunk(out, q), chunk(out, q), left)
    yield
    for s in (1, 2):
        a.wait_recv()
        a = links.start(chunk(out, q + 8 - s), chunk(out, q + 8 - s), right)
        b.wait_recv()
        b = links.start(chunk(out, q + s), chunk(out, q + s), left)
        yield
    a.wait_recv()
    piece = part(out, (q + 5) % 8, 0, half)
    a = links.start(piece, piece, right)
    b.wait_recv()
    piece = part(out, (q + 3) % 8, half, half)
    b = links.start(piece, piece, left)
    yield
    a.wait_recv()
    b.wait_recv()


def together(*stages):
    done = object()
    live = list(stages)
    while live:
        live = [s for s in live if next(s, done) is not done]


def block_inverse(e):
    lane = lax.broadcasted_iota(jnp.int32, (8, 128), 1)
    sub = lax.broadcasted_iota(jnp.int32, (8, 128), 0)
    group = (lane // 64) * 64

    def pick(tile, index):
        return jnp.take_along_axis(tile, group + index, axis=1)

    e = list(e)
    for g in range(4):
        cols = [[pick(e[i], 8 * g + t) for i in range(g, 4)] for t in range(8)]
        for t in range(8):
            pivot = cols[t][0][t : t + 1, :]
            inv = pl.reciprocal(pivot, approx=True)
            inv = inv * (2.0 - pivot * inv)
            for n, i in enumerate(range(g, 4)):
                f = cols[t][n] * inv
                if n == 0:
                    f = jnp.where(sub > t, f, 0.0)
                e[i] = e[i] - f * e[g][t : t + 1, :]
                for s in range(t + 1, 8):
                    cols[s][n] = cols[s][n] - f * cols[s][0][t : t + 1, :]
    return [tile * lax.rsqrt(pick(tile, 8 * i + sub)) for i, tile in enumerate(e)]


def invert_factor(a_ref, out, after):
    lane = lax.broadcasted_iota(jnp.int32, (32, 128), 1)
    row = lax.broadcasted_iota(jnp.int32, (32, 128), 0)
    eye = jnp.where(lane % 32 == row, 1.0, 0.0)
    col = lax.broadcasted_iota(jnp.int32, (32, 256), 1)
    wide_row = lax.broadcasted_iota(jnp.int32, (32, 256), 0)

    def turned(v, by):
        return pltpu.roll(v, by % 128, 1) if by % 128 else v

    blocks = [a_ref[m, 0:32, 0:128] for m in range(2)]
    panels = None
    for k in range(8):
        at, below = 32 * k, 32 * k + 32
        base, low = at // 128 * 128, below // 128 * 128
        if k > 0:
            for m in range(2):
                change = exact_dot(panels[m][:, base:256], panels[m], TN)
                under = lax.broadcasted_iota(jnp.int32, (256 - at, 256), 1)
                rest = jnp.where(
                    (under >= at - 32) & (under < at), 0.0, a_ref[m, at:256, :]
                )
                a_ref[m, at:256, :] = rest - change[at - base :, :]
        d0, d1 = turned(blocks[0], base - at), turned(blocks[1], 64 + base - at)
        e = jnp.where(lane < 32, d0, jnp.where((lane >= 64) & (lane < 96), d1, eye))
        e = jnp.concatenate(
            block_inverse([e[8 * i : 8 * i + 8] for i in range(4)]), axis=0
        )
        inside = (col >= at) & (col < below)
        wide_eye = jnp.where(col - at == wide_row, 1.0, 0.0)
        panels, blocks = [], []
        for m in range(2):
            t = turned(e, 96 - 64 * m)[:, 0:32]
            panel = exact_dot(t, jnp.where(inside, wide_eye, a_ref[m, at:below, :]))
            panels.append(panel)
            if below < 256:
                near = panel[:, low : low + 128]
                change = exact_dot(near, near, TN)
                blocks.append(
                    a_ref[m, below : below + 32, low : low + 128]
                    - change[below - low : below - low + 32, :]
                )
            a_ref[m, at:below, :] = panel
            out[m, at:below, :] = jnp.where(col <= at + wide_row, panel, 0.0)
        after(k)


def main_kernel(
    bw, bn, wb, nb,
    ow, on, fac, sq,
    bh, bl, vh, vl, part, full, swap, land, gram, cross, slices, zland, gathered,
    wpart, wfull, wland, inverse, sq_land,
    send, recv,
):
    z = lax.axis_index("mp")
    f = lax.axis_index("fsdp")
    c = f % 2
    x = (f // 2) % 4
    y = f // 8

    def plane(xx, yy, cc):
        return {"fsdp": ((yy % 4) * 4 + xx % 4) * 2 + cc}

    sibling = plane(x, y, 1 - c)
    xs = [plane(x + d, y, c) for d in (1, 2, 3)]
    others = [(d, {"fsdp": (f + d) % 32}) for d in range(1, 32)]
    ys = [plane(x, y + d, c) for d in (1, 2, 3)]
    zs = [{"mp": (z + d) % 8} for d in range(1, 8)]

    barrier = pltpu.get_barrier_semaphore()
    partners = [device for _, device in others] + zs
    for device in partners:
        pl.semaphore_signal(barrier, inc=1, device_id=device, device_id_type=MESH)

    links = Links(send, recv)

    def split_basis(cc):
        for kind, basis in enumerate((wb, nb)):
            high, low = split(basis[cc])
            vh[cc, kind] = high
            vl[cc, kind] = low

    def raw_rows_of(cc, kind, r, n, buffer):
        rows = pl.ds(pl.multiple_of(cc * HALF + r, 16), n)
        high, low = split(buffer)
        bh[rows, :] = high
        bl[rows, :] = low
        v_high = vh[cc, kind]
        raw = bf16_dot(high, v_high) + (bf16_dot(high, vl[cc, kind]) + bf16_dot(low, v_high))
        part[0, rows, :] = raw[:, 0:128]
        part[1, rows, :] = raw[:, 128:256]

    def raw_half(cc):
        split_basis(cc)
        raw_rows_of(cc, 0, 0, 512, bw[cc, 0:512, :])
        raw_rows_of(cc, 0, 512, 512, bw[cc, 512:1024, :])
        raw_rows_of(cc, 1, WIDE, NARROW, bn[cc])

    def half_rows(cc, start, n):
        return pl.ds(pl.multiple_of(cc * HALF + start, 8), n)

    raw_half(1 - c)
    pl.semaphore_wait(barrier, len(partners))
    mine = half_rows(c, 0, HALF)
    exchange = links.start(part.at[:, half_rows(1 - c, 0, HALF)], swap, sibling)
    raw_half(c)
    exchange.wait_recv()
    part[:, mine, :] += swap[...]

    x_ring = dict(q=x, peers=xs)
    y_ring = dict(q=y, peers=ys)
    base = c * HALF

    def gather_both(buffer, h, start, sizes, first, second):
        yield from direct_gather(
            links, buffer, h, start + first["q"] * sizes[0], sizes[1], **second
        )
        yield from ring_gather(links, buffer, h, start, sizes[0], sizes[0] // 2, **first)

    shares = []

    big, small = HALF // 4, HALF // 16

    def whole_sum(h):
        first, second = (x_ring, y_ring) if h == 0 else (y_ring, x_ring)
        yield from ring_reduce(
            links, part, part, h, base, big, big // 2, land=land.at[h, 0], **first
        )
        yield from direct_reduce(
            links, part, full, h, base + first["q"] * big, small, land=land.at[h, 1], **second
        )
        yield from gather_both(full, h, base, (big, small), first, second)
        done = full.at[h, mine]
        shares.append(links.start(done, done, sibling))

    together(whole_sum(0), whole_sum(1))

    def raw_rows(start, n):
        rows = pl.ds(pl.multiple_of(start, 8), n)
        return jnp.concatenate([full[0, rows, :], full[1, rows, :]], axis=1)

    def own_gram(start, n):
        raw = raw_rows(base + start, n)
        high = raw.astype(BF16)
        middle, low = split(raw - high.astype(F32))
        cross[...] = bf16_dot(high, middle, TN) + bf16_dot(high, low, TN)
        mirrored = cross[...] + cross[...].T
        return bf16_dot(high, high, TN) + (mirrored + bf16_dot(middle, middle, TN))

    def w_of(cc, start, n):
        start = cc * HALF + start
        rows = pl.ds(pl.multiple_of(start, 16), n)
        high, low = split(raw_rows(start, n))
        b_high = bh[rows, :]
        return bf16_dot(b_high, high, TN) + (
            bf16_dot(b_high, low, TN) + bf16_dot(bl[rows, :], high, TN)
        )

    gram[0] = own_gram(0, WIDE)
    gram[1] = own_gram(WIDE, NARROW)

    places = (x * 4 + y, y * 4 + x)
    for t in range(8):
        h, m, r = t // 4, (t // 2) % 2, t % 2
        rows = pl.ds(pl.multiple_of(places[h] * 16 + r * 8, 8), 8)
        slices[t] = gram[m, rows, h * 128 : h * 128 + 128]
    gram_sends = [
        links.start(slices.at[(z + d) % 8], zland.at[d - 1], zs[d - 1]) for d in range(1, 8)
    ]

    def put_w(i, kind, w):
        row = i * 64 + kind * 32
        for k in range(8):
            wpart[k, row : row + 32, :] = w[k * 32 : k * 32 + 32, :]

    def z_chain(i):
        return z_reduce_gather(links, wpart, wfull, wland, 64 * i, 64, z, zs[0], zs[6])

    put_w(0, 0, w_of(c, 0, WIDE))
    put_w(0, 1, w_of(c, WIDE, NARROW))
    chains = [z_chain(0)]
    next(chains[0])

    def z_step():
        for chain in chains:
            next(chain, None)

    for copy in gram_sends:
        copy.wait_recv()
    total = slices[z]
    for d in range(7):
        total = total + zland[d]
    place = places[0] + (z // 4) * (places[1] - places[0])
    own = gathered.at[z // 4, pl.ds(pl.multiple_of(place * 32 + (z % 4) * 8, 8), 8)]
    own[...] = total
    gram_sends = [links.start(own, own, zs[d]) for d in range(7)]
    for copy in shares:
        copy.wait_recv()
    put_w(1, 0, w_of(1 - c, 0, WIDE))
    put_w(1, 1, w_of(1 - c, WIDE, NARROW))
    z_step()
    chains.append(z_chain(1))
    next(chains[1])
    for copy in gram_sends:
        copy.wait_recv()
    stages = [
        gather_both(gathered, 0, 0, (128, 32), x_ring, y_ring),
        gather_both(gathered, 1, 0, (128, 32), y_ring, x_ring),
    ]
    for i in range(4):
        for stage in stages:
            next(stage, None)
        if i < 3:
            links.finish(24)
        z_step()
    for h in range(2):
        for p in range(16):
            for m in range(2):
                gram[m, p * 16 : p * 16 + 16, h * 128 : h * 128 + 128] = gathered[
                    h, p * 32 + m * 16 : p * 32 + m * 16 + 16, :
                ]

    exchanges = []

    def after_block(k):
        if k % 2:
            done = inverse.at[c, :, pl.ds(32 * (k - 1), 64)]
            exchanges.append(links.start(done, done, sibling))
            z_step()

    invert_factor(gram, inverse.at[c], after_block)
    for chain in chains:
        for _ in chain:
            pass

    def times_inverse(a, cc, kind):
        i_high, i_low = split(inverse[cc, kind])
        high, low = split(a)
        return bf16_dot(high, i_high, NT) + (
            bf16_dot(high, i_low, NT) + bf16_dot(low, i_high, NT)
        )

    def factor_of(i, cc, kind):
        row = i * 64 + kind * 32
        w = jnp.concatenate([wfull[k, row : row + 32, :] for k in range(8)], axis=0)
        factor = times_inverse(w, cc, kind)
        fac[2 * kind + cc] = factor
        squares = jnp.sum(factor * factor, axis=0, keepdims=True)
        return [squares[:, 0:128], squares[:, 128:256]]

    def ortho_half(cc):
        start = cc * HALF
        ow[cc] = times_inverse(raw_rows(start, WIDE), cc, 0)
        on[cc] = times_inverse(raw_rows(start + WIDE, NARROW), cc, 1)

    for kind in range(2):
        for h, squares in enumerate(factor_of(0, c, kind)):
            row = pl.ds(pl.multiple_of((2 * kind + c) * 2, 2) + h, 1)
            sq[row, :] = squares
    for copy in exchanges:
        copy.wait_recv()
    for kind in range(2):
        for h, squares in enumerate(factor_of(1, 1 - c, kind)):
            row = pl.ds(pl.multiple_of((2 * kind + 1 - c) * 2, 2) + h, 1)
            sq[row, :] = squares
    sq_land[0] = sq[...]
    sends = [links.start(sq_land.at[0], sq_land.at[d], device) for d, device in others]
    ortho_half(c)
    ortho_half(1 - c)
    total = sq_land[0]
    for (d, _), copy in zip(others, sends):
        copy.wait_recv()
        total = total + sq_land[d]
    sq[...] = total
    links.finish()


def last_kernel(
    bw, bn, ow, on, fac, sq, wmo, wbo, wup, nmo, nbo, nup, f_t, b_high, b_low
):
    kinds = ((bw, ow, wmo, wbo, wup, D), (bn, on, nmo, nbo, nup, KVW))

    @pl.when(pl.program_id(1) == 0)
    def _():
        for kind in range(2):
            factor = fac[kind, 0]
            basis = factor * lax.rsqrt(sq[kind, 0] + 1e-6)
            kinds[kind][3][0] = basis
            f_t[kind] = factor.astype(BF16).T
            b_high[kind], b_low[kind] = split(basis.T)

    for kind, (buffer, ortho, m_out, _, update, rows) in enumerate(kinds):
        o_high, o_low = split(ortho[0])
        m_out[0] = buffer[0] - 0.05 * bf16_dot(o_high, f_t[kind])
        product = bf16_dot(o_high, b_high[kind]) + (
            bf16_dot(o_high, b_low[kind]) + bf16_dot(o_low, b_high[kind])
        )
        update[0] = ((rows * D / RANK) ** 0.5 * product).astype(BF16)


def local(wide_momentum, wide_grad, wide_basis, narrow_momentum, narrow_grad, narrow_basis):
    vmem = pl.BlockSpec(memory_space=pltpu.VMEM)
    bw = wide_momentum + wide_grad.astype(F32)
    bn = narrow_momentum + narrow_grad.astype(F32)
    copies = 136
    ow, on, fac, sq = pl.pallas_call(
        main_kernel,
        out_shape=(
            jax.ShapeDtypeStruct((2, WIDE, RANK), F32),
            jax.ShapeDtypeStruct((2, NARROW, RANK), F32),
            jax.ShapeDtypeStruct((4, COLS, RANK), F32),
            jax.ShapeDtypeStruct((8, 128), F32),
        ),
        in_specs=[vmem] * 4,
        out_specs=[vmem] * 4,
        scratch_shapes=[
            pltpu.VMEM((2 * HALF, COLS), BF16),
            pltpu.VMEM((2 * HALF, COLS), BF16),
            pltpu.VMEM((2, 2, COLS, RANK), BF16),
            pltpu.VMEM((2, 2, COLS, RANK), BF16),
            pltpu.VMEM((2, 2 * HALF, 128), F32),
            pltpu.VMEM((2, 2 * HALF, 128), F32),
            pltpu.VMEM((2, HALF, 128), F32),
            pltpu.VMEM((2, 2, 4, 288, 128), F32),
            pltpu.VMEM((2, RANK, RANK), F32),
            pltpu.VMEM((RANK, RANK), F32),
            pltpu.VMEM((8, 8, 128), F32),
            pltpu.VMEM((7, 8, 128), F32),
            pltpu.VMEM((2, 512, 128), F32),
            pltpu.VMEM((8, 128, RANK), F32),
            pltpu.VMEM((8, 128, RANK), F32),
            pltpu.VMEM((2, 4, 128, RANK), F32),
            pltpu.VMEM((2, 2, RANK, RANK), F32),
            pltpu.VMEM((32, 8, 128), F32),
            pltpu.SemaphoreType.DMA((copies,)),
            pltpu.SemaphoreType.DMA((copies,)),
        ],
        compiler_params=pltpu.CompilerParams(
            collective_id=0, has_side_effects=True, vmem_limit_bytes=36 * 2**20
        ),
    )(bw, bn, wide_basis, narrow_basis)

    def rows(n):
        return pl.BlockSpec((1, n, COLS), lambda m, i: (m, i, 0))

    def whole(*lead):
        return pl.BlockSpec(lead, lambda m, i: (0, m, 0, 0))

    basis_out = pl.BlockSpec((1, COLS, RANK), lambda m, i: (m, 0, 0))
    steps = 2
    w, n = WIDE // steps, NARROW // steps
    return pl.pallas_call(
        last_kernel,
        grid=(2, steps),
        out_shape=(
            jax.ShapeDtypeStruct((2, WIDE, COLS), F32),
            jax.ShapeDtypeStruct((2, COLS, RANK), F32),
            jax.ShapeDtypeStruct((2, WIDE, COLS), BF16),
            jax.ShapeDtypeStruct((2, NARROW, COLS), F32),
            jax.ShapeDtypeStruct((2, COLS, RANK), F32),
            jax.ShapeDtypeStruct((2, NARROW, COLS), BF16),
        ),
        in_specs=[
            rows(w), rows(n), rows(w), rows(n),
            whole(2, 1, COLS, RANK), whole(2, 1, 1, RANK),
        ],
        out_specs=[rows(w), basis_out, rows(w), rows(n), basis_out, rows(n)],
        scratch_shapes=[pltpu.VMEM((2, RANK, COLS), BF16)] * 3,
        compiler_params=pltpu.CompilerParams(vmem_limit_bytes=24 * 2**20),
    )(
        bw, bn, ow, on,
        fac.reshape(2, 2, COLS, RANK), sq.reshape(2, 2, 1, RANK),
    )


def solution(mesh):
    return jax.shard_map(
        local,
        mesh=mesh,
        in_specs=(
            P(None, "mp", "fsdp"),
            P(None, "mp", "fsdp"),
            P(None, "fsdp", None),
            P(None, "mp", "fsdp"),
            P(None, "mp", "fsdp"),
            P(None, "fsdp", None),
        ),
        out_specs=(
            P(None, "mp", "fsdp"),
            P(None, "fsdp", None),
            P(None, "mp", "fsdp"),
            P(None, "mp", "fsdp"),
            P(None, "fsdp", None),
            P(None, "mp", "fsdp"),
        ),
        check_vma=False,
    )
```

```python
import jax
import jax.numpy as jnp
from jax import lax
from jax.experimental import pallas as pl
from jax.experimental.pallas import tpu as pltpu
from jax.sharding import PartitionSpec as P

D = 8192
KVW = 1024
RANK = 256
WIDE = 1024
NARROW = 128
COLS = 256
HALF = WIDE + NARROW
F32 = jnp.float32
BF16 = jnp.bfloat16
MESH = pl.DeviceIdType.MESH
EXACT = lax.Precision.HIGHEST

NN = (((1,), (0,)), ((), ()))
NT = (((1,), (1,)), ((), ()))
TN = (((0,), (0,)), ((), ()))


def exact_dot(a, b, dims=NN):
    return lax.dot_general(a, b, dims, precision=EXACT, preferred_element_type=F32)


def split(a):
    high = a.astype(BF16)
    return high, (a - high.astype(F32)).astype(BF16)


def bf16_dot(a, b, dims=NN):
    return lax.dot_general(a, b, dims, preferred_element_type=F32)


class Links:
    def __init__(self, send, recv):
        self.send, self.recv = send, recv
        self.count = 0
        self.started = []

    def start(self, src, dst, device):
        i = self.count
        self.count += 1
        copy = pltpu.make_async_remote_copy(
            src_ref=src,
            dst_ref=dst,
            send_sem=self.send.at[i],
            recv_sem=self.recv.at[i],
            device_id=device,
            device_id_type=MESH,
        )
        copy.start()
        self.started.append(copy)
        return copy

    def finish(self, most=None):
        n = len(self.started) if most is None else most
        for copy in self.started[:n]:
            copy.wait_send()
        self.started = self.started[n:]


def ring_reduce(links, buf, out, h, base, chunk, cut, q, peers, land):
    after, before = (q + 1) % 4, (q + 3) % 4
    right, left = peers[0], peers[2]

    def rows(c, lo, n):
        return pl.ds(pl.multiple_of(base + c * chunk + lo, 8), n)

    far = (q + 2) % 4
    a = links.start(buf.at[h, rows(far, 0, cut)], land.at[0, pl.ds(0, cut)], right)
    b = links.start(
        buf.at[h, rows(far, cut, chunk - cut)], land.at[1, pl.ds(0, chunk - cut)], left
    )
    yield
    a.wait_recv()
    buf[h, rows(after, 0, cut), :] += land[0, 0:cut, :]
    a = links.start(buf.at[h, rows(after, 0, chunk)], land.at[2, pl.ds(0, chunk)], right)
    b.wait_recv()
    buf[h, rows(before, cut, chunk - cut), :] += land[1, 0 : chunk - cut, :]
    b = links.start(buf.at[h, rows(before, 0, chunk)], land.at[3, pl.ds(0, chunk)], left)
    yield
    a.wait_recv()
    b.wait_recv()
    out[h, rows(q, 0, chunk), :] = (
        buf[h, rows(q, 0, chunk), :] + land[2, 0:chunk, :] + land[3, 0:chunk, :]
    )


def ring_gather(links, buf, h, base, chunk, cut, q, peers):
    after, before = (q + 1) % 4, (q + 3) % 4
    right, left = peers[0], peers[2]

    def part(c, lo, n):
        return buf.at[h, pl.ds(pl.multiple_of(base + c * chunk + lo, 8), n)]

    own = part(q, 0, chunk)
    a = links.start(own, own, right)
    b = links.start(own, own, left)
    yield
    a.wait_recv()
    piece = part(before, 0, cut)
    a = links.start(piece, piece, right)
    b.wait_recv()
    piece = part(after, cut, chunk - cut)
    b = links.start(piece, piece, left)
    yield
    a.wait_recv()
    b.wait_recv()


def direct_reduce(links, buf, out, h, base, chunk, q, peers, land):
    def rows(c):
        return pl.ds(pl.multiple_of(base + c * chunk, 8), chunk)

    copies = [
        links.start(buf.at[h, rows((q + d) % 4)], land.at[d, pl.ds(0, chunk)], peers[d - 1])
        for d in (2, 1, 3)
    ]
    yield
    for copy in copies:
        copy.wait_recv()
    total = buf[h, rows(q), :]
    for d in (1, 2, 3):
        total = total + land[d, 0:chunk, :]
    out[h, rows(q), :] = total


def direct_gather(links, buf, h, base, chunk, q, peers):
    own = buf.at[h, pl.ds(pl.multiple_of(base + q * chunk, 8), chunk)]
    copies = [links.start(own, own, peers[d - 1]) for d in (2, 1, 3)]
    yield
    for copy in copies:
        copy.wait_recv()


def z_reduce_gather(links, buf, out, land, lo, n, q, right, left):
    half = n // 2

    def part(ref, i, start, size):
        return ref.at[i, pl.ds(lo + start, size)]

    def chunk(ref, i):
        return part(ref, i % 8, 0, n)

    def add(i, slot, start, size):
        rows = slice(lo + start, lo + start + size)
        buf[i % 8, rows, :] += land[slot[0], slot[1], rows, :]

    a = links.start(
        part(buf, (q + 4) % 8, 0, half), part(land.at[0], 0, 0, half), right
    )
    b = links.start(
        part(buf, (q + 4) % 8, half, half), part(land.at[1], 0, half, half), left
    )
    yield
    for s in (1, 2, 3):
        size = half if s == 1 else n
        a.wait_recv()
        add(q + 4 - s, (0, s - 1), 0, size)
        a = links.start(chunk(buf, q + 4 - s), part(land.at[0], s, 0, n), right)
        b.wait_recv()
        add(q + 4 + s, (1, s - 1), n - size, size)
        b = links.start(chunk(buf, q + 4 + s), part(land.at[1], s, 0, n), left)
        yield
    a.wait_recv()
    b.wait_recv()
    rows = slice(lo, lo + n)
    out[q, rows, :] = buf[q, rows, :] + land[0, 3, rows, :] + land[1, 3, rows, :]
    a = links.start(chunk(out, q), chunk(out, q), right)
    b = links.start(chunk(out, q), chunk(out, q), left)
    yield
    for s in (1, 2):
        a.wait_recv()
        a = links.start(chunk(out, q + 8 - s), chunk(out, q + 8 - s), right)
        b.wait_recv()
        b = links.start(chunk(out, q + s), chunk(out, q + s), left)
        yield
    a.wait_recv()
    piece = part(out, (q + 5) % 8, 0, half)
    a = links.start(piece, piece, right)
    b.wait_recv()
    piece = part(out, (q + 3) % 8, half, half)
    b = links.start(piece, piece, left)
    yield
    a.wait_recv()
    b.wait_recv()


def together(first, second, after):
    done = object()
    ended = False
    while first or second:
        first = [s for s in first if next(s, done) is not done]
        if not first and not ended:
            after()
            ended = True
        second = [s for s in second if next(s, done) is not done]


def block_inverse(e):
    lane = lax.broadcasted_iota(jnp.int32, (8, 128), 1)
    sub = lax.broadcasted_iota(jnp.int32, (8, 128), 0)
    group = (lane // 64) * 64

    def pick(tile, index):
        return jnp.take_along_axis(tile, group + index, axis=1)

    e = list(e)
    for g in range(4):
        cols = [[pick(e[i], 8 * g + t) for i in range(g, 4)] for t in range(8)]
        for t in range(8):
            pivot = cols[t][0][t : t + 1, :]
            inv = pl.reciprocal(pivot, approx=True)
            inv = inv * (2.0 - pivot * inv)
            for n, i in enumerate(range(g, 4)):
                f = cols[t][n] * inv
                if n == 0:
                    f = jnp.where(sub > t, f, 0.0)
                e[i] = e[i] - f * e[g][t : t + 1, :]
                for s in range(t + 1, 8):
                    cols[s][n] = cols[s][n] - f * cols[s][0][t : t + 1, :]
    return [tile * lax.rsqrt(pick(tile, 8 * i + sub)) for i, tile in enumerate(e)]


def invert_factor(a_ref, out, after):
    lane = lax.broadcasted_iota(jnp.int32, (32, 128), 1)
    row = lax.broadcasted_iota(jnp.int32, (32, 128), 0)
    eye = jnp.where(lane % 32 == row, 1.0, 0.0)
    col = lax.broadcasted_iota(jnp.int32, (32, 256), 1)
    wide_row = lax.broadcasted_iota(jnp.int32, (32, 256), 0)

    def turned(v, by):
        return pltpu.roll(v, by % 128, 1) if by % 128 else v

    blocks = [a_ref[m, 0:32, 0:128] for m in range(2)]
    panels = None
    for k in range(8):
        at, below = 32 * k, 32 * k + 32
        base, low = at // 128 * 128, below // 128 * 128
        if k > 0:
            for m in range(2):
                change = exact_dot(panels[m][:, base:256], panels[m], TN)
                under = lax.broadcasted_iota(jnp.int32, (256 - at, 256), 1)
                rest = jnp.where(
                    (under >= at - 32) & (under < at), 0.0, a_ref[m, at:256, :]
                )
                a_ref[m, at:256, :] = rest - change[at - base :, :]
        d0, d1 = turned(blocks[0], base - at), turned(blocks[1], 64 + base - at)
        e = jnp.where(lane < 32, d0, jnp.where((lane >= 64) & (lane < 96), d1, eye))
        e = jnp.concatenate(
            block_inverse([e[8 * i : 8 * i + 8] for i in range(4)]), axis=0
        )
        inside = (col >= at) & (col < below)
        wide_eye = jnp.where(col - at == wide_row, 1.0, 0.0)
        panels, blocks = [], []
        for m in range(2):
            t = turned(e, 96 - 64 * m)[:, 0:32]
            panel = exact_dot(t, jnp.where(inside, wide_eye, a_ref[m, at:below, :]))
            panels.append(panel)
            if below < 256:
                near = panel[:, low : low + 128]
                change = exact_dot(near, near, TN)
                blocks.append(
                    a_ref[m, below : below + 32, low : low + 128]
                    - change[below - low : below - low + 32, :]
                )
            a_ref[m, at:below, :] = panel
            out[m, at:below, :] = jnp.where(col <= at + wide_row, panel, 0.0)
        after(k)


def main_kernel(
    bw, bn, wb, nb,
    ow, on, fac, sq,
    bh, bl, vh, vl, part, full, swap, land, gram, cross, w_first, slices, zland, gathered,
    wpart, wfull, wland, inverse, sq_land,
    send, recv,
):
    z = lax.axis_index("mp")
    f = lax.axis_index("fsdp")
    c = f % 2
    x = (f // 2) % 4
    y = f // 8

    def plane(xx, yy, cc):
        return {"fsdp": ((yy % 4) * 4 + xx % 4) * 2 + cc}

    sibling = plane(x, y, 1 - c)
    xs = [plane(x + d, y, c) for d in (1, 2, 3)]
    others = [(d, {"fsdp": (f + d) % 32}) for d in range(1, 32)]
    ys = [plane(x, y + d, c) for d in (1, 2, 3)]
    zs = [{"mp": (z + d) % 8} for d in range(1, 8)]

    barrier = pltpu.get_barrier_semaphore()
    partners = [device for _, device in others] + zs
    for device in partners:
        pl.semaphore_signal(barrier, inc=1, device_id=device, device_id_type=MESH)

    links = Links(send, recv)
    sets = ((0, 640), (640, 512))
    wide_b = WIDE - 640

    def split_basis(cc):
        for kind, basis in enumerate((wb, nb)):
            high, low = split(basis[cc])
            vh[cc, kind] = high
            vl[cc, kind] = low

    def raw_rows_of(cc, kind, r, n, buffer):
        rows = pl.ds(pl.multiple_of(cc * HALF + r, 16), n)
        high, low = split(buffer)
        bh[rows, :] = high
        bl[rows, :] = low
        v_high = vh[cc, kind]
        raw = bf16_dot(high, v_high) + (bf16_dot(high, vl[cc, kind]) + bf16_dot(low, v_high))
        part[0, rows, :] = raw[:, 0:128]
        part[1, rows, :] = raw[:, 128:256]

    def raw_set(cc, i):
        lo, n = ((0, 640), (640, wide_b))[i]
        raw_rows_of(cc, 0, lo, n, bw[cc, lo : lo + n, :])

        if i == 1:
            raw_rows_of(cc, 1, WIDE, NARROW, bn[cc])

    def half_rows(cc, start, n):
        return pl.ds(pl.multiple_of(cc * HALF + start, 8), n)

    split_basis(1 - c)
    raw_set(1 - c, 0)
    pl.semaphore_wait(barrier, len(partners))
    exchanges = []
    for i, (start, n) in enumerate(sets):
        if i == 1:
            raw_set(1 - c, 1)
        exchanges.append(
            links.start(
                part.at[:, half_rows(1 - c, start, n)], swap.at[:, pl.ds(start, n)], sibling
            )
        )
    split_basis(c)

    x_ring = dict(q=x, peers=xs)
    y_ring = dict(q=y, peers=ys)
    base = c * HALF

    def gather_both(buffer, h, start, sizes, first, second):
        yield from direct_gather(
            links, buffer, h, start + first["q"] * sizes[0], sizes[1], **second
        )
        yield from ring_gather(links, buffer, h, start, sizes[0], sizes[0] // 2, **first)

    shares = []

    def whole_sum(i, h):
        start, n = sets[i]
        big, small = n // 4, n // 16
        first, second = (x_ring, y_ring) if h == 0 else (y_ring, x_ring)
        yield from ring_reduce(
            links, part, part, h, base + start, big, big // 2, land=land.at[i, h, 0], **first
        )
        yield from direct_reduce(
            links, part, full, h, base + start + first["q"] * big, small,
            land=land.at[i, h, 1], **second
        )
        yield from gather_both(full, h, base + start, (big, small), first, second)
        done = full.at[h, half_rows(c, start, n)]
        shares.append(links.start(done, done, sibling))

    stages = []
    for i, (start, n) in enumerate(sets):
        raw_set(c, i)
        exchanges[i].wait_recv()
        rows = half_rows(c, start, n)
        part[:, rows, :] += swap[:, start : start + n, :]
        for h in range(2):
            stage = whole_sum(i, h)
            next(stage)
            stages.append(stage)

    def raw_rows(start, n):
        rows = pl.ds(pl.multiple_of(start, 8), n)
        return jnp.concatenate([full[0, rows, :], full[1, rows, :]], axis=1)

    def own_gram(start, n):
        raw = raw_rows(base + start, n)
        high = raw.astype(BF16)
        middle, low = split(raw - high.astype(F32))
        cross[...] = bf16_dot(high, middle, TN) + bf16_dot(high, low, TN)
        mirrored = cross[...] + cross[...].T
        return bf16_dot(high, high, TN) + (mirrored + bf16_dot(middle, middle, TN))

    def w_of(cc, start, n):
        start = cc * HALF + start
        rows = pl.ds(pl.multiple_of(start, 16), n)
        high, low = split(raw_rows(start, n))
        b_high = bh[rows, :]
        return bf16_dot(b_high, high, TN) + (
            bf16_dot(b_high, low, TN) + bf16_dot(bl[rows, :], high, TN)
        )

    def first_set():
        gram[0] = own_gram(0, 640)
        w_first[...] = w_of(c, 0, 640)

    together(stages[0:2], stages[2:4], after=first_set)
    gram[0] += own_gram(640, wide_b)
    gram[1] = own_gram(WIDE, NARROW)

    places = (x * 4 + y, y * 4 + x)
    for t in range(8):
        h, m, r = t // 4, (t // 2) % 2, t % 2
        rows = pl.ds(pl.multiple_of(places[h] * 16 + r * 8, 8), 8)
        slices[t] = gram[m, rows, h * 128 : h * 128 + 128]
    gram_sends = [
        links.start(slices.at[(z + d) % 8], zland.at[d - 1], zs[d - 1]) for d in range(1, 8)
    ]

    def put_w(i, kind, w):
        row = i * 64 + kind * 32
        for k in range(8):
            wpart[k, row : row + 32, :] = w[k * 32 : k * 32 + 32, :]

    def z_chain(i):
        return z_reduce_gather(links, wpart, wfull, wland, 64 * i, 64, z, zs[0], zs[6])

    put_w(0, 0, w_first[...] + w_of(c, 640, wide_b))
    put_w(0, 1, w_of(c, WIDE, NARROW))
    chains = [z_chain(0)]
    next(chains[0])

    def z_step():
        for chain in chains:
            next(chain, None)

    for copy in gram_sends:
        copy.wait_recv()
    total = slices[z]
    for d in range(7):
        total = total + zland[d]
    place = places[0] + (z // 4) * (places[1] - places[0])
    own = gathered.at[z // 4, pl.ds(pl.multiple_of(place * 32 + (z % 4) * 8, 8), 8)]
    own[...] = total
    gram_sends = [links.start(own, own, zs[d]) for d in range(7)]
    for copy in shares:
        copy.wait_recv()
    put_w(1, 0, w_of(1 - c, 0, WIDE))
    put_w(1, 1, w_of(1 - c, WIDE, NARROW))
    z_step()
    chains.append(z_chain(1))
    next(chains[1])
    for copy in gram_sends:
        copy.wait_recv()
    def gather_gram(h, first, second):
        yield from direct_gather(links, gathered, h, first["q"] * 128, 32, **second)
        yield from direct_gather(links, gathered, h, 0, 128, **first)

    stages = [gather_gram(0, x_ring, y_ring), gather_gram(1, y_ring, x_ring)]
    for i in range(3):
        for stage in stages:
            next(stage, None)
        if i < 2:
            links.finish(48)
        z_step()
    for h in range(2):
        for p in range(16):
            for m in range(2):
                gram[m, p * 16 : p * 16 + 16, h * 128 : h * 128 + 128] = gathered[
                    h, p * 32 + m * 16 : p * 32 + m * 16 + 16, :
                ]

    exchanges = []

    def after_block(k):
        if k % 2:
            done = inverse.at[c, :, pl.ds(32 * (k - 1), 64)]
            exchanges.append(links.start(done, done, sibling))
            z_step()

    invert_factor(gram, inverse.at[c], after_block)
    def times_inverse(a, cc, kind):
        i_high, i_low = split(inverse[cc, kind])
        high, low = split(a)
        return bf16_dot(high, i_high, NT) + (
            bf16_dot(high, i_low, NT) + bf16_dot(low, i_high, NT)
        )

    def factor_of(i, cc, kind):
        row = i * 64 + kind * 32
        w = jnp.concatenate([wfull[k, row : row + 32, :] for k in range(8)], axis=0)
        factor = times_inverse(w, cc, kind)
        fac[2 * kind + cc] = factor
        squares = jnp.sum(factor * factor, axis=0, keepdims=True)
        return [squares[:, 0:128], squares[:, 128:256]]

    def ortho_half(cc):
        start = cc * HALF
        ow[cc] = times_inverse(raw_rows(start, WIDE), cc, 0)
        on[cc] = times_inverse(raw_rows(start + WIDE, NARROW), cc, 1)

    for _ in chains[0]:
        pass
    for kind in range(2):
        for h, squares in enumerate(factor_of(0, c, kind)):
            row = pl.ds(pl.multiple_of((2 * kind + c) * 2, 2) + h, 1)
            sq[row, :] = squares
    for _ in chains[1]:
        pass
    for copy in exchanges:
        copy.wait_recv()
    for kind in range(2):
        for h, squares in enumerate(factor_of(1, 1 - c, kind)):
            row = pl.ds(pl.multiple_of((2 * kind + 1 - c) * 2, 2) + h, 1)
            sq[row, :] = squares
    sq_land[0] = sq[...]
    sends = [links.start(sq_land.at[0], sq_land.at[d], device) for d, device in others]
    ortho_half(c)
    ortho_half(1 - c)
    total = sq_land[0]
    for (d, _), copy in zip(others, sends):
        copy.wait_recv()
        total = total + sq_land[d]
    sq[...] = total
    links.finish()


def last_kernel(
    bw, bn, ow, on, fac, sq, wmo, wbo, wup, nmo, nbo, nup, f_t, b_high, b_low
):
    kinds = ((bw, ow, wmo, wbo, wup, D), (bn, on, nmo, nbo, nup, KVW))

    which, step = pl.program_id(0), pl.program_id(1)

    @pl.when(step == 0)
    def _():
        for kind in range(2):
            factor = fac[kind, which]
            basis = factor * lax.rsqrt(sq[kind, which] + 1e-6)
            kinds[kind][3][0] = basis
            f_t[kind] = factor.astype(BF16).T
            b_high[kind], b_low[kind] = split(basis.T)

    for kind, (buffer, ortho, m_out, _, update, rows) in enumerate(kinds):
        n = m_out.shape[1]
        at = pl.ds(pl.multiple_of(step * n, n), n)
        o_high, o_low = split(ortho[which, at, :])
        m_out[0] = buffer[which, at, :] - 0.05 * bf16_dot(o_high, f_t[kind])
        product = bf16_dot(o_high, b_high[kind]) + (
            bf16_dot(o_high, b_low[kind]) + bf16_dot(o_low, b_high[kind])
        )
        update[0] = ((rows * D / RANK) ** 0.5 * product).astype(BF16)


def local(wide_momentum, wide_grad, wide_basis, narrow_momentum, narrow_grad, narrow_basis):
    vmem = pl.BlockSpec(memory_space=pltpu.VMEM)
    bw = wide_momentum + wide_grad.astype(F32)
    bn = narrow_momentum + narrow_grad.astype(F32)
    copies = 160
    ow, on, fac, sq = pl.pallas_call(
        main_kernel,
        out_shape=(
            jax.ShapeDtypeStruct((2, WIDE, RANK), F32),
            jax.ShapeDtypeStruct((2, NARROW, RANK), F32),
            jax.ShapeDtypeStruct((4, COLS, RANK), F32),
            jax.ShapeDtypeStruct((8, 128), F32),
        ),
        in_specs=[vmem] * 4,
        out_specs=[vmem] * 4,
        scratch_shapes=[
            pltpu.VMEM((2 * HALF, COLS), BF16),
            pltpu.VMEM((2 * HALF, COLS), BF16),
            pltpu.VMEM((2, 2, COLS, RANK), BF16),
            pltpu.VMEM((2, 2, COLS, RANK), BF16),
            pltpu.VMEM((2, 2 * HALF, 128), F32),
            pltpu.VMEM((2, 2 * HALF, 128), F32),
            pltpu.VMEM((2, HALF, 128), F32),
            pltpu.VMEM((2, 2, 2, 4, 160, 128), F32),
            pltpu.VMEM((2, RANK, RANK), F32),
            pltpu.VMEM((RANK, RANK), F32),
            pltpu.VMEM((COLS, RANK), F32),
            pltpu.VMEM((8, 8, 128), F32),
            pltpu.VMEM((7, 8, 128), F32),
            pltpu.VMEM((2, 512, 128), F32),
            pltpu.VMEM((8, 128, RANK), F32),
            pltpu.VMEM((8, 128, RANK), F32),
            pltpu.VMEM((2, 4, 128, RANK), F32),
            pltpu.VMEM((2, 2, RANK, RANK), F32),
            pltpu.VMEM((32, 8, 128), F32),
            pltpu.SemaphoreType.DMA((copies,)),
            pltpu.SemaphoreType.DMA((copies,)),
        ],
        compiler_params=pltpu.CompilerParams(
            collective_id=0, has_side_effects=True, vmem_limit_bytes=36 * 2**20
        ),
    )(bw, bn, wide_basis, narrow_basis)

    def rows(n):
        return pl.BlockSpec((1, n, COLS), lambda m, i: (m, i, 0))

    basis_out = pl.BlockSpec((1, COLS, RANK), lambda m, i: (m, 0, 0))
    steps = 2
    w, n = WIDE // steps, NARROW // steps
    return pl.pallas_call(
        last_kernel,
        grid=(2, steps),
        out_shape=(
            jax.ShapeDtypeStruct((2, WIDE, COLS), F32),
            jax.ShapeDtypeStruct((2, COLS, RANK), F32),
            jax.ShapeDtypeStruct((2, WIDE, COLS), BF16),
            jax.ShapeDtypeStruct((2, NARROW, COLS), F32),
            jax.ShapeDtypeStruct((2, COLS, RANK), F32),
            jax.ShapeDtypeStruct((2, NARROW, COLS), BF16),
        ),
        in_specs=[
            vmem,
        ] * 6,
        out_specs=[rows(w), basis_out, rows(w), rows(n), basis_out, rows(n)],
        scratch_shapes=[pltpu.VMEM((2, RANK, COLS), BF16)] * 3,
        compiler_params=pltpu.CompilerParams(vmem_limit_bytes=24 * 2**20),
    )(
        bw, bn, ow, on,
        fac.reshape(2, 2, COLS, RANK), sq.reshape(2, 2, 1, RANK),
    )


def solution(mesh):
    return jax.shard_map(
        local,
        mesh=mesh,
        in_specs=(
            P(None, "mp", "fsdp"),
            P(None, "mp", "fsdp"),
            P(None, "fsdp", None),
            P(None, "mp", "fsdp"),
            P(None, "mp", "fsdp"),
            P(None, "fsdp", None),
        ),
        out_specs=(
            P(None, "mp", "fsdp"),
            P(None, "fsdp", None),
            P(None, "mp", "fsdp"),
            P(None, "mp", "fsdp"),
            P(None, "fsdp", None),
            P(None, "mp", "fsdp"),
        ),
        check_vma=False,
    )
```

```python
import jax
import jax.numpy as jnp
from jax import lax
from jax.experimental import pallas as pl
from jax.experimental.pallas import tpu as pltpu
from jax.sharding import PartitionSpec as P

D = 8192
KVW = 1024
RANK = 256
WIDE = 1024
NARROW = 128
COLS = 256
HALF = WIDE + NARROW
F32 = jnp.float32
BF16 = jnp.bfloat16
MESH = pl.DeviceIdType.MESH
EXACT = lax.Precision.HIGHEST

NN = (((1,), (0,)), ((), ()))
NT = (((1,), (1,)), ((), ()))
TN = (((0,), (0,)), ((), ()))


def exact_dot(a, b, dims=NN):
    return lax.dot_general(a, b, dims, precision=EXACT, preferred_element_type=F32)


def split(a):
    high = a.astype(BF16)
    return high, (a - high.astype(F32)).astype(BF16)


def bf16_dot(a, b, dims=NN):
    return lax.dot_general(a, b, dims, preferred_element_type=F32)


class Links:
    def __init__(self, send, recv):
        self.send, self.recv = send, recv
        self.count = 0
        self.started = []

    def start(self, src, dst, device):
        i = self.count
        self.count += 1
        copy = pltpu.make_async_remote_copy(
            src_ref=src,
            dst_ref=dst,
            send_sem=self.send.at[i],
            recv_sem=self.recv.at[i],
            device_id=device,
            device_id_type=MESH,
        )
        copy.start()
        self.started.append(copy)
        return copy

    def finish(self, most=None):
        n = len(self.started) if most is None else most
        for copy in self.started[:n]:
            copy.wait_send()
        self.started = self.started[n:]


def ring_reduce(links, buf, out, h, base, chunk, cut, q, peers, land):
    after, before = (q + 1) % 4, (q + 3) % 4
    right, left = peers[0], peers[2]

    def rows(c, lo, n):
        return pl.ds(pl.multiple_of(base + c * chunk + lo, 8), n)

    far = (q + 2) % 4
    a = links.start(buf.at[h, rows(far, 0, cut)], land.at[0, pl.ds(0, cut)], right)
    b = links.start(
        buf.at[h, rows(far, cut, chunk - cut)], land.at[1, pl.ds(0, chunk - cut)], left
    )
    yield
    a.wait_recv()
    buf[h, rows(after, 0, cut), :] += land[0, 0:cut, :]
    a = links.start(buf.at[h, rows(after, 0, chunk)], land.at[2, pl.ds(0, chunk)], right)
    b.wait_recv()
    buf[h, rows(before, cut, chunk - cut), :] += land[1, 0 : chunk - cut, :]
    b = links.start(buf.at[h, rows(before, 0, chunk)], land.at[3, pl.ds(0, chunk)], left)
    yield
    a.wait_recv()
    b.wait_recv()
    out[h, rows(q, 0, chunk), :] = (
        buf[h, rows(q, 0, chunk), :] + land[2, 0:chunk, :] + land[3, 0:chunk, :]
    )


def ring_gather(links, buf, h, base, chunk, cut, q, peers):
    after, before = (q + 1) % 4, (q + 3) % 4
    right, left = peers[0], peers[2]

    def part(c, lo, n):
        return buf.at[h, pl.ds(pl.multiple_of(base + c * chunk + lo, 8), n)]

    own = part(q, 0, chunk)
    a = links.start(own, own, right)
    b = links.start(own, own, left)
    yield
    a.wait_recv()
    piece = part(before, 0, cut)
    a = links.start(piece, piece, right)
    b.wait_recv()
    piece = part(after, cut, chunk - cut)
    b = links.start(piece, piece, left)
    yield
    a.wait_recv()
    b.wait_recv()


def direct_reduce(links, buf, out, h, base, chunk, q, peers, land):
    def rows(c):
        return pl.ds(pl.multiple_of(base + c * chunk, 8), chunk)

    copies = [
        links.start(buf.at[h, rows((q + d) % 4)], land.at[d, pl.ds(0, chunk)], peers[d - 1])
        for d in (2, 1, 3)
    ]
    yield
    for copy in copies:
        copy.wait_recv()
    total = buf[h, rows(q), :]
    for d in (1, 2, 3):
        total = total + land[d, 0:chunk, :]
    out[h, rows(q), :] = total


def direct_gather(links, buf, h, base, chunk, q, peers):
    own = buf.at[h, pl.ds(pl.multiple_of(base + q * chunk, 8), chunk)]
    copies = [links.start(own, own, peers[d - 1]) for d in (2, 1, 3)]
    yield
    for copy in copies:
        copy.wait_recv()


def z_reduce_gather(links, buf, out, land, lo, n, q, right, left):
    half = n // 2

    def part(ref, i, start, size):
        return ref.at[i, pl.ds(lo + start, size)]

    def chunk(ref, i):
        return part(ref, i % 8, 0, n)

    def add(i, slot, start, size):
        rows = slice(lo + start, lo + start + size)
        buf[i % 8, rows, :] += land[slot[0], slot[1], rows, :]

    a = links.start(
        part(buf, (q + 4) % 8, 0, half), part(land.at[0], 0, 0, half), right
    )
    b = links.start(
        part(buf, (q + 4) % 8, half, half), part(land.at[1], 0, half, half), left
    )
    yield
    for s in (1, 2, 3):
        size = half if s == 1 else n
        a.wait_recv()
        add(q + 4 - s, (0, s - 1), 0, size)
        a = links.start(chunk(buf, q + 4 - s), part(land.at[0], s, 0, n), right)
        b.wait_recv()
        add(q + 4 + s, (1, s - 1), n - size, size)
        b = links.start(chunk(buf, q + 4 + s), part(land.at[1], s, 0, n), left)
        yield
    a.wait_recv()
    b.wait_recv()
    rows = slice(lo, lo + n)
    out[q, rows, :] = buf[q, rows, :] + land[0, 3, rows, :] + land[1, 3, rows, :]
    a = links.start(chunk(out, q), chunk(out, q), right)
    b = links.start(chunk(out, q), chunk(out, q), left)
    yield
    for s in (1, 2):
        a.wait_recv()
        a = links.start(chunk(out, q + 8 - s), chunk(out, q + 8 - s), right)
        b.wait_recv()
        b = links.start(chunk(out, q + s), chunk(out, q + s), left)
        yield
    a.wait_recv()
    piece = part(out, (q + 5) % 8, 0, half)
    a = links.start(piece, piece, right)
    b.wait_recv()
    piece = part(out, (q + 3) % 8, half, half)
    b = links.start(piece, piece, left)
    yield
    a.wait_recv()
    b.wait_recv()


def together(first, second, after):
    done = object()
    ended = False
    while first or second:
        first = [s for s in first if next(s, done) is not done]
        if not first and not ended:
            after()
            ended = True
        second = [s for s in second if next(s, done) is not done]


def block_inverse(e):
    lane = lax.broadcasted_iota(jnp.int32, (8, 128), 1)
    sub = lax.broadcasted_iota(jnp.int32, (8, 128), 0)
    group = (lane // 64) * 64

    def pick(tile, index):
        return jnp.take_along_axis(tile, group + index, axis=1)

    e = list(e)
    for g in range(4):
        cols = [[pick(e[i], 8 * g + t) for i in range(g, 4)] for t in range(8)]
        for t in range(8):
            pivot = cols[t][0][t : t + 1, :]
            inv = pl.reciprocal(pivot, approx=True)
            inv = inv * (2.0 - pivot * inv)
            for n, i in enumerate(range(g, 4)):
                f = cols[t][n] * inv
                if n == 0:
                    f = jnp.where(sub > t, f, 0.0)
                e[i] = e[i] - f * e[g][t : t + 1, :]
                for s in range(t + 1, 8):
                    cols[s][n] = cols[s][n] - f * cols[s][0][t : t + 1, :]
    return [tile * lax.rsqrt(pick(tile, 8 * i + sub)) for i, tile in enumerate(e)]


def invert_factor(a_ref, out, after):
    lane = lax.broadcasted_iota(jnp.int32, (32, 128), 1)
    row = lax.broadcasted_iota(jnp.int32, (32, 128), 0)
    eye = jnp.where(lane % 32 == row, 1.0, 0.0)
    col = lax.broadcasted_iota(jnp.int32, (32, 256), 1)
    wide_row = lax.broadcasted_iota(jnp.int32, (32, 256), 0)

    def turned(v, by):
        return pltpu.roll(v, by % 128, 1) if by % 128 else v

    blocks = [a_ref[m, 0:32, 0:128] for m in range(2)]
    panels = None
    for k in range(8):
        at, below = 32 * k, 32 * k + 32
        base, low = at // 128 * 128, below // 128 * 128
        if k > 0:
            for m in range(2):
                change = exact_dot(panels[m][:, base:256], panels[m], TN)
                under = lax.broadcasted_iota(jnp.int32, (256 - at, 256), 1)
                rest = jnp.where(
                    (under >= at - 32) & (under < at), 0.0, a_ref[m, at:256, :]
                )
                a_ref[m, at:256, :] = rest - change[at - base :, :]
        d0, d1 = turned(blocks[0], base - at), turned(blocks[1], 64 + base - at)
        e = jnp.where(lane < 32, d0, jnp.where((lane >= 64) & (lane < 96), d1, eye))
        e = jnp.concatenate(
            block_inverse([e[8 * i : 8 * i + 8] for i in range(4)]), axis=0
        )
        inside = (col >= at) & (col < below)
        wide_eye = jnp.where(col - at == wide_row, 1.0, 0.0)
        panels, blocks = [], []
        for m in range(2):
            t = turned(e, 96 - 64 * m)[:, 0:32]
            panel = exact_dot(t, jnp.where(inside, wide_eye, a_ref[m, at:below, :]))
            panels.append(panel)
            if below < 256:
                near = panel[:, low : low + 128]
                change = exact_dot(near, near, TN)
                blocks.append(
                    a_ref[m, below : below + 32, low : low + 128]
                    - change[below - low : below - low + 32, :]
                )
            a_ref[m, at:below, :] = panel
            out[m, at:below, :] = jnp.where(col <= at + wide_row, panel, 0.0)
        after(k)


def main_kernel(
    bw, bn, wb, nb,
    ow, on, fac, sq,
    bh, bl, vh, vl, part, full, swap, land, gram, cross, w_first, slices, zland, gathered,
    wpart, wfull, wland, inverse, sq_land,
    send, recv,
):
    z = lax.axis_index("mp")
    f = lax.axis_index("fsdp")
    c = f % 2
    x = (f // 2) % 4
    y = f // 8

    def plane(xx, yy, cc):
        return {"fsdp": ((yy % 4) * 4 + xx % 4) * 2 + cc}

    sibling = plane(x, y, 1 - c)
    xs = [plane(x + d, y, c) for d in (1, 2, 3)]
    others = [(d, {"fsdp": (f + d) % 32}) for d in range(1, 32)]
    ys = [plane(x, y + d, c) for d in (1, 2, 3)]
    zs = [{"mp": (z + d) % 8} for d in range(1, 8)]

    barrier = pltpu.get_barrier_semaphore()
    partners = [device for _, device in others] + zs
    for device in partners:
        pl.semaphore_signal(barrier, inc=1, device_id=device, device_id_type=MESH)

    links = Links(send, recv)
    sets = ((0, 640), (640, 512))
    wide_b = WIDE - 640

    def split_basis(cc):
        for kind, basis in enumerate((wb, nb)):
            high, low = split(basis[cc])
            vh[cc, kind] = high
            vl[cc, kind] = low

    def raw_rows_of(cc, kind, r, n, buffer):
        rows = pl.ds(pl.multiple_of(cc * HALF + r, 16), n)
        high, low = split(buffer)
        bh[rows, :] = high
        bl[rows, :] = low
        v_high = vh[cc, kind]
        raw = bf16_dot(high, v_high) + (bf16_dot(high, vl[cc, kind]) + bf16_dot(low, v_high))
        part[0, rows, :] = raw[:, 0:128]
        part[1, rows, :] = raw[:, 128:256]

    def raw_set(cc, i):
        lo, n = ((0, 640), (640, wide_b))[i]
        raw_rows_of(cc, 0, lo, n, bw[cc, lo : lo + n, :])

        if i == 1:
            raw_rows_of(cc, 1, WIDE, NARROW, bn[cc])

    def half_rows(cc, start, n):
        return pl.ds(pl.multiple_of(cc * HALF + start, 8), n)

    split_basis(1 - c)
    raw_set(1 - c, 0)
    pl.semaphore_wait(barrier, len(partners))
    exchanges = []
    for i, (start, n) in enumerate(sets):
        if i == 1:
            raw_set(1 - c, 1)
        exchanges.append(
            links.start(
                part.at[:, half_rows(1 - c, start, n)], swap.at[:, pl.ds(start, n)], sibling
            )
        )
    split_basis(c)

    x_ring = dict(q=x, peers=xs)
    y_ring = dict(q=y, peers=ys)
    base = c * HALF

    def gather_both(buffer, h, start, sizes, first, second):
        yield from direct_gather(
            links, buffer, h, start + first["q"] * sizes[0], sizes[1], **second
        )
        yield from ring_gather(links, buffer, h, start, sizes[0], sizes[0] // 2, **first)

    shares = []

    def whole_sum(i, h):
        start, n = sets[i]
        big, small = n // 4, n // 16
        first, second = (x_ring, y_ring) if h == 0 else (y_ring, x_ring)
        yield from ring_reduce(
            links, part, part, h, base + start, big, big // 2, land=land.at[i, h, 0], **first
        )
        yield from direct_reduce(
            links, part, full, h, base + start + first["q"] * big, small,
            land=land.at[i, h, 1], **second
        )
        yield from gather_both(full, h, base + start, (big, small), first, second)
        done = full.at[h, half_rows(c, start, n)]
        shares.append(links.start(done, done, sibling))

    stages = []
    for i, (start, n) in enumerate(sets):
        raw_set(c, i)
        exchanges[i].wait_recv()
        rows = half_rows(c, start, n)
        part[:, rows, :] += swap[:, start : start + n, :]
        for h in range(2):
            stage = whole_sum(i, h)
            next(stage)
            stages.append(stage)

    def raw_rows(start, n):
        rows = pl.ds(pl.multiple_of(start, 8), n)
        return jnp.concatenate([full[0, rows, :], full[1, rows, :]], axis=1)

    def own_gram(start, n):
        raw = raw_rows(base + start, n)
        high = raw.astype(BF16)
        middle, low = split(raw - high.astype(F32))
        cross[...] = bf16_dot(high, middle, TN) + bf16_dot(high, low, TN)
        mirrored = cross[...] + cross[...].T
        return bf16_dot(high, high, TN) + (mirrored + bf16_dot(middle, middle, TN))

    def w_of(cc, start, n):
        start = cc * HALF + start
        rows = pl.ds(pl.multiple_of(start, 16), n)
        high, low = split(raw_rows(start, n))
        b_high = bh[rows, :]
        return bf16_dot(b_high, high, TN) + (
            bf16_dot(b_high, low, TN) + bf16_dot(bl[rows, :], high, TN)
        )

    def first_set():
        gram[0] = own_gram(0, 640)
        w_first[...] = w_of(c, 0, 640)

    together(stages[0:2], stages[2:4], after=first_set)
    def put_w(i, kind, w):
        row = i * 64 + kind * 32
        for k in range(8):
            wpart[k, row : row + 32, :] = w[k * 32 : k * 32 + 32, :]

    def z_chain(i):
        return z_reduce_gather(links, wpart, wfull, wland, 64 * i, 64, z, zs[0], zs[6])

    put_w(0, 0, w_first[...] + w_of(c, 640, wide_b))
    put_w(0, 1, w_of(c, WIDE, NARROW))
    chains = [z_chain(0)]
    next(chains[0])

    gram[0] += own_gram(640, wide_b)
    gram[1] = own_gram(WIDE, NARROW)

    places = (x * 4 + y, y * 4 + x)
    for t in range(8):
        h, m, r = t // 4, (t // 2) % 2, t % 2
        rows = pl.ds(pl.multiple_of(places[h] * 16 + r * 8, 8), 8)
        slices[t] = gram[m, rows, h * 128 : h * 128 + 128]
    gram_sends = [
        links.start(slices.at[(z + d) % 8], zland.at[d - 1], zs[d - 1]) for d in range(1, 8)
    ]

    for copy in shares:
        copy.wait_recv()
    put_w(1, 0, w_of(1 - c, 0, WIDE))
    put_w(1, 1, w_of(1 - c, WIDE, NARROW))
    chains.append(z_chain(1))
    next(chains[1])

    def z_step():
        for chain in chains:
            next(chain, None)

    for copy in gram_sends:
        copy.wait_recv()
    total = slices[z]
    for d in range(7):
        total = total + zland[d]
    place = places[0] + (z // 4) * (places[1] - places[0])
    own = gathered.at[z // 4, pl.ds(pl.multiple_of(place * 32 + (z % 4) * 8, 8), 8)]
    own[...] = total
    gram_sends = [links.start(own, own, zs[d]) for d in range(7)]
    z_step()
    for copy in gram_sends:
        copy.wait_recv()
    def gather_gram(h, first, second):
        yield from direct_gather(links, gathered, h, first["q"] * 128, 32, **second)
        yield from direct_gather(links, gathered, h, 0, 128, **first)

    stages = [gather_gram(0, x_ring, y_ring), gather_gram(1, y_ring, x_ring)]
    for i in range(3):
        for stage in stages:
            next(stage, None)
        if i < 2:
            links.finish(48)
        z_step()
    for h in range(2):
        for p in range(16):
            for m in range(2):
                gram[m, p * 16 : p * 16 + 16, h * 128 : h * 128 + 128] = gathered[
                    h, p * 32 + m * 16 : p * 32 + m * 16 + 16, :
                ]

    exchanges = []

    def after_block(k):
        if k % 2:
            done = inverse.at[c, :, pl.ds(32 * (k - 1), 64)]
            exchanges.append(links.start(done, done, sibling))
            z_step()

    invert_factor(gram, inverse.at[c], after_block)
    def times_inverse(a, cc, kind):
        i_high, i_low = split(inverse[cc, kind])
        high, low = split(a)
        return bf16_dot(high, i_high, NT) + (
            bf16_dot(high, i_low, NT) + bf16_dot(low, i_high, NT)
        )

    def factor_of(i, cc, kind):
        row = i * 64 + kind * 32
        w = jnp.concatenate([wfull[k, row : row + 32, :] for k in range(8)], axis=0)
        factor = times_inverse(w, cc, kind)
        fac[2 * kind + cc] = factor
        squares = jnp.sum(factor * factor, axis=0, keepdims=True)
        return [squares[:, 0:128], squares[:, 128:256]]

    def ortho_half(cc):
        start = cc * HALF
        ow[cc] = times_inverse(raw_rows(start, WIDE), cc, 0)
        on[cc] = times_inverse(raw_rows(start + WIDE, NARROW), cc, 1)

    for _ in chains[0]:
        pass
    for kind in range(2):
        for h, squares in enumerate(factor_of(0, c, kind)):
            row = pl.ds(pl.multiple_of((2 * kind + c) * 2, 2) + h, 1)
            sq[row, :] = squares
    for _ in chains[1]:
        pass
    for copy in exchanges:
        copy.wait_recv()
    for kind in range(2):
        for h, squares in enumerate(factor_of(1, 1 - c, kind)):
            row = pl.ds(pl.multiple_of((2 * kind + 1 - c) * 2, 2) + h, 1)
            sq[row, :] = squares
    sq_land[0] = sq[...]
    sends = [links.start(sq_land.at[0], sq_land.at[d], device) for d, device in others]
    ortho_half(c)
    ortho_half(1 - c)
    total = sq_land[0]
    for (d, _), copy in zip(others, sends):
        copy.wait_recv()
        total = total + sq_land[d]
    sq[...] = total
    links.finish()


def last_kernel(
    bw, bn, ow, on, fac, sq, wmo, wbo, wup, nmo, nbo, nup, f_t, b_high, b_low
):
    kinds = ((bw, ow, wmo, wbo, wup, D), (bn, on, nmo, nbo, nup, KVW))

    which, step = pl.program_id(0), pl.program_id(1)

    @pl.when(step == 0)
    def _():
        for kind in range(2):
            factor = fac[kind, which]
            basis = factor * lax.rsqrt(sq[kind, which] + 1e-6)
            kinds[kind][3][0] = basis
            f_t[kind] = factor.astype(BF16).T
            b_high[kind], b_low[kind] = split(basis.T)

    for kind, (buffer, ortho, m_out, _, update, rows) in enumerate(kinds):
        n = m_out.shape[1]
        at = pl.ds(pl.multiple_of(step * n, n), n)
        o_high, o_low = split(ortho[which, at, :])
        m_out[0] = buffer[which, at, :] - 0.05 * bf16_dot(o_high, f_t[kind])
        product = bf16_dot(o_high, b_high[kind]) + (
            bf16_dot(o_high, b_low[kind]) + bf16_dot(o_low, b_high[kind])
        )
        update[0] = ((rows * D / RANK) ** 0.5 * product).astype(BF16)


def local(wide_momentum, wide_grad, wide_basis, narrow_momentum, narrow_grad, narrow_basis):
    vmem = pl.BlockSpec(memory_space=pltpu.VMEM)
    bw = wide_momentum + wide_grad.astype(F32)
    bn = narrow_momentum + narrow_grad.astype(F32)
    copies = 160
    ow, on, fac, sq = pl.pallas_call(
        main_kernel,
        out_shape=(
            jax.ShapeDtypeStruct((2, WIDE, RANK), F32),
            jax.ShapeDtypeStruct((2, NARROW, RANK), F32),
            jax.ShapeDtypeStruct((4, COLS, RANK), F32),
            jax.ShapeDtypeStruct((8, 128), F32),
        ),
        in_specs=[vmem] * 4,
        out_specs=[vmem] * 4,
        scratch_shapes=[
            pltpu.VMEM((2 * HALF, COLS), BF16),
            pltpu.VMEM((2 * HALF, COLS), BF16),
            pltpu.VMEM((2, 2, COLS, RANK), BF16),
            pltpu.VMEM((2, 2, COLS, RANK), BF16),
            pltpu.VMEM((2, 2 * HALF, 128), F32),
            pltpu.VMEM((2, 2 * HALF, 128), F32),
            pltpu.VMEM((2, HALF, 128), F32),
            pltpu.VMEM((2, 2, 2, 4, 160, 128), F32),
            pltpu.VMEM((2, RANK, RANK), F32),
            pltpu.VMEM((RANK, RANK), F32),
            pltpu.VMEM((COLS, RANK), F32),
            pltpu.VMEM((8, 8, 128), F32),
            pltpu.VMEM((7, 8, 128), F32),
            pltpu.VMEM((2, 512, 128), F32),
            pltpu.VMEM((8, 128, RANK), F32),
            pltpu.VMEM((8, 128, RANK), F32),
            pltpu.VMEM((2, 4, 128, RANK), F32),
            pltpu.VMEM((2, 2, RANK, RANK), F32),
            pltpu.VMEM((32, 8, 128), F32),
            pltpu.SemaphoreType.DMA((copies,)),
            pltpu.SemaphoreType.DMA((copies,)),
        ],
        compiler_params=pltpu.CompilerParams(
            collective_id=0, has_side_effects=True, vmem_limit_bytes=36 * 2**20
        ),
    )(bw, bn, wide_basis, narrow_basis)

    def rows(n):
        return pl.BlockSpec((1, n, COLS), lambda m, i: (m, i, 0))

    basis_out = pl.BlockSpec((1, COLS, RANK), lambda m, i: (m, 0, 0))
    steps = 2
    w, n = WIDE // steps, NARROW // steps
    return pl.pallas_call(
        last_kernel,
        grid=(2, steps),
        out_shape=(
            jax.ShapeDtypeStruct((2, WIDE, COLS), F32),
            jax.ShapeDtypeStruct((2, COLS, RANK), F32),
            jax.ShapeDtypeStruct((2, WIDE, COLS), BF16),
            jax.ShapeDtypeStruct((2, NARROW, COLS), F32),
            jax.ShapeDtypeStruct((2, COLS, RANK), F32),
            jax.ShapeDtypeStruct((2, NARROW, COLS), BF16),
        ),
        in_specs=[
            vmem,
        ] * 6,
        out_specs=[rows(w), basis_out, rows(w), rows(n), basis_out, rows(n)],
        scratch_shapes=[pltpu.VMEM((2, RANK, COLS), BF16)] * 3,
        compiler_params=pltpu.CompilerParams(vmem_limit_bytes=24 * 2**20),
    )(
        bw, bn, ow, on,
        fac.reshape(2, 2, COLS, RANK), sq.reshape(2, 2, 1, RANK),
    )


def solution(mesh):
    return jax.shard_map(
        local,
        mesh=mesh,
        in_specs=(
            P(None, "mp", "fsdp"),
            P(None, "mp", "fsdp"),
            P(None, "fsdp", None),
            P(None, "mp", "fsdp"),
            P(None, "mp", "fsdp"),
            P(None, "fsdp", None),
        ),
        out_specs=(
            P(None, "mp", "fsdp"),
            P(None, "fsdp", None),
            P(None, "mp", "fsdp"),
            P(None, "mp", "fsdp"),
            P(None, "fsdp", None),
            P(None, "mp", "fsdp"),
        ),
        check_vma=False,
    )
```

```python
import jax
import jax.numpy as jnp
from jax import lax
from jax.experimental import pallas as pl
from jax.experimental.pallas import tpu as pltpu
from jax.sharding import PartitionSpec as P

D = 8192
KVW = 1024
RANK = 256
WIDE = 1024
NARROW = 128
COLS = 256
HALF = WIDE + NARROW
F32 = jnp.float32
BF16 = jnp.bfloat16
MESH = pl.DeviceIdType.MESH
EXACT = lax.Precision.HIGHEST

NN = (((1,), (0,)), ((), ()))
NT = (((1,), (1,)), ((), ()))
TN = (((0,), (0,)), ((), ()))


def exact_dot(a, b, dims=NN):
    return lax.dot_general(a, b, dims, precision=EXACT, preferred_element_type=F32)


def split(a):
    high = a.astype(BF16)
    return high, (a - high.astype(F32)).astype(BF16)


def bf16_dot(a, b, dims=NN):
    return lax.dot_general(a, b, dims, preferred_element_type=F32)


class Links:
    def __init__(self, send, recv):
        self.send, self.recv = send, recv
        self.count = 0
        self.started = []

    def start(self, src, dst, device):
        i = self.count
        self.count += 1
        copy = pltpu.make_async_remote_copy(
            src_ref=src,
            dst_ref=dst,
            send_sem=self.send.at[i],
            recv_sem=self.recv.at[i],
            device_id=device,
            device_id_type=MESH,
        )
        copy.start()
        self.started.append(copy)
        return copy

    def finish(self, most=None):
        n = len(self.started) if most is None else most
        for copy in self.started[:n]:
            copy.wait_send()
        self.started = self.started[n:]


def ring_reduce(links, buf, out, h, base, chunk, cut, q, peers, land):
    after, before = (q + 1) % 4, (q + 3) % 4
    right, left = peers[0], peers[2]

    def rows(c, lo, n):
        return pl.ds(pl.multiple_of(base + c * chunk + lo, 8), n)

    far = (q + 2) % 4
    a = links.start(buf.at[h, rows(far, 0, cut)], land.at[0, pl.ds(0, cut)], right)
    b = links.start(
        buf.at[h, rows(far, cut, chunk - cut)], land.at[1, pl.ds(0, chunk - cut)], left
    )
    yield
    a.wait_recv()
    buf[h, rows(after, 0, cut), :] += land[0, 0:cut, :]
    a = links.start(buf.at[h, rows(after, 0, chunk)], land.at[2, pl.ds(0, chunk)], right)
    b.wait_recv()
    buf[h, rows(before, cut, chunk - cut), :] += land[1, 0 : chunk - cut, :]
    b = links.start(buf.at[h, rows(before, 0, chunk)], land.at[3, pl.ds(0, chunk)], left)
    yield
    a.wait_recv()
    b.wait_recv()
    out[h, rows(q, 0, chunk), :] = (
        buf[h, rows(q, 0, chunk), :] + land[2, 0:chunk, :] + land[3, 0:chunk, :]
    )


def ring_gather(links, buf, h, base, chunk, cut, q, peers):
    after, before = (q + 1) % 4, (q + 3) % 4
    right, left = peers[0], peers[2]

    def part(c, lo, n):
        return buf.at[h, pl.ds(pl.multiple_of(base + c * chunk + lo, 8), n)]

    own = part(q, 0, chunk)
    a = links.start(own, own, right)
    b = links.start(own, own, left)
    yield
    a.wait_recv()
    piece = part(before, 0, cut)
    a = links.start(piece, piece, right)
    b.wait_recv()
    piece = part(after, cut, chunk - cut)
    b = links.start(piece, piece, left)
    yield
    a.wait_recv()
    b.wait_recv()


def direct_reduce(links, buf, out, h, base, chunk, q, peers, land):
    def rows(c):
        return pl.ds(pl.multiple_of(base + c * chunk, 8), chunk)

    copies = [
        links.start(buf.at[h, rows((q + d) % 4)], land.at[d, pl.ds(0, chunk)], peers[d - 1])
        for d in (2, 1, 3)
    ]
    yield
    for copy in copies:
        copy.wait_recv()
    total = buf[h, rows(q), :]
    for d in (1, 2, 3):
        total = total + land[d, 0:chunk, :]
    out[h, rows(q), :] = total


def direct_gather(links, buf, h, base, chunk, q, peers):
    own = buf.at[h, pl.ds(pl.multiple_of(base + q * chunk, 8), chunk)]
    copies = [links.start(own, own, peers[d - 1]) for d in (2, 1, 3)]
    yield
    for copy in copies:
        copy.wait_recv()


def z_reduce_gather(links, buf, out, land, lo, n, q, right, left):
    half = n // 2

    def part(ref, i, start, size):
        return ref.at[i, pl.ds(lo + start, size)]

    def chunk(ref, i):
        return part(ref, i % 8, 0, n)

    def add(i, slot, start, size):
        rows = slice(lo + start, lo + start + size)
        buf[i % 8, rows, :] += land[slot[0], slot[1], rows, :]

    a = links.start(
        part(buf, (q + 4) % 8, 0, half), part(land.at[0], 0, 0, half), right
    )
    b = links.start(
        part(buf, (q + 4) % 8, half, half), part(land.at[1], 0, half, half), left
    )
    yield
    for s in (1, 2, 3):
        size = half if s == 1 else n
        a.wait_recv()
        add(q + 4 - s, (0, s - 1), 0, size)
        a = links.start(chunk(buf, q + 4 - s), part(land.at[0], s, 0, n), right)
        b.wait_recv()
        add(q + 4 + s, (1, s - 1), n - size, size)
        b = links.start(chunk(buf, q + 4 + s), part(land.at[1], s, 0, n), left)
        yield
    a.wait_recv()
    b.wait_recv()
    rows = slice(lo, lo + n)
    out[q, rows, :] = buf[q, rows, :] + land[0, 3, rows, :] + land[1, 3, rows, :]
    a = links.start(chunk(out, q), chunk(out, q), right)
    b = links.start(chunk(out, q), chunk(out, q), left)
    yield
    for s in (1, 2):
        a.wait_recv()
        a = links.start(chunk(out, q + 8 - s), chunk(out, q + 8 - s), right)
        b.wait_recv()
        b = links.start(chunk(out, q + s), chunk(out, q + s), left)
        yield
    a.wait_recv()
    piece = part(out, (q + 5) % 8, 0, half)
    a = links.start(piece, piece, right)
    b.wait_recv()
    piece = part(out, (q + 3) % 8, half, half)
    b = links.start(piece, piece, left)
    yield
    a.wait_recv()
    b.wait_recv()


def together(first, second, after):
    done = object()
    ended = False
    while first or second:
        first = [s for s in first if next(s, done) is not done]
        if not first and not ended:
            after()
            ended = True
        second = [s for s in second if next(s, done) is not done]


def block_inverse(e):
    lane = lax.broadcasted_iota(jnp.int32, (8, 128), 1)
    sub = lax.broadcasted_iota(jnp.int32, (8, 128), 0)
    group = (lane // 64) * 64

    def pick(tile, index):
        return jnp.take_along_axis(tile, group + index, axis=1)

    e = list(e)
    for g in range(4):
        cols = [[pick(e[i], 8 * g + t) for i in range(g, 4)] for t in range(8)]
        for t in range(8):
            pivot = cols[t][0][t : t + 1, :]
            inv = pl.reciprocal(pivot, approx=True)
            inv = inv * (2.0 - pivot * inv)
            for n, i in enumerate(range(g, 4)):
                f = cols[t][n] * inv
                if n == 0:
                    f = jnp.where(sub > t, f, 0.0)
                e[i] = e[i] - f * e[g][t : t + 1, :]
                for s in range(t + 1, 8):
                    cols[s][n] = cols[s][n] - f * cols[s][0][t : t + 1, :]
    return [tile * lax.rsqrt(pick(tile, 8 * i + sub)) for i, tile in enumerate(e)]


def invert_factor(a_ref, out, after):
    lane = lax.broadcasted_iota(jnp.int32, (32, 128), 1)
    row = lax.broadcasted_iota(jnp.int32, (32, 128), 0)
    eye = jnp.where(lane % 32 == row, 1.0, 0.0)
    col = lax.broadcasted_iota(jnp.int32, (32, 256), 1)
    wide_row = lax.broadcasted_iota(jnp.int32, (32, 256), 0)

    def turned(v, by):
        return pltpu.roll(v, by % 128, 1) if by % 128 else v

    blocks = [a_ref[m, 0:32, 0:128] for m in range(2)]
    panels = None
    for k in range(8):
        at, below = 32 * k, 32 * k + 32
        base, low = at // 128 * 128, below // 128 * 128
        if k > 0:
            for m in range(2):
                change = exact_dot(panels[m][:, base:256], panels[m], TN)
                under = lax.broadcasted_iota(jnp.int32, (256 - at, 256), 1)
                rest = jnp.where(
                    (under >= at - 32) & (under < at), 0.0, a_ref[m, at:256, :]
                )
                a_ref[m, at:256, :] = rest - change[at - base :, :]
        d0, d1 = turned(blocks[0], base - at), turned(blocks[1], 64 + base - at)
        e = jnp.where(lane < 32, d0, jnp.where((lane >= 64) & (lane < 96), d1, eye))
        e = jnp.concatenate(
            block_inverse([e[8 * i : 8 * i + 8] for i in range(4)]), axis=0
        )
        inside = (col >= at) & (col < below)
        wide_eye = jnp.where(col - at == wide_row, 1.0, 0.0)
        panels, blocks = [], []
        for m in range(2):
            t = turned(e, 96 - 64 * m)[:, 0:32]
            panel = exact_dot(t, jnp.where(inside, wide_eye, a_ref[m, at:below, :]))
            panels.append(panel)
            if below < 256:
                near = panel[:, low : low + 128]
                change = exact_dot(near, near, TN)
                blocks.append(
                    a_ref[m, below : below + 32, low : low + 128]
                    - change[below - low : below - low + 32, :]
                )
            a_ref[m, at:below, :] = panel
            out[m, at:below, :] = jnp.where(col <= at + wide_row, panel, 0.0)
        after(k)


def main_kernel(
    bw, bn, wb, nb,
    ow, on, fac, sq,
    bh, bl, vh, vl, part, full, swap, land, gram, cross, w_first, slices, zland, gathered,
    wpart, wfull, wland, inverse, sq_land,
    send, recv,
):
    z = lax.axis_index("mp")
    f = lax.axis_index("fsdp")
    c = f % 2
    x = (f // 2) % 4
    y = f // 8

    def plane(xx, yy, cc):
        return {"fsdp": ((yy % 4) * 4 + xx % 4) * 2 + cc}

    sibling = plane(x, y, 1 - c)
    xs = [plane(x + d, y, c) for d in (1, 2, 3)]
    others = [(d, {"fsdp": (f + d) % 32}) for d in range(1, 32)]
    ys = [plane(x, y + d, c) for d in (1, 2, 3)]
    zs = [{"mp": (z + d) % 8} for d in range(1, 8)]

    barrier = pltpu.get_barrier_semaphore()
    partners = [device for _, device in others] + zs
    for device in partners:
        pl.semaphore_signal(barrier, inc=1, device_id=device, device_id_type=MESH)

    links = Links(send, recv)
    sets = ((0, 640), (640, 512))
    wide_b = WIDE - 640

    def split_basis(cc):
        for kind, basis in enumerate((wb, nb)):
            high, low = split(basis[cc])
            vh[cc, kind] = high
            vl[cc, kind] = low

    def raw_rows_of(cc, kind, r, n, buffer):
        rows = pl.ds(pl.multiple_of(cc * HALF + r, 16), n)
        high, low = split(buffer)
        bh[rows, :] = high
        bl[rows, :] = low
        v_high = vh[cc, kind]
        raw = bf16_dot(high, v_high) + (bf16_dot(high, vl[cc, kind]) + bf16_dot(low, v_high))
        part[0, rows, :] = raw[:, 0:128]
        part[1, rows, :] = raw[:, 128:256]

    def raw_set(cc, i):
        lo, n = ((0, 640), (640, wide_b))[i]
        raw_rows_of(cc, 0, lo, n, bw[cc, lo : lo + n, :])

        if i == 1:
            raw_rows_of(cc, 1, WIDE, NARROW, bn[cc])

    def half_rows(cc, start, n):
        return pl.ds(pl.multiple_of(cc * HALF + start, 8), n)

    split_basis(1 - c)
    raw_set(1 - c, 0)
    pl.semaphore_wait(barrier, len(partners))
    exchanges = []
    for i, (start, n) in enumerate(sets):
        if i == 1:
            raw_set(1 - c, 1)
        exchanges.append(
            links.start(
                part.at[:, half_rows(1 - c, start, n)], swap.at[:, pl.ds(start, n)], sibling
            )
        )
    split_basis(c)

    x_ring = dict(q=x, peers=xs)
    y_ring = dict(q=y, peers=ys)
    base = c * HALF

    def gather_both(buffer, h, start, sizes, first, second):
        yield from direct_gather(
            links, buffer, h, start + first["q"] * sizes[0], sizes[1], **second
        )
        yield from ring_gather(links, buffer, h, start, sizes[0], sizes[0] // 2, **first)

    shares = []

    def whole_sum(i, h):
        start, n = sets[i]
        big, small = n // 4, n // 16
        first, second = (x_ring, y_ring) if h == 0 else (y_ring, x_ring)
        yield from ring_reduce(
            links, part, part, h, base + start, big, big // 2, land=land.at[i, h, 0], **first
        )
        yield from direct_reduce(
            links, part, full, h, base + start + first["q"] * big, small,
            land=land.at[i, h, 1], **second
        )
        yield from gather_both(full, h, base + start, (big, small), first, second)
        done = full.at[h, half_rows(c, start, n)]
        shares.append(links.start(done, done, sibling))

    stages = []
    for i, (start, n) in enumerate(sets):
        raw_set(c, i)
        exchanges[i].wait_recv()
        rows = half_rows(c, start, n)
        part[:, rows, :] += swap[:, start : start + n, :]
        for h in range(2):
            stage = whole_sum(i, h)
            next(stage)
            stages.append(stage)

    def raw_rows(start, n):
        rows = pl.ds(pl.multiple_of(start, 8), n)
        return jnp.concatenate([full[0, rows, :], full[1, rows, :]], axis=1)

    def own_gram(start, n):
        raw = raw_rows(base + start, n)
        high = raw.astype(BF16)
        middle, low = split(raw - high.astype(F32))
        cross[...] = bf16_dot(high, middle, TN) + bf16_dot(high, low, TN)
        mirrored = cross[...] + cross[...].T
        return bf16_dot(high, high, TN) + (mirrored + bf16_dot(middle, middle, TN))

    def w_of(cc, start, n):
        start = cc * HALF + start
        rows = pl.ds(pl.multiple_of(start, 16), n)
        high, low = split(raw_rows(start, n))
        b_high = bh[rows, :]
        return bf16_dot(b_high, high, TN) + (
            bf16_dot(b_high, low, TN) + bf16_dot(bl[rows, :], high, TN)
        )

    def first_set():
        gram[0] = own_gram(0, 640)
        w_first[...] = w_of(c, 0, 640)

    together(stages[0:2], stages[2:4], after=first_set)
    def put_w(i, kind, w):
        row = i * 64 + kind * 32
        for k in range(8):
            wpart[k, row : row + 32, :] = w[k * 32 : k * 32 + 32, :]

    chains = []

    def z_chain(i, kind, w):
        put_w(i, kind, w)
        row = i * 64 + kind * 32
        chain = z_reduce_gather(links, wpart, wfull, wland, row, 32, z, zs[0], zs[6])
        next(chain)
        chains.append(chain)

    z_chain(0, 0, w_first[...] + w_of(c, 640, wide_b))
    z_chain(0, 1, w_of(c, WIDE, NARROW))

    gram[0] += own_gram(640, wide_b)
    gram[1] = own_gram(WIDE, NARROW)

    places = (x * 4 + y, y * 4 + x)
    for t in range(8):
        h, m, r = t // 4, (t // 2) % 2, t % 2
        rows = pl.ds(pl.multiple_of(places[h] * 16 + r * 8, 8), 8)
        slices[t] = gram[m, rows, h * 128 : h * 128 + 128]
    gram_sends = [
        links.start(slices.at[(z + d) % 8], zland.at[d - 1], zs[d - 1]) for d in range(1, 8)
    ]

    for copy in shares:
        copy.wait_recv()
    z_chain(1, 0, w_of(1 - c, 0, WIDE))
    z_chain(1, 1, w_of(1 - c, WIDE, NARROW))

    def z_step():
        for chain in chains:
            next(chain, None)

    for copy in gram_sends:
        copy.wait_recv()
    total = slices[z]
    for d in range(7):
        total = total + zland[d]
    place = places[0] + (z // 4) * (places[1] - places[0])
    own = gathered.at[z // 4, pl.ds(pl.multiple_of(place * 32 + (z % 4) * 8, 8), 8)]
    own[...] = total
    gram_sends = [links.start(own, own, zs[d]) for d in range(7)]
    z_step()
    for copy in gram_sends:
        copy.wait_recv()
    def gather_gram(h, first, second):
        yield from direct_gather(links, gathered, h, first["q"] * 128, 32, **second)
        yield from direct_gather(links, gathered, h, 0, 128, **first)

    stages = [gather_gram(0, x_ring, y_ring), gather_gram(1, y_ring, x_ring)]
    for i in range(3):
        for stage in stages:
            next(stage, None)
        if i < 2:
            links.finish(40)
        z_step()
    for h in range(2):
        for p in range(16):
            for m in range(2):
                gram[m, p * 16 : p * 16 + 16, h * 128 : h * 128 + 128] = gathered[
                    h, p * 32 + m * 16 : p * 32 + m * 16 + 16, :
                ]

    exchanges = []

    def after_block(k):
        if k % 2:
            done = inverse.at[c, :, pl.ds(32 * (k - 1), 64)]
            exchanges.append(links.start(done, done, sibling))
            z_step()

    invert_factor(gram, inverse.at[c], after_block)
    def times_inverse(a, cc, kind):
        i_high, i_low = split(inverse[cc, kind])
        high, low = split(a)
        return bf16_dot(high, i_high, NT) + (
            bf16_dot(high, i_low, NT) + bf16_dot(low, i_high, NT)
        )

    def factor_of(i, cc, kind):
        row = i * 64 + kind * 32
        w = jnp.concatenate([wfull[k, row : row + 32, :] for k in range(8)], axis=0)
        factor = times_inverse(w, cc, kind)
        fac[2 * kind + cc] = factor
        squares = jnp.sum(factor * factor, axis=0, keepdims=True)
        return [squares[:, 0:128], squares[:, 128:256]]

    def ortho_half(cc):
        start = cc * HALF
        ow[cc] = times_inverse(raw_rows(start, WIDE), cc, 0)
        on[cc] = times_inverse(raw_rows(start + WIDE, NARROW), cc, 1)

    for chain in chains[0:2]:
        for _ in chain:
            pass
    for kind in range(2):
        for h, squares in enumerate(factor_of(0, c, kind)):
            row = pl.ds(pl.multiple_of((2 * kind + c) * 2, 2) + h, 1)
            sq[row, :] = squares
    for chain in chains[2:4]:
        for _ in chain:
            pass
    for copy in exchanges:
        copy.wait_recv()
    for kind in range(2):
        for h, squares in enumerate(factor_of(1, 1 - c, kind)):
            row = pl.ds(pl.multiple_of((2 * kind + 1 - c) * 2, 2) + h, 1)
            sq[row, :] = squares
    sq_land[0] = sq[...]
    sends = [links.start(sq_land.at[0], sq_land.at[d], device) for d, device in others]
    ortho_half(c)
    ortho_half(1 - c)
    total = sq_land[0]
    for (d, _), copy in zip(others, sends):
        copy.wait_recv()
        total = total + sq_land[d]
    sq[...] = total
    links.finish()


def last_kernel(
    bw, bn, ow, on, fac, sq, wmo, wbo, wup, nmo, nbo, nup, f_t, b_high, b_low
):
    kinds = ((bw, ow, wmo, wbo, wup, D), (bn, on, nmo, nbo, nup, KVW))

    which, step = pl.program_id(0), pl.program_id(1)

    @pl.when(step == 0)
    def _():
        for kind in range(2):
            factor = fac[kind, which]
            basis = factor * lax.rsqrt(sq[kind, which] + 1e-6)
            kinds[kind][3][0] = basis
            f_t[kind] = factor.astype(BF16).T
            b_high[kind], b_low[kind] = split(basis.T)

    for kind, (buffer, ortho, m_out, _, update, rows) in enumerate(kinds):
        n = m_out.shape[1]
        at = pl.ds(pl.multiple_of(step * n, n), n)
        o_high, o_low = split(ortho[which, at, :])
        m_out[0] = buffer[which, at, :] - 0.05 * bf16_dot(o_high, f_t[kind])
        product = bf16_dot(o_high, b_high[kind]) + (
            bf16_dot(o_high, b_low[kind]) + bf16_dot(o_low, b_high[kind])
        )
        update[0] = ((rows * D / RANK) ** 0.5 * product).astype(BF16)


def local(wide_momentum, wide_grad, wide_basis, narrow_momentum, narrow_grad, narrow_basis):
    vmem = pl.BlockSpec(memory_space=pltpu.VMEM)
    bw = wide_momentum + wide_grad.astype(F32)
    bn = narrow_momentum + narrow_grad.astype(F32)
    copies = 192
    ow, on, fac, sq = pl.pallas_call(
        main_kernel,
        out_shape=(
            jax.ShapeDtypeStruct((2, WIDE, RANK), F32),
            jax.ShapeDtypeStruct((2, NARROW, RANK), F32),
            jax.ShapeDtypeStruct((4, COLS, RANK), F32),
            jax.ShapeDtypeStruct((8, 128), F32),
        ),
        in_specs=[vmem] * 4,
        out_specs=[vmem] * 4,
        scratch_shapes=[
            pltpu.VMEM((2 * HALF, COLS), BF16),
            pltpu.VMEM((2 * HALF, COLS), BF16),
            pltpu.VMEM((2, 2, COLS, RANK), BF16),
            pltpu.VMEM((2, 2, COLS, RANK), BF16),
            pltpu.VMEM((2, 2 * HALF, 128), F32),
            pltpu.VMEM((2, 2 * HALF, 128), F32),
            pltpu.VMEM((2, HALF, 128), F32),
            pltpu.VMEM((2, 2, 2, 4, 160, 128), F32),
            pltpu.VMEM((2, RANK, RANK), F32),
            pltpu.VMEM((RANK, RANK), F32),
            pltpu.VMEM((COLS, RANK), F32),
            pltpu.VMEM((8, 8, 128), F32),
            pltpu.VMEM((7, 8, 128), F32),
            pltpu.VMEM((2, 512, 128), F32),
            pltpu.VMEM((8, 128, RANK), F32),
            pltpu.VMEM((8, 128, RANK), F32),
            pltpu.VMEM((2, 4, 128, RANK), F32),
            pltpu.VMEM((2, 2, RANK, RANK), F32),
            pltpu.VMEM((32, 8, 128), F32),
            pltpu.SemaphoreType.DMA((copies,)),
            pltpu.SemaphoreType.DMA((copies,)),
        ],
        compiler_params=pltpu.CompilerParams(
            collective_id=0, has_side_effects=True, vmem_limit_bytes=36 * 2**20
        ),
    )(bw, bn, wide_basis, narrow_basis)

    def rows(n):
        return pl.BlockSpec((1, n, COLS), lambda m, i: (m, i, 0))

    basis_out = pl.BlockSpec((1, COLS, RANK), lambda m, i: (m, 0, 0))
    steps = 2
    w, n = WIDE // steps, NARROW // steps
    return pl.pallas_call(
        last_kernel,
        grid=(2, steps),
        out_shape=(
            jax.ShapeDtypeStruct((2, WIDE, COLS), F32),
            jax.ShapeDtypeStruct((2, COLS, RANK), F32),
            jax.ShapeDtypeStruct((2, WIDE, COLS), BF16),
            jax.ShapeDtypeStruct((2, NARROW, COLS), F32),
            jax.ShapeDtypeStruct((2, COLS, RANK), F32),
            jax.ShapeDtypeStruct((2, NARROW, COLS), BF16),
        ),
        in_specs=[
            vmem,
        ] * 6,
        out_specs=[rows(w), basis_out, rows(w), rows(n), basis_out, rows(n)],
        scratch_shapes=[pltpu.VMEM((2, RANK, COLS), BF16)] * 3,
        compiler_params=pltpu.CompilerParams(vmem_limit_bytes=24 * 2**20),
    )(
        bw, bn, ow, on,
        fac.reshape(2, 2, COLS, RANK), sq.reshape(2, 2, 1, RANK),
    )


def solution(mesh):
    return jax.shard_map(
        local,
        mesh=mesh,
        in_specs=(
            P(None, "mp", "fsdp"),
            P(None, "mp", "fsdp"),
            P(None, "fsdp", None),
            P(None, "mp", "fsdp"),
            P(None, "mp", "fsdp"),
            P(None, "fsdp", None),
        ),
        out_specs=(
            P(None, "mp", "fsdp"),
            P(None, "fsdp", None),
            P(None, "mp", "fsdp"),
            P(None, "mp", "fsdp"),
            P(None, "fsdp", None),
            P(None, "mp", "fsdp"),
        ),
        check_vma=False,
    )
```

```python
import jax
import jax.numpy as jnp
from jax import lax
from jax.experimental import pallas as pl
from jax.experimental.pallas import tpu as pltpu
from jax.sharding import PartitionSpec as P

D = 8192
KVW = 1024
RANK = 256
WIDE = 1024
NARROW = 128
COLS = 256
HALF = WIDE + NARROW
F32 = jnp.float32
BF16 = jnp.bfloat16
MESH = pl.DeviceIdType.MESH
EXACT = lax.Precision.HIGHEST

NN = (((1,), (0,)), ((), ()))
NT = (((1,), (1,)), ((), ()))
TN = (((0,), (0,)), ((), ()))


def exact_dot(a, b, dims=NN):
    return lax.dot_general(a, b, dims, precision=EXACT, preferred_element_type=F32)


def split(a):
    high = a.astype(BF16)
    return high, (a - high.astype(F32)).astype(BF16)


def bf16_dot(a, b, dims=NN):
    return lax.dot_general(a, b, dims, preferred_element_type=F32)


class Links:
    def __init__(self, send, recv):
        self.send, self.recv = send, recv
        self.count = 0
        self.started = []

    def start(self, src, dst, device):
        i = self.count
        self.count += 1
        copy = pltpu.make_async_remote_copy(
            src_ref=src,
            dst_ref=dst,
            send_sem=self.send.at[i],
            recv_sem=self.recv.at[i],
            device_id=device,
            device_id_type=MESH,
        )
        copy.start()
        self.started.append(copy)
        return copy

    def finish(self, most=None):
        n = len(self.started) if most is None else most
        for copy in self.started[:n]:
            copy.wait_send()
        self.started = self.started[n:]


def ring_reduce(links, buf, out, h, base, chunk, cut, q, peers, land):
    after, before = (q + 1) % 4, (q + 3) % 4
    right, left = peers[0], peers[2]

    def rows(c, lo, n):
        return pl.ds(pl.multiple_of(base + c * chunk + lo, 8), n)

    far = (q + 2) % 4
    a = links.start(buf.at[h, rows(far, 0, cut)], land.at[0, pl.ds(0, cut)], right)
    b = links.start(
        buf.at[h, rows(far, cut, chunk - cut)], land.at[1, pl.ds(0, chunk - cut)], left
    )
    yield
    a.wait_recv()
    buf[h, rows(after, 0, cut), :] += land[0, 0:cut, :]
    a = links.start(buf.at[h, rows(after, 0, chunk)], land.at[2, pl.ds(0, chunk)], right)
    b.wait_recv()
    buf[h, rows(before, cut, chunk - cut), :] += land[1, 0 : chunk - cut, :]
    b = links.start(buf.at[h, rows(before, 0, chunk)], land.at[3, pl.ds(0, chunk)], left)
    yield
    a.wait_recv()
    b.wait_recv()
    out[h, rows(q, 0, chunk), :] = (
        buf[h, rows(q, 0, chunk), :] + land[2, 0:chunk, :] + land[3, 0:chunk, :]
    )


def ring_gather(links, buf, h, base, chunk, cut, q, peers):
    after, before = (q + 1) % 4, (q + 3) % 4
    right, left = peers[0], peers[2]

    def part(c, lo, n):
        return buf.at[h, pl.ds(pl.multiple_of(base + c * chunk + lo, 8), n)]

    own = part(q, 0, chunk)
    a = links.start(own, own, right)
    b = links.start(own, own, left)
    yield
    a.wait_recv()
    piece = part(before, 0, cut)
    a = links.start(piece, piece, right)
    b.wait_recv()
    piece = part(after, cut, chunk - cut)
    b = links.start(piece, piece, left)
    yield
    a.wait_recv()
    b.wait_recv()


def direct_reduce(links, buf, out, h, base, chunk, q, peers, land):
    def rows(c):
        return pl.ds(pl.multiple_of(base + c * chunk, 8), chunk)

    copies = [
        links.start(buf.at[h, rows((q + d) % 4)], land.at[d, pl.ds(0, chunk)], peers[d - 1])
        for d in (2, 1, 3)
    ]
    yield
    for copy in copies:
        copy.wait_recv()
    total = buf[h, rows(q), :]
    for d in (1, 2, 3):
        total = total + land[d, 0:chunk, :]
    out[h, rows(q), :] = total


def direct_gather(links, buf, h, base, chunk, q, peers):
    own = buf.at[h, pl.ds(pl.multiple_of(base + q * chunk, 8), chunk)]
    copies = [links.start(own, own, peers[d - 1]) for d in (2, 1, 3)]
    yield
    for copy in copies:
        copy.wait_recv()


def z_reduce_gather(links, buf, out, land, lo, n, q, right, left):
    half = n // 2

    def part(ref, i, start, size):
        return ref.at[i, pl.ds(lo + start, size)]

    def chunk(ref, i):
        return part(ref, i % 8, 0, n)

    def add(i, slot, start, size):
        rows = slice(lo + start, lo + start + size)
        buf[i % 8, rows, :] += land[slot[0], slot[1], rows, :]

    a = links.start(
        part(buf, (q + 4) % 8, 0, half), part(land.at[0], 0, 0, half), right
    )
    b = links.start(
        part(buf, (q + 4) % 8, half, half), part(land.at[1], 0, half, half), left
    )
    yield
    for s in (1, 2, 3):
        size = half if s == 1 else n
        a.wait_recv()
        add(q + 4 - s, (0, s - 1), 0, size)
        a = links.start(chunk(buf, q + 4 - s), part(land.at[0], s, 0, n), right)
        b.wait_recv()
        add(q + 4 + s, (1, s - 1), n - size, size)
        b = links.start(chunk(buf, q + 4 + s), part(land.at[1], s, 0, n), left)
        yield
    a.wait_recv()
    b.wait_recv()
    rows = slice(lo, lo + n)
    out[q, rows, :] = buf[q, rows, :] + land[0, 3, rows, :] + land[1, 3, rows, :]
    a = links.start(chunk(out, q), chunk(out, q), right)
    b = links.start(chunk(out, q), chunk(out, q), left)
    yield
    for s in (1, 2):
        a.wait_recv()
        a = links.start(chunk(out, q + 8 - s), chunk(out, q + 8 - s), right)
        b.wait_recv()
        b = links.start(chunk(out, q + s), chunk(out, q + s), left)
        yield
    a.wait_recv()
    piece = part(out, (q + 5) % 8, 0, half)
    a = links.start(piece, piece, right)
    b.wait_recv()
    piece = part(out, (q + 3) % 8, half, half)
    b = links.start(piece, piece, left)
    yield
    a.wait_recv()
    b.wait_recv()


def together(first, second, after):
    done = object()
    ended = False
    while first or second:
        first = [s for s in first if next(s, done) is not done]
        if not first and not ended:
            after()
            ended = True
        second = [s for s in second if next(s, done) is not done]


def block_inverse(e):
    lane = lax.broadcasted_iota(jnp.int32, (8, 128), 1)
    sub = lax.broadcasted_iota(jnp.int32, (8, 128), 0)
    group = (lane // 64) * 64

    def pick(tile, index):
        return jnp.take_along_axis(tile, group + index, axis=1)

    e = list(e)
    for g in range(4):
        cols = [[pick(e[i], 8 * g + t) for i in range(g, 4)] for t in range(8)]
        for t in range(8):
            pivot = cols[t][0][t : t + 1, :]
            inv = pl.reciprocal(pivot, approx=True)
            inv = inv * (2.0 - pivot * inv)
            for n, i in enumerate(range(g, 4)):
                f = cols[t][n] * inv
                if n == 0:
                    f = jnp.where(sub > t, f, 0.0)
                e[i] = e[i] - f * e[g][t : t + 1, :]
                for s in range(t + 1, 8):
                    cols[s][n] = cols[s][n] - f * cols[s][0][t : t + 1, :]
    return [tile * lax.rsqrt(pick(tile, 8 * i + sub)) for i, tile in enumerate(e)]


def invert_factor(a_ref, out, after):
    lane = lax.broadcasted_iota(jnp.int32, (32, 128), 1)
    row = lax.broadcasted_iota(jnp.int32, (32, 128), 0)
    eye = jnp.where(lane % 32 == row, 1.0, 0.0)
    col = lax.broadcasted_iota(jnp.int32, (32, 256), 1)
    wide_row = lax.broadcasted_iota(jnp.int32, (32, 256), 0)

    def turned(v, by):
        return pltpu.roll(v, by % 128, 1) if by % 128 else v

    blocks = [a_ref[m, 0:32, 0:128] for m in range(2)]
    panels = None
    for k in range(8):
        at, below = 32 * k, 32 * k + 32
        base, low = at // 128 * 128, below // 128 * 128
        if k > 0:
            for m in range(2):
                change = exact_dot(panels[m][:, base:256], panels[m], TN)
                under = lax.broadcasted_iota(jnp.int32, (256 - at, 256), 1)
                rest = jnp.where(
                    (under >= at - 32) & (under < at), 0.0, a_ref[m, at:256, :]
                )
                a_ref[m, at:256, :] = rest - change[at - base :, :]
        d0, d1 = turned(blocks[0], base - at), turned(blocks[1], 64 + base - at)
        e = jnp.where(lane < 32, d0, jnp.where((lane >= 64) & (lane < 96), d1, eye))
        e = jnp.concatenate(
            block_inverse([e[8 * i : 8 * i + 8] for i in range(4)]), axis=0
        )
        inside = (col >= at) & (col < below)
        wide_eye = jnp.where(col - at == wide_row, 1.0, 0.0)
        panels, blocks = [], []
        for m in range(2):
            t = turned(e, 96 - 64 * m)[:, 0:32]
            panel = exact_dot(t, jnp.where(inside, wide_eye, a_ref[m, at:below, :]))
            panels.append(panel)
            if below < 256:
                near = panel[:, low : low + 128]
                change = exact_dot(near, near, TN)
                blocks.append(
                    a_ref[m, below : below + 32, low : low + 128]
                    - change[below - low : below - low + 32, :]
                )
            a_ref[m, at:below, :] = panel
            out[m, at:below, :] = jnp.where(col <= at + wide_row, panel, 0.0)
        after(k)


def main_kernel(
    bw, bn, wb, nb,
    ow, on, fac, sq,
    bh, bl, vh, vl, part, full, swap, land, gram, cross, w_first, slices, zland, gathered,
    wpart, wfull, wland, inverse, sq_land,
    send, recv,
):
    z = lax.axis_index("mp")
    f = lax.axis_index("fsdp")
    c = f % 2
    x = (f // 2) % 4
    y = f // 8

    def plane(xx, yy, cc):
        return {"fsdp": ((yy % 4) * 4 + xx % 4) * 2 + cc}

    sibling = plane(x, y, 1 - c)
    xs = [plane(x + d, y, c) for d in (1, 2, 3)]
    others = [(d, {"fsdp": (f + d) % 32}) for d in range(1, 32)]
    ys = [plane(x, y + d, c) for d in (1, 2, 3)]
    zs = [{"mp": (z + d) % 8} for d in range(1, 8)]

    barrier = pltpu.get_barrier_semaphore()
    partners = [device for _, device in others] + zs
    for device in partners:
        pl.semaphore_signal(barrier, inc=1, device_id=device, device_id_type=MESH)

    links = Links(send, recv)
    sets = ((0, 640), (640, 512))
    wide_b = WIDE - 640

    def split_basis(cc):
        for kind, basis in enumerate((wb, nb)):
            high, low = split(basis[cc])
            vh[cc, kind] = high
            vl[cc, kind] = low

    def raw_rows_of(cc, kind, r, n, buffer):
        rows = pl.ds(pl.multiple_of(cc * HALF + r, 16), n)
        high, low = split(buffer)
        bh[rows, :] = high
        bl[rows, :] = low
        v_high = vh[cc, kind]
        raw = bf16_dot(high, v_high) + (bf16_dot(high, vl[cc, kind]) + bf16_dot(low, v_high))
        part[0, rows, :] = raw[:, 0:128]
        part[1, rows, :] = raw[:, 128:256]

    def raw_set(cc, i):
        lo, n = ((0, 640), (640, wide_b))[i]
        raw_rows_of(cc, 0, lo, n, bw[cc, lo : lo + n, :])

        if i == 1:
            raw_rows_of(cc, 1, WIDE, NARROW, bn[cc])

    def half_rows(cc, start, n):
        return pl.ds(pl.multiple_of(cc * HALF + start, 8), n)

    split_basis(1 - c)
    raw_set(1 - c, 0)
    pl.semaphore_wait(barrier, len(partners))
    exchanges = []
    for i, (start, n) in enumerate(sets):
        if i == 1:
            raw_set(1 - c, 1)
        exchanges.append(
            links.start(
                part.at[:, half_rows(1 - c, start, n)], swap.at[:, pl.ds(start, n)], sibling
            )
        )
    split_basis(c)

    x_ring = dict(q=x, peers=xs)
    y_ring = dict(q=y, peers=ys)
    base = c * HALF

    def gather_both(buffer, h, start, sizes, first, second):
        yield from direct_gather(
            links, buffer, h, start + first["q"] * sizes[0], sizes[1], **second
        )
        yield from ring_gather(links, buffer, h, start, sizes[0], sizes[0] // 2, **first)

    shares = []

    def whole_sum(i, h):
        start, n = sets[i]
        big, small = n // 4, n // 16
        first, second = (x_ring, y_ring) if h == 0 else (y_ring, x_ring)
        yield from ring_reduce(
            links, part, part, h, base + start, big, big // 2, land=land.at[i, h, 0], **first
        )
        yield from direct_reduce(
            links, part, full, h, base + start + first["q"] * big, small,
            land=land.at[i, h, 1], **second
        )
        yield from gather_both(full, h, base + start, (big, small), first, second)
        done = full.at[h, half_rows(c, start, n)]
        shares.append(links.start(done, done, sibling))

    stages = []
    for i, (start, n) in enumerate(sets):
        raw_set(c, i)
        exchanges[i].wait_recv()
        rows = half_rows(c, start, n)
        part[:, rows, :] += swap[:, start : start + n, :]
        for h in range(2):
            stage = whole_sum(i, h)
            next(stage)
            stages.append(stage)

    def raw_rows(start, n):
        rows = pl.ds(pl.multiple_of(start, 8), n)
        return jnp.concatenate([full[0, rows, :], full[1, rows, :]], axis=1)

    def own_gram(start, n):
        raw = raw_rows(base + start, n)
        high = raw.astype(BF16)
        middle, low = split(raw - high.astype(F32))
        cross[...] = bf16_dot(high, middle, TN) + bf16_dot(high, low, TN)
        mirrored = cross[...] + cross[...].T
        return bf16_dot(high, high, TN) + (mirrored + bf16_dot(middle, middle, TN))

    def w_of(cc, start, n):
        start = cc * HALF + start
        rows = pl.ds(pl.multiple_of(start, 16), n)
        high, low = split(raw_rows(start, n))
        b_high = bh[rows, :]
        return bf16_dot(b_high, high, TN) + (
            bf16_dot(b_high, low, TN) + bf16_dot(bl[rows, :], high, TN)
        )

    def first_set():
        gram[0] = own_gram(0, 640)
        w_first[...] = w_of(c, 0, 640)

    together(stages[0:2], stages[2:4], after=first_set)
    def put_w(i, kind, w):
        row = i * 64 + kind * 32
        for k in range(8):
            wpart[k, row : row + 32, :] = w[k * 32 : k * 32 + 32, :]

    chains = []

    def z_chain(i, kind, w):
        put_w(i, kind, w)
        row = i * 64 + kind * 32
        chain = z_reduce_gather(links, wpart, wfull, wland, row, 32, z, zs[0], zs[6])
        next(chain)
        chains.append(chain)

    z_chain(0, 0, w_first[...] + w_of(c, 640, wide_b))
    z_chain(0, 1, w_of(c, WIDE, NARROW))

    gram[0] += own_gram(640, wide_b)
    gram[1] = own_gram(WIDE, NARROW)

    places = (x * 4 + y, y * 4 + x)
    for t in range(8):
        h, m, r = t // 4, (t // 2) % 2, t % 2
        rows = pl.ds(pl.multiple_of(places[h] * 16 + r * 8, 8), 8)
        slices[t] = gram[m, rows, h * 128 : h * 128 + 128]
    gram_sends = [
        links.start(slices.at[(z + d) % 8], zland.at[d - 1], zs[d - 1]) for d in range(1, 8)
    ]

    for copy in shares:
        copy.wait_recv()
    z_chain(1, 0, w_of(1 - c, 0, WIDE))
    z_chain(1, 1, w_of(1 - c, WIDE, NARROW))

    def z_step(live=4, sent=0):
        links.finish(sent)
        for chain in chains[0:live]:
            next(chain, None)

    for copy in gram_sends:
        copy.wait_recv()
    total = slices[z]
    for d in range(7):
        total = total + zland[d]
    place = places[0] + (z // 4) * (places[1] - places[0])
    own = gathered.at[z // 4, pl.ds(pl.multiple_of(place * 32 + (z % 4) * 8, 8), 8)]
    own[...] = total
    gram_sends = [links.start(own, own, zs[d]) for d in range(7)]
    z_step(live=2)
    for copy in gram_sends:
        copy.wait_recv()
    def gather_gram(h, first, second):
        yield from direct_gather(links, gathered, h, first["q"] * 128, 32, **second)
        yield from direct_gather(links, gathered, h, 0, 128, **first)

    stages = [gather_gram(0, x_ring, y_ring), gather_gram(1, y_ring, x_ring)]
    for i in range(3):
        for stage in stages:
            next(stage, None)
        if i < 2:
            links.finish(40)
        z_step()
    for h in range(2):
        for p in range(16):
            for m in range(2):
                gram[m, p * 16 : p * 16 + 16, h * 128 : h * 128 + 128] = gathered[
                    h, p * 32 + m * 16 : p * 32 + m * 16 + 16, :
                ]

    exchanges = []

    def after_block(k):
        if k % 2:
            done = inverse.at[c, :, pl.ds(32 * (k - 1), 64)]
            exchanges.append(links.start(done, done, sibling))
        if k in (1, 3, 4, 6, 7):
            z_step(sent=16)

    invert_factor(gram, inverse.at[c], after_block)
    def times_inverse(a, cc, kind):
        i_high, i_low = split(inverse[cc, kind])
        high, low = split(a)
        return bf16_dot(high, i_high, NT) + (
            bf16_dot(high, i_low, NT) + bf16_dot(low, i_high, NT)
        )

    def factor_of(i, cc, kind):
        row = i * 64 + kind * 32
        w = jnp.concatenate([wfull[k, row : row + 32, :] for k in range(8)], axis=0)
        factor = times_inverse(w, cc, kind)
        fac[2 * kind + cc] = factor
        squares = jnp.sum(factor * factor, axis=0, keepdims=True)
        return [squares[:, 0:128], squares[:, 128:256]]

    def ortho_half(cc):
        start = cc * HALF
        ow[cc] = times_inverse(raw_rows(start, WIDE), cc, 0)
        on[cc] = times_inverse(raw_rows(start + WIDE, NARROW), cc, 1)

    for chain in chains[0:2]:
        for _ in chain:
            pass
    for kind in range(2):
        for h, squares in enumerate(factor_of(0, c, kind)):
            row = pl.ds(pl.multiple_of((2 * kind + c) * 2, 2) + h, 1)
            sq[row, :] = squares
    for chain in chains[2:4]:
        for _ in chain:
            pass
    for copy in exchanges:
        copy.wait_recv()
    for kind in range(2):
        for h, squares in enumerate(factor_of(1, 1 - c, kind)):
            row = pl.ds(pl.multiple_of((2 * kind + 1 - c) * 2, 2) + h, 1)
            sq[row, :] = squares
    sq_land[0] = sq[...]
    sends = [links.start(sq_land.at[0], sq_land.at[d], device) for d, device in others]
    ortho_half(c)
    ortho_half(1 - c)
    total = sq_land[0]
    for (d, _), copy in zip(others, sends):
        copy.wait_recv()
        total = total + sq_land[d]
    sq[...] = total
    links.finish()


def last_kernel(
    bw, bn, ow, on, fac, sq, wmo, wbo, wup, nmo, nbo, nup, f_t, b_high, b_low
):
    kinds = ((bw, ow, wmo, wbo, wup, D), (bn, on, nmo, nbo, nup, KVW))

    which, step = pl.program_id(0), pl.program_id(1)

    @pl.when(step == 0)
    def _():
        for kind in range(2):
            factor = fac[kind, which]
            basis = factor * lax.rsqrt(sq[kind, which] + 1e-6)
            kinds[kind][3][0] = basis
            f_t[kind] = factor.astype(BF16).T
            b_high[kind], b_low[kind] = split(basis.T)

    for kind, (buffer, ortho, m_out, _, update, rows) in enumerate(kinds):
        n = m_out.shape[1]
        at = pl.ds(pl.multiple_of(step * n, n), n)
        o_high, o_low = split(ortho[which, at, :])
        m_out[0] = buffer[which, at, :] - 0.05 * bf16_dot(o_high, f_t[kind])
        product = bf16_dot(o_high, b_high[kind]) + (
            bf16_dot(o_high, b_low[kind]) + bf16_dot(o_low, b_high[kind])
        )
        update[0] = ((rows * D / RANK) ** 0.5 * product).astype(BF16)


def local(wide_momentum, wide_grad, wide_basis, narrow_momentum, narrow_grad, narrow_basis):
    vmem = pl.BlockSpec(memory_space=pltpu.VMEM)
    bw = wide_momentum + wide_grad.astype(F32)
    bn = narrow_momentum + narrow_grad.astype(F32)
    copies = 192
    ow, on, fac, sq = pl.pallas_call(
        main_kernel,
        out_shape=(
            jax.ShapeDtypeStruct((2, WIDE, RANK), F32),
            jax.ShapeDtypeStruct((2, NARROW, RANK), F32),
            jax.ShapeDtypeStruct((4, COLS, RANK), F32),
            jax.ShapeDtypeStruct((8, 128), F32),
        ),
        in_specs=[vmem] * 4,
        out_specs=[vmem] * 4,
        scratch_shapes=[
            pltpu.VMEM((2 * HALF, COLS), BF16),
            pltpu.VMEM((2 * HALF, COLS), BF16),
            pltpu.VMEM((2, 2, COLS, RANK), BF16),
            pltpu.VMEM((2, 2, COLS, RANK), BF16),
            pltpu.VMEM((2, 2 * HALF, 128), F32),
            pltpu.VMEM((2, 2 * HALF, 128), F32),
            pltpu.VMEM((2, HALF, 128), F32),
            pltpu.VMEM((2, 2, 2, 4, 160, 128), F32),
            pltpu.VMEM((2, RANK, RANK), F32),
            pltpu.VMEM((RANK, RANK), F32),
            pltpu.VMEM((COLS, RANK), F32),
            pltpu.VMEM((8, 8, 128), F32),
            pltpu.VMEM((7, 8, 128), F32),
            pltpu.VMEM((2, 512, 128), F32),
            pltpu.VMEM((8, 128, RANK), F32),
            pltpu.VMEM((8, 128, RANK), F32),
            pltpu.VMEM((2, 4, 128, RANK), F32),
            pltpu.VMEM((2, 2, RANK, RANK), F32),
            pltpu.VMEM((32, 8, 128), F32),
            pltpu.SemaphoreType.DMA((copies,)),
            pltpu.SemaphoreType.DMA((copies,)),
        ],
        compiler_params=pltpu.CompilerParams(
            collective_id=0, has_side_effects=True, vmem_limit_bytes=36 * 2**20
        ),
    )(bw, bn, wide_basis, narrow_basis)

    def rows(n):
        return pl.BlockSpec((1, n, COLS), lambda m, i: (m, i, 0))

    basis_out = pl.BlockSpec((1, COLS, RANK), lambda m, i: (m, 0, 0))
    steps = 2
    w, n = WIDE // steps, NARROW // steps
    return pl.pallas_call(
        last_kernel,
        grid=(2, steps),
        out_shape=(
            jax.ShapeDtypeStruct((2, WIDE, COLS), F32),
            jax.ShapeDtypeStruct((2, COLS, RANK), F32),
            jax.ShapeDtypeStruct((2, WIDE, COLS), BF16),
            jax.ShapeDtypeStruct((2, NARROW, COLS), F32),
            jax.ShapeDtypeStruct((2, COLS, RANK), F32),
            jax.ShapeDtypeStruct((2, NARROW, COLS), BF16),
        ),
        in_specs=[
            vmem,
        ] * 6,
        out_specs=[rows(w), basis_out, rows(w), rows(n), basis_out, rows(n)],
        scratch_shapes=[pltpu.VMEM((2, RANK, COLS), BF16)] * 3,
        compiler_params=pltpu.CompilerParams(vmem_limit_bytes=24 * 2**20),
    )(
        bw, bn, ow, on,
        fac.reshape(2, 2, COLS, RANK), sq.reshape(2, 2, 1, RANK),
    )


def solution(mesh):
    return jax.shard_map(
        local,
        mesh=mesh,
        in_specs=(
            P(None, "mp", "fsdp"),
            P(None, "mp", "fsdp"),
            P(None, "fsdp", None),
            P(None, "mp", "fsdp"),
            P(None, "mp", "fsdp"),
            P(None, "fsdp", None),
        ),
        out_specs=(
            P(None, "mp", "fsdp"),
            P(None, "fsdp", None),
            P(None, "mp", "fsdp"),
            P(None, "mp", "fsdp"),
            P(None, "fsdp", None),
            P(None, "mp", "fsdp"),
        ),
        check_vma=False,
    )
```

```python
import jax
import jax.numpy as jnp
from jax import lax
from jax.experimental import pallas as pl
from jax.experimental.pallas import tpu as pltpu
from jax.sharding import PartitionSpec as P

D = 8192
KVW = 1024
RANK = 256
WIDE = 1024
NARROW = 128
COLS = 256
HALF = WIDE + NARROW
F32 = jnp.float32
BF16 = jnp.bfloat16
MESH = pl.DeviceIdType.MESH
EXACT = lax.Precision.HIGHEST

NN = (((1,), (0,)), ((), ()))
NT = (((1,), (1,)), ((), ()))
TN = (((0,), (0,)), ((), ()))


def exact_dot(a, b, dims=NN):
    return lax.dot_general(a, b, dims, precision=EXACT, preferred_element_type=F32)


def split(a):
    high = a.astype(BF16)
    return high, (a - high.astype(F32)).astype(BF16)


def bf16_dot(a, b, dims=NN):
    return lax.dot_general(a, b, dims, preferred_element_type=F32)


class Links:
    def __init__(self, send, recv):
        self.send, self.recv = send, recv
        self.count = 0
        self.started = []

    def start(self, src, dst, device):
        i = self.count
        self.count += 1
        copy = pltpu.make_async_remote_copy(
            src_ref=src,
            dst_ref=dst,
            send_sem=self.send.at[i],
            recv_sem=self.recv.at[i],
            device_id=device,
            device_id_type=MESH,
        )
        copy.start()
        self.started.append(copy)
        return copy

    def finish(self, most=None):
        n = len(self.started) if most is None else most
        for copy in self.started[:n]:
            copy.wait_send()
        self.started = self.started[n:]


def ring_reduce(links, buf, out, h, base, chunk, cut, q, peers, land):
    after, before = (q + 1) % 4, (q + 3) % 4
    right, left = peers[0], peers[2]

    def rows(c, lo, n):
        return pl.ds(pl.multiple_of(base + c * chunk + lo, 8), n)

    far = (q + 2) % 4
    a = links.start(buf.at[h, rows(far, 0, cut)], land.at[0, pl.ds(0, cut)], right)
    b = links.start(
        buf.at[h, rows(far, cut, chunk - cut)], land.at[1, pl.ds(0, chunk - cut)], left
    )
    yield
    a.wait_recv()
    buf[h, rows(after, 0, cut), :] += land[0, 0:cut, :]
    a = links.start(buf.at[h, rows(after, 0, chunk)], land.at[2, pl.ds(0, chunk)], right)
    b.wait_recv()
    buf[h, rows(before, cut, chunk - cut), :] += land[1, 0 : chunk - cut, :]
    b = links.start(buf.at[h, rows(before, 0, chunk)], land.at[3, pl.ds(0, chunk)], left)
    yield
    a.wait_recv()
    b.wait_recv()
    out[h, rows(q, 0, chunk), :] = (
        buf[h, rows(q, 0, chunk), :] + land[2, 0:chunk, :] + land[3, 0:chunk, :]
    )


def ring_gather(links, buf, h, base, chunk, cut, q, peers):
    after, before = (q + 1) % 4, (q + 3) % 4
    right, left = peers[0], peers[2]

    def part(c, lo, n):
        return buf.at[h, pl.ds(pl.multiple_of(base + c * chunk + lo, 8), n)]

    own = part(q, 0, chunk)
    a = links.start(own, own, right)
    b = links.start(own, own, left)
    yield
    a.wait_recv()
    piece = part(before, 0, cut)
    a = links.start(piece, piece, right)
    b.wait_recv()
    piece = part(after, cut, chunk - cut)
    b = links.start(piece, piece, left)
    yield
    a.wait_recv()
    b.wait_recv()


def direct_reduce(links, buf, out, h, base, chunk, q, peers, land):
    def rows(c):
        return pl.ds(pl.multiple_of(base + c * chunk, 8), chunk)

    copies = [
        links.start(buf.at[h, rows((q + d) % 4)], land.at[d, pl.ds(0, chunk)], peers[d - 1])
        for d in (2, 1, 3)
    ]
    yield
    for copy in copies:
        copy.wait_recv()
    total = buf[h, rows(q), :]
    for d in (1, 2, 3):
        total = total + land[d, 0:chunk, :]
    out[h, rows(q), :] = total


def direct_gather(links, buf, h, base, chunk, q, peers):
    own = buf.at[h, pl.ds(pl.multiple_of(base + q * chunk, 8), chunk)]
    copies = [links.start(own, own, peers[d - 1]) for d in (2, 1, 3)]
    yield
    for copy in copies:
        copy.wait_recv()


def z_reduce_gather(links, buf, out, land, lo, n, q, right, left):
    half = n // 2

    def part(ref, i, start, size):
        return ref.at[i, pl.ds(lo + start, size)]

    def chunk(ref, i):
        return part(ref, i % 8, 0, n)

    def add(i, slot, start, size):
        rows = slice(lo + start, lo + start + size)
        buf[i % 8, rows, :] += land[slot[0], slot[1], rows, :]

    a = links.start(
        part(buf, (q + 4) % 8, 0, half), part(land.at[0], 0, 0, half), right
    )
    b = links.start(
        part(buf, (q + 4) % 8, half, half), part(land.at[1], 0, half, half), left
    )
    yield
    for s in (1, 2, 3):
        size = half if s == 1 else n
        a.wait_recv()
        add(q + 4 - s, (0, s - 1), 0, size)
        a = links.start(chunk(buf, q + 4 - s), part(land.at[0], s, 0, n), right)
        b.wait_recv()
        add(q + 4 + s, (1, s - 1), n - size, size)
        b = links.start(chunk(buf, q + 4 + s), part(land.at[1], s, 0, n), left)
        yield
    a.wait_recv()
    b.wait_recv()
    rows = slice(lo, lo + n)
    out[q, rows, :] = buf[q, rows, :] + land[0, 3, rows, :] + land[1, 3, rows, :]
    a = links.start(chunk(out, q), chunk(out, q), right)
    b = links.start(chunk(out, q), chunk(out, q), left)
    yield
    for s in (1, 2):
        a.wait_recv()
        a = links.start(chunk(out, q + 8 - s), chunk(out, q + 8 - s), right)
        b.wait_recv()
        b = links.start(chunk(out, q + s), chunk(out, q + s), left)
        yield
    a.wait_recv()
    piece = part(out, (q + 5) % 8, 0, half)
    a = links.start(piece, piece, right)
    b.wait_recv()
    piece = part(out, (q + 3) % 8, half, half)
    b = links.start(piece, piece, left)
    yield
    a.wait_recv()
    b.wait_recv()


def together(first, second, after):
    done = object()
    ended = False
    while first or second:
        first = [s for s in first if next(s, done) is not done]
        if not first and not ended:
            after()
            ended = True
        second = [s for s in second if next(s, done) is not done]


def block_inverse(e):
    lane = lax.broadcasted_iota(jnp.int32, (8, 128), 1)
    sub = lax.broadcasted_iota(jnp.int32, (8, 128), 0)
    group = (lane // 64) * 64

    def pick(tile, index):
        return jnp.take_along_axis(tile, group + index, axis=1)

    e = list(e)
    for g in range(4):
        cols = [[pick(e[i], 8 * g + t) for i in range(g, 4)] for t in range(8)]
        for t in range(8):
            pivot = cols[t][0][t : t + 1, :]
            inv = pl.reciprocal(pivot, approx=True)
            inv = inv * (2.0 - pivot * inv)
            for n, i in enumerate(range(g, 4)):
                f = cols[t][n] * inv
                if n == 0:
                    f = jnp.where(sub > t, f, 0.0)
                e[i] = e[i] - f * e[g][t : t + 1, :]
                for s in range(t + 1, 8):
                    cols[s][n] = cols[s][n] - f * cols[s][0][t : t + 1, :]
    return [tile * lax.rsqrt(pick(tile, 8 * i + sub)) for i, tile in enumerate(e)]


def invert_factor(a_ref, out, after):
    lane = lax.broadcasted_iota(jnp.int32, (32, 128), 1)
    row = lax.broadcasted_iota(jnp.int32, (32, 128), 0)
    eye = jnp.where(lane % 32 == row, 1.0, 0.0)
    col = lax.broadcasted_iota(jnp.int32, (32, 256), 1)
    wide_row = lax.broadcasted_iota(jnp.int32, (32, 256), 0)

    def turned(v, by):
        return pltpu.roll(v, by % 128, 1) if by % 128 else v

    blocks = [a_ref[m, 0:32, 0:128] for m in range(2)]
    panels = None
    for k in range(8):
        at, below = 32 * k, 32 * k + 32
        base, low = at // 128 * 128, below // 128 * 128
        if k > 0:
            for m in range(2):
                change = exact_dot(panels[m][:, base:256], panels[m], TN)
                under = lax.broadcasted_iota(jnp.int32, (256 - at, 256), 1)
                rest = jnp.where(
                    (under >= at - 32) & (under < at), 0.0, a_ref[m, at:256, :]
                )
                a_ref[m, at:256, :] = rest - change[at - base :, :]
        d0, d1 = turned(blocks[0], base - at), turned(blocks[1], 64 + base - at)
        e = jnp.where(lane < 32, d0, jnp.where((lane >= 64) & (lane < 96), d1, eye))
        e = jnp.concatenate(
            block_inverse([e[8 * i : 8 * i + 8] for i in range(4)]), axis=0
        )
        inside = (col >= at) & (col < below)
        wide_eye = jnp.where(col - at == wide_row, 1.0, 0.0)
        panels, blocks = [], []
        for m in range(2):
            t = turned(e, 96 - 64 * m)[:, 0:32]
            panel = exact_dot(t, jnp.where(inside, wide_eye, a_ref[m, at:below, :]))
            panels.append(panel)
            if below < 256:
                near = panel[:, low : low + 128]
                change = exact_dot(near, near, TN)
                blocks.append(
                    a_ref[m, below : below + 32, low : low + 128]
                    - change[below - low : below - low + 32, :]
                )
            a_ref[m, at:below, :] = panel
            out[m, at:below, :] = jnp.where(col <= at + wide_row, panel, 0.0)
        after(k)


def main_kernel(
    bw, bn, wb, nb,
    ow, on, fac, sq,
    bh, bl, vh, vl, part, full, swap, land, gram, cross, w_first, slices, zland, gathered,
    wpart, wfull, wland, inverse, sq_land,
    send, recv,
):
    z = lax.axis_index("mp")
    f = lax.axis_index("fsdp")
    c = f % 2
    x = (f // 2) % 4
    y = f // 8

    def plane(xx, yy, cc):
        return {"fsdp": ((yy % 4) * 4 + xx % 4) * 2 + cc}

    sibling = plane(x, y, 1 - c)
    xs = [plane(x + d, y, c) for d in (1, 2, 3)]
    others = [(d, {"fsdp": (f + d) % 32}) for d in range(1, 32)]
    ys = [plane(x, y + d, c) for d in (1, 2, 3)]
    zs = [{"mp": (z + d) % 8} for d in range(1, 8)]

    barrier = pltpu.get_barrier_semaphore()
    partners = [device for _, device in others] + zs
    for device in partners:
        pl.semaphore_signal(barrier, inc=1, device_id=device, device_id_type=MESH)

    links = Links(send, recv)
    sets = ((0, 640), (640, 512))
    wide_b = WIDE - 640

    def split_basis(cc):
        for kind, basis in enumerate((wb, nb)):
            high, low = split(basis[cc])
            vh[cc, kind] = high
            vl[cc, kind] = low

    def raw_rows_of(cc, kind, r, n, buffer):
        rows = pl.ds(pl.multiple_of(cc * HALF + r, 16), n)
        high, low = split(buffer)
        bh[rows, :] = high
        bl[rows, :] = low
        v_high = vh[cc, kind]
        raw = bf16_dot(high, v_high) + (bf16_dot(high, vl[cc, kind]) + bf16_dot(low, v_high))
        part[0, rows, :] = raw[:, 0:128]
        part[1, rows, :] = raw[:, 128:256]

    def raw_set(cc, i):
        lo, n = ((0, 640), (640, wide_b))[i]
        raw_rows_of(cc, 0, lo, n, bw[cc, lo : lo + n, :])

        if i == 1:
            raw_rows_of(cc, 1, WIDE, NARROW, bn[cc])

    def half_rows(cc, start, n):
        return pl.ds(pl.multiple_of(cc * HALF + start, 8), n)

    split_basis(1 - c)
    raw_set(1 - c, 0)
    pl.semaphore_wait(barrier, len(partners))
    exchanges = []
    for i, (start, n) in enumerate(sets):
        if i == 1:
            raw_set(1 - c, 1)
        exchanges.append(
            links.start(
                part.at[:, half_rows(1 - c, start, n)], swap.at[:, pl.ds(start, n)], sibling
            )
        )
    split_basis(c)

    x_ring = dict(q=x, peers=xs)
    y_ring = dict(q=y, peers=ys)
    base = c * HALF

    def gather_both(buffer, h, start, sizes, first, second):
        yield from direct_gather(
            links, buffer, h, start + first["q"] * sizes[0], sizes[1], **second
        )
        yield from ring_gather(links, buffer, h, start, sizes[0], sizes[0] // 2, **first)

    shares = []

    def whole_sum(i, h):
        start, n = sets[i]
        big, small = n // 4, n // 16
        first, second = (x_ring, y_ring) if h == 0 else (y_ring, x_ring)
        yield from ring_reduce(
            links, part, part, h, base + start, big, big // 2, land=land.at[i, h, 0], **first
        )
        yield from direct_reduce(
            links, part, full, h, base + start + first["q"] * big, small,
            land=land.at[i, h, 1], **second
        )
        yield from gather_both(full, h, base + start, (big, small), first, second)
        done = full.at[h, half_rows(c, start, n)]
        shares.append(links.start(done, done, sibling))

    stages = []
    for i, (start, n) in enumerate(sets):
        raw_set(c, i)
        exchanges[i].wait_recv()
        rows = half_rows(c, start, n)
        part[:, rows, :] += swap[:, start : start + n, :]
        for h in range(2):
            stage = whole_sum(i, h)
            next(stage)
            stages.append(stage)

    def raw_rows(start, n):
        rows = pl.ds(pl.multiple_of(start, 8), n)
        return jnp.concatenate([full[0, rows, :], full[1, rows, :]], axis=1)

    def own_gram(start, n):
        raw = raw_rows(base + start, n)
        high = raw.astype(BF16)
        middle, low = split(raw - high.astype(F32))
        cross[...] = bf16_dot(high, middle, TN) + bf16_dot(high, low, TN)
        mirrored = cross[...] + cross[...].T
        return bf16_dot(high, high, TN) + (mirrored + bf16_dot(middle, middle, TN))

    def w_of(cc, start, n):
        start = cc * HALF + start
        rows = pl.ds(pl.multiple_of(start, 16), n)
        high, low = split(raw_rows(start, n))
        b_high = bh[rows, :]
        return bf16_dot(b_high, high, TN) + (
            bf16_dot(b_high, low, TN) + bf16_dot(bl[rows, :], high, TN)
        )

    def first_set():
        gram[0] = own_gram(0, 640)
        w_first[...] = w_of(c, 0, 640)

    together(stages[0:2], stages[2:4], after=first_set)
    def put_w(i, kind, w):
        row = i * 64 + kind * 32
        for k in range(8):
            wpart[k, row : row + 32, :] = w[k * 32 : k * 32 + 32, :]

    chains = []

    def z_chain(i, kind, w):
        put_w(i, kind, w)
        row = i * 64 + kind * 32
        chain = z_reduce_gather(links, wpart, wfull, wland, row, 32, z, zs[0], zs[6])
        next(chain)
        chains.append(chain)

    z_chain(0, 0, w_first[...] + w_of(c, 640, wide_b))
    z_chain(0, 1, w_of(c, WIDE, NARROW))

    gram[0] += own_gram(640, wide_b)
    gram[1] = own_gram(WIDE, NARROW)

    places = (x * 4 + y, y * 4 + x)
    for t in range(8):
        h, m, r = t // 4, (t // 2) % 2, t % 2
        rows = pl.ds(pl.multiple_of(places[h] * 16 + r * 8, 8), 8)
        slices[t] = gram[m, rows, h * 128 : h * 128 + 128]
    gram_sends = [
        links.start(slices.at[(z + d) % 8], zland.at[d - 1], zs[d - 1]) for d in range(1, 8)
    ]

    for copy in shares:
        copy.wait_recv()
    z_chain(1, 0, w_of(1 - c, 0, WIDE))
    z_chain(1, 1, w_of(1 - c, WIDE, NARROW))

    def z_step(live=4):
        for chain in chains[0:live]:
            next(chain, None)

    for copy in gram_sends:
        copy.wait_recv()
    total = slices[z]
    for d in range(7):
        total = total + zland[d]
    place = places[0] + (z // 4) * (places[1] - places[0])
    own = gathered.at[z // 4, pl.ds(pl.multiple_of(place * 32 + (z % 4) * 8, 8), 8)]
    own[...] = total
    gram_sends = [links.start(own, own, zs[d]) for d in range(7)]
    z_step(live=2)
    for copy in gram_sends:
        copy.wait_recv()
    def gather_gram(h, first, second):
        yield from direct_gather(links, gathered, h, first["q"] * 128, 32, **second)
        yield from direct_gather(links, gathered, h, 0, 128, **first)

    stages = [gather_gram(0, x_ring, y_ring), gather_gram(1, y_ring, x_ring)]
    for i in range(3):
        for stage in stages:
            next(stage, None)
        if i < 2:
            links.finish(40)
        z_step()
    for h in range(2):
        for p in range(16):
            for m in range(2):
                gram[m, p * 16 : p * 16 + 16, h * 128 : h * 128 + 128] = gathered[
                    h, p * 32 + m * 16 : p * 32 + m * 16 + 16, :
                ]

    exchanges = []

    def after_block(k):
        if k % 2:
            done = inverse.at[c, :, pl.ds(32 * (k - 1), 64)]
            exchanges.append(links.start(done, done, sibling))
            z_step()

    invert_factor(gram, inverse.at[c], after_block)
    def times_inverse(a, cc, kind):
        i_high, i_low = split(inverse[cc, kind])
        high, low = split(a)
        return bf16_dot(high, i_high, NT) + (
            bf16_dot(high, i_low, NT) + bf16_dot(low, i_high, NT)
        )

    def factor_of(i, cc, kind):
        row = i * 64 + kind * 32
        w = jnp.concatenate([wfull[k, row : row + 32, :] for k in range(8)], axis=0)
        factor = times_inverse(w, cc, kind)
        fac[2 * kind + cc] = factor
        squares = jnp.sum(factor * factor, axis=0, keepdims=True)
        return [squares[:, 0:128], squares[:, 128:256]]

    def ortho_half(cc):
        start = cc * HALF
        ow[cc] = times_inverse(raw_rows(start, WIDE), cc, 0)
        on[cc] = times_inverse(raw_rows(start + WIDE, NARROW), cc, 1)

    for chain in chains[0:2]:
        for _ in chain:
            pass
    for kind in range(2):
        for h, squares in enumerate(factor_of(0, c, kind)):
            row = pl.ds(pl.multiple_of((2 * kind + c) * 2, 2) + h, 1)
            sq[row, :] = squares
    links.finish(40)
    for chain in chains[2:4]:
        for _ in chain:
            pass
    for copy in exchanges:
        copy.wait_recv()
    for kind in range(2):
        for h, squares in enumerate(factor_of(1, 1 - c, kind)):
            row = pl.ds(pl.multiple_of((2 * kind + 1 - c) * 2, 2) + h, 1)
            sq[row, :] = squares
    sq_land[0] = sq[...]
    sends = [links.start(sq_land.at[0], sq_land.at[d], device) for d, device in others]
    ortho_half(c)
    ortho_half(1 - c)
    total = sq_land[0]
    for (d, _), copy in zip(others, sends):
        copy.wait_recv()
        total = total + sq_land[d]
    sq[...] = total
    links.finish()


def last_kernel(
    bw, bn, ow, on, fac, sq, wmo, wbo, wup, nmo, nbo, nup, f_t, b_high, b_low
):
    kinds = ((bw, ow, wmo, wbo, wup, D), (bn, on, nmo, nbo, nup, KVW))

    which, step = pl.program_id(0), pl.program_id(1)

    @pl.when(step == 0)
    def _():
        for kind in range(2):
            factor = fac[kind, which]
            basis = factor * lax.rsqrt(sq[kind, which] + 1e-6)
            kinds[kind][3][0] = basis
            f_t[kind] = factor.astype(BF16).T
            b_high[kind], b_low[kind] = split(basis.T)

    for kind, (buffer, ortho, m_out, _, update, rows) in enumerate(kinds):
        n = m_out.shape[1]
        at = pl.ds(pl.multiple_of(step * n, n), n)
        o_high, o_low = split(ortho[which, at, :])
        m_out[0] = buffer[which, at, :] - 0.05 * bf16_dot(o_high, f_t[kind])
        product = bf16_dot(o_high, b_high[kind]) + (
            bf16_dot(o_high, b_low[kind]) + bf16_dot(o_low, b_high[kind])
        )
        update[0] = ((rows * D / RANK) ** 0.5 * product).astype(BF16)


def local(wide_momentum, wide_grad, wide_basis, narrow_momentum, narrow_grad, narrow_basis):
    vmem = pl.BlockSpec(memory_space=pltpu.VMEM)
    bw = wide_momentum + wide_grad.astype(F32)
    bn = narrow_momentum + narrow_grad.astype(F32)
    copies = 192
    ow, on, fac, sq = pl.pallas_call(
        main_kernel,
        out_shape=(
            jax.ShapeDtypeStruct((2, WIDE, RANK), F32),
            jax.ShapeDtypeStruct((2, NARROW, RANK), F32),
            jax.ShapeDtypeStruct((4, COLS, RANK), F32),
            jax.ShapeDtypeStruct((8, 128), F32),
        ),
        in_specs=[vmem] * 4,
        out_specs=[vmem] * 4,
        scratch_shapes=[
            pltpu.VMEM((2 * HALF, COLS), BF16),
            pltpu.VMEM((2 * HALF, COLS), BF16),
            pltpu.VMEM((2, 2, COLS, RANK), BF16),
            pltpu.VMEM((2, 2, COLS, RANK), BF16),
            pltpu.VMEM((2, 2 * HALF, 128), F32),
            pltpu.VMEM((2, 2 * HALF, 128), F32),
            pltpu.VMEM((2, HALF, 128), F32),
            pltpu.VMEM((2, 2, 2, 4, 160, 128), F32),
            pltpu.VMEM((2, RANK, RANK), F32),
            pltpu.VMEM((RANK, RANK), F32),
            pltpu.VMEM((COLS, RANK), F32),
            pltpu.VMEM((8, 8, 128), F32),
            pltpu.VMEM((7, 8, 128), F32),
            pltpu.VMEM((2, 512, 128), F32),
            pltpu.VMEM((8, 128, RANK), F32),
            pltpu.VMEM((8, 128, RANK), F32),
            pltpu.VMEM((2, 4, 128, RANK), F32),
            pltpu.VMEM((2, 2, RANK, RANK), F32),
            pltpu.VMEM((32, 8, 128), F32),
            pltpu.SemaphoreType.DMA((copies,)),
            pltpu.SemaphoreType.DMA((copies,)),
        ],
        compiler_params=pltpu.CompilerParams(
            collective_id=0, has_side_effects=True, vmem_limit_bytes=36 * 2**20
        ),
    )(bw, bn, wide_basis, narrow_basis)

    def rows(n):
        return pl.BlockSpec((1, n, COLS), lambda m, i: (m, i, 0))

    basis_out = pl.BlockSpec((1, COLS, RANK), lambda m, i: (m, 0, 0))
    steps = 4
    w, n = WIDE // steps, NARROW // steps
    return pl.pallas_call(
        last_kernel,
        grid=(2, steps),
        out_shape=(
            jax.ShapeDtypeStruct((2, WIDE, COLS), F32),
            jax.ShapeDtypeStruct((2, COLS, RANK), F32),
            jax.ShapeDtypeStruct((2, WIDE, COLS), BF16),
            jax.ShapeDtypeStruct((2, NARROW, COLS), F32),
            jax.ShapeDtypeStruct((2, COLS, RANK), F32),
            jax.ShapeDtypeStruct((2, NARROW, COLS), BF16),
        ),
        in_specs=[
            vmem,
        ] * 6,
        out_specs=[rows(w), basis_out, rows(w), rows(n), basis_out, rows(n)],
        scratch_shapes=[pltpu.VMEM((2, RANK, COLS), BF16)] * 3,
        compiler_params=pltpu.CompilerParams(vmem_limit_bytes=24 * 2**20),
    )(
        bw, bn, ow, on,
        fac.reshape(2, 2, COLS, RANK), sq.reshape(2, 2, 1, RANK),
    )


def solution(mesh):
    return jax.shard_map(
        local,
        mesh=mesh,
        in_specs=(
            P(None, "mp", "fsdp"),
            P(None, "mp", "fsdp"),
            P(None, "fsdp", None),
            P(None, "mp", "fsdp"),
            P(None, "mp", "fsdp"),
            P(None, "fsdp", None),
        ),
        out_specs=(
            P(None, "mp", "fsdp"),
            P(None, "fsdp", None),
            P(None, "mp", "fsdp"),
            P(None, "mp", "fsdp"),
            P(None, "fsdp", None),
            P(None, "mp", "fsdp"),
        ),
        check_vma=False,
    )
```

```python
import jax
import jax.numpy as jnp
from jax import lax
from jax.experimental import pallas as pl
from jax.experimental.pallas import tpu as pltpu
from jax.sharding import PartitionSpec as P

D = 8192
KVW = 1024
RANK = 256
WIDE = 1024
NARROW = 128
COLS = 256
HALF = WIDE + NARROW
F32 = jnp.float32
BF16 = jnp.bfloat16
MESH = pl.DeviceIdType.MESH
EXACT = lax.Precision.HIGHEST

NN = (((1,), (0,)), ((), ()))
NT = (((1,), (1,)), ((), ()))
TN = (((0,), (0,)), ((), ()))


def exact_dot(a, b, dims=NN):
    return lax.dot_general(a, b, dims, precision=EXACT, preferred_element_type=F32)


def split(a):
    high = a.astype(BF16)
    return high, (a - high.astype(F32)).astype(BF16)


def bf16_dot(a, b, dims=NN):
    return lax.dot_general(a, b, dims, preferred_element_type=F32)


class Links:
    def __init__(self, send, recv):
        self.send, self.recv = send, recv
        self.count = 0
        self.started = []

    def start(self, src, dst, device):
        i = self.count
        self.count += 1
        copy = pltpu.make_async_remote_copy(
            src_ref=src,
            dst_ref=dst,
            send_sem=self.send.at[i],
            recv_sem=self.recv.at[i],
            device_id=device,
            device_id_type=MESH,
        )
        copy.start()
        self.started.append(copy)
        return copy

    def finish(self, most=None):
        n = len(self.started) if most is None else most
        for copy in self.started[:n]:
            copy.wait_send()
        self.started = self.started[n:]


def ring_reduce(links, buf, out, h, base, chunk, cut, q, peers, land):
    after, before = (q + 1) % 4, (q + 3) % 4
    right, left = peers[0], peers[2]

    def rows(c, lo, n):
        return pl.ds(pl.multiple_of(base + c * chunk + lo, 8), n)

    far = (q + 2) % 4
    a = links.start(buf.at[h, rows(far, 0, cut)], land.at[0, pl.ds(0, cut)], right)
    b = links.start(
        buf.at[h, rows(far, cut, chunk - cut)], land.at[1, pl.ds(0, chunk - cut)], left
    )
    yield
    a.wait_recv()
    buf[h, rows(after, 0, cut), :] += land[0, 0:cut, :]
    a = links.start(buf.at[h, rows(after, 0, chunk)], land.at[2, pl.ds(0, chunk)], right)
    b.wait_recv()
    buf[h, rows(before, cut, chunk - cut), :] += land[1, 0 : chunk - cut, :]
    b = links.start(buf.at[h, rows(before, 0, chunk)], land.at[3, pl.ds(0, chunk)], left)
    yield
    a.wait_recv()
    b.wait_recv()
    out[h, rows(q, 0, chunk), :] = (
        buf[h, rows(q, 0, chunk), :] + land[2, 0:chunk, :] + land[3, 0:chunk, :]
    )


def ring_gather(links, buf, h, base, chunk, cut, q, peers):
    after, before = (q + 1) % 4, (q + 3) % 4
    right, left = peers[0], peers[2]

    def part(c, lo, n):
        return buf.at[h, pl.ds(pl.multiple_of(base + c * chunk + lo, 8), n)]

    own = part(q, 0, chunk)
    a = links.start(own, own, right)
    b = links.start(own, own, left)
    yield
    a.wait_recv()
    piece = part(before, 0, cut)
    a = links.start(piece, piece, right)
    b.wait_recv()
    piece = part(after, cut, chunk - cut)
    b = links.start(piece, piece, left)
    yield
    a.wait_recv()
    b.wait_recv()


def direct_reduce(links, buf, out, h, base, chunk, q, peers, land):
    def rows(c):
        return pl.ds(pl.multiple_of(base + c * chunk, 8), chunk)

    copies = [
        links.start(buf.at[h, rows((q + d) % 4)], land.at[d, pl.ds(0, chunk)], peers[d - 1])
        for d in (2, 1, 3)
    ]
    yield
    for copy in copies:
        copy.wait_recv()
    total = buf[h, rows(q), :]
    for d in (1, 2, 3):
        total = total + land[d, 0:chunk, :]
    out[h, rows(q), :] = total


def direct_gather(links, buf, h, base, chunk, q, peers):
    own = buf.at[h, pl.ds(pl.multiple_of(base + q * chunk, 8), chunk)]
    copies = [links.start(own, own, peers[d - 1]) for d in (2, 1, 3)]
    yield
    for copy in copies:
        copy.wait_recv()


def z_reduce_gather(links, buf, out, land, lo, n, q, right, left):
    half = n // 2

    def part(ref, i, start, size):
        return ref.at[i, pl.ds(lo + start, size)]

    def chunk(ref, i):
        return part(ref, i % 8, 0, n)

    def add(i, slot, start, size):
        rows = slice(lo + start, lo + start + size)
        buf[i % 8, rows, :] += land[slot[0], slot[1], rows, :]

    a = links.start(
        part(buf, (q + 4) % 8, 0, half), part(land.at[0], 0, 0, half), right
    )
    b = links.start(
        part(buf, (q + 4) % 8, half, half), part(land.at[1], 0, half, half), left
    )
    yield
    for s in (1, 2, 3):
        size = half if s == 1 else n
        a.wait_recv()
        add(q + 4 - s, (0, s - 1), 0, size)
        a = links.start(chunk(buf, q + 4 - s), part(land.at[0], s, 0, n), right)
        b.wait_recv()
        add(q + 4 + s, (1, s - 1), n - size, size)
        b = links.start(chunk(buf, q + 4 + s), part(land.at[1], s, 0, n), left)
        yield
    a.wait_recv()
    b.wait_recv()
    rows = slice(lo, lo + n)
    out[q, rows, :] = buf[q, rows, :] + land[0, 3, rows, :] + land[1, 3, rows, :]
    a = links.start(chunk(out, q), chunk(out, q), right)
    b = links.start(chunk(out, q), chunk(out, q), left)
    yield
    for s in (1, 2):
        a.wait_recv()
        a = links.start(chunk(out, q + 8 - s), chunk(out, q + 8 - s), right)
        b.wait_recv()
        b = links.start(chunk(out, q + s), chunk(out, q + s), left)
        yield
    a.wait_recv()
    piece = part(out, (q + 5) % 8, 0, half)
    a = links.start(piece, piece, right)
    b.wait_recv()
    piece = part(out, (q + 3) % 8, half, half)
    b = links.start(piece, piece, left)
    yield
    a.wait_recv()
    b.wait_recv()


def together(first, second, after):
    done = object()
    ended = False
    while first or second:
        first = [s for s in first if next(s, done) is not done]
        if not first and not ended:
            after()
            ended = True
        second = [s for s in second if next(s, done) is not done]


def block_inverse(e):
    lane = lax.broadcasted_iota(jnp.int32, (8, 128), 1)
    sub = lax.broadcasted_iota(jnp.int32, (8, 128), 0)
    group = (lane // 64) * 64

    def pick(tile, index):
        return jnp.take_along_axis(tile, group + index, axis=1)

    e = list(e)
    for g in range(4):
        cols = [[pick(e[i], 8 * g + t) for i in range(g, 4)] for t in range(8)]
        for t in range(8):
            pivot = cols[t][0][t : t + 1, :]
            inv = pl.reciprocal(pivot, approx=True)
            inv = inv * (2.0 - pivot * inv)
            for n, i in enumerate(range(g, 4)):
                f = cols[t][n] * inv
                if n == 0:
                    f = jnp.where(sub > t, f, 0.0)
                e[i] = e[i] - f * e[g][t : t + 1, :]
                for s in range(t + 1, 8):
                    cols[s][n] = cols[s][n] - f * cols[s][0][t : t + 1, :]
    return [tile * lax.rsqrt(pick(tile, 8 * i + sub)) for i, tile in enumerate(e)]


def invert_factor(a_ref, out, after):
    lane = lax.broadcasted_iota(jnp.int32, (32, 128), 1)
    row = lax.broadcasted_iota(jnp.int32, (32, 128), 0)
    eye = jnp.where(lane % 32 == row, 1.0, 0.0)
    col = lax.broadcasted_iota(jnp.int32, (32, 256), 1)
    wide_row = lax.broadcasted_iota(jnp.int32, (32, 256), 0)

    def turned(v, by):
        return pltpu.roll(v, by % 128, 1) if by % 128 else v

    blocks = [a_ref[m, 0:32, 0:128] for m in range(2)]
    panels = None
    for k in range(8):
        at, below = 32 * k, 32 * k + 32
        base, low = at // 128 * 128, below // 128 * 128
        if k > 0:
            for m in range(2):
                change = exact_dot(panels[m][:, base:256], panels[m], TN)
                under = lax.broadcasted_iota(jnp.int32, (256 - at, 256), 1)
                rest = jnp.where(
                    (under >= at - 32) & (under < at), 0.0, a_ref[m, at:256, :]
                )
                a_ref[m, at:256, :] = rest - change[at - base :, :]
        d0, d1 = turned(blocks[0], base - at), turned(blocks[1], 64 + base - at)
        e = jnp.where(lane < 32, d0, jnp.where((lane >= 64) & (lane < 96), d1, eye))
        e = jnp.concatenate(
            block_inverse([e[8 * i : 8 * i + 8] for i in range(4)]), axis=0
        )
        inside = (col >= at) & (col < below)
        wide_eye = jnp.where(col - at == wide_row, 1.0, 0.0)
        panels, blocks = [], []
        for m in range(2):
            t = turned(e, 96 - 64 * m)[:, 0:32]
            panel = exact_dot(t, jnp.where(inside, wide_eye, a_ref[m, at:below, :]))
            panels.append(panel)
            if below < 256:
                near = panel[:, low : low + 128]
                change = exact_dot(near, near, TN)
                blocks.append(
                    a_ref[m, below : below + 32, low : low + 128]
                    - change[below - low : below - low + 32, :]
                )
            a_ref[m, at:below, :] = panel
            out[m, at:below, :] = jnp.where(col <= at + wide_row, panel, 0.0)
        after(k)


def main_kernel(
    bw, bn, wb, nb,
    ow, on, fac, sq,
    bh, bl, vh, vl, part, full, swap, land, gram, cross, w_first, slices, zland, gathered,
    wpart, wfull, wland, inverse, sq_land,
    send, recv,
):
    z = lax.axis_index("mp")
    f = lax.axis_index("fsdp")
    c = f % 2
    x = (f // 2) % 4
    y = f // 8

    def plane(xx, yy, cc):
        return {"fsdp": ((yy % 4) * 4 + xx % 4) * 2 + cc}

    sibling = plane(x, y, 1 - c)
    xs = [plane(x + d, y, c) for d in (1, 2, 3)]
    others = [(d, {"fsdp": (f + d) % 32}) for d in range(1, 32)]
    ys = [plane(x, y + d, c) for d in (1, 2, 3)]
    zs = [{"mp": (z + d) % 8} for d in range(1, 8)]

    barrier = pltpu.get_barrier_semaphore()
    partners = [device for _, device in others] + zs
    for device in partners:
        pl.semaphore_signal(barrier, inc=1, device_id=device, device_id_type=MESH)

    links = Links(send, recv)
    sets = ((0, 640), (640, 512))
    wide_b = WIDE - 640

    def split_basis(cc):
        for kind, basis in enumerate((wb, nb)):
            high, low = split(basis[cc])
            vh[cc, kind] = high
            vl[cc, kind] = low

    def raw_rows_of(cc, kind, r, n, buffer):
        rows = pl.ds(pl.multiple_of(cc * HALF + r, 16), n)
        high, low = split(buffer)
        bh[rows, :] = high
        bl[rows, :] = low
        v_high = vh[cc, kind]
        raw = bf16_dot(high, v_high) + (bf16_dot(high, vl[cc, kind]) + bf16_dot(low, v_high))
        part[0, rows, :] = raw[:, 0:128]
        part[1, rows, :] = raw[:, 128:256]

    def raw_set(cc, i):
        lo, n = ((0, 640), (640, wide_b))[i]
        raw_rows_of(cc, 0, lo, n, bw[cc, lo : lo + n, :])

        if i == 1:
            raw_rows_of(cc, 1, WIDE, NARROW, bn[cc])

    def half_rows(cc, start, n):
        return pl.ds(pl.multiple_of(cc * HALF + start, 8), n)

    split_basis(1 - c)
    raw_set(1 - c, 0)
    pl.semaphore_wait(barrier, len(partners))
    exchanges = []
    for i, (start, n) in enumerate(sets):
        if i == 1:
            raw_set(1 - c, 1)
        exchanges.append(
            links.start(
                part.at[:, half_rows(1 - c, start, n)], swap.at[:, pl.ds(start, n)], sibling
            )
        )
    split_basis(c)

    x_ring = dict(q=x, peers=xs)
    y_ring = dict(q=y, peers=ys)
    base = c * HALF

    def gather_both(buffer, h, start, sizes, first, second):
        yield from direct_gather(
            links, buffer, h, start + first["q"] * sizes[0], sizes[1], **second
        )
        yield from ring_gather(links, buffer, h, start, sizes[0], sizes[0] // 2, **first)

    shares = []

    def whole_sum(i, h):
        start, n = sets[i]
        big, small = n // 4, n // 16
        first, second = (x_ring, y_ring) if h == 0 else (y_ring, x_ring)
        yield from ring_reduce(
            links, part, part, h, base + start, big, big // 2, land=land.at[i, h, 0], **first
        )
        yield from direct_reduce(
            links, part, full, h, base + start + first["q"] * big, small,
            land=land.at[i, h, 1], **second
        )
        yield from gather_both(full, h, base + start, (big, small), first, second)
        done = full.at[h, half_rows(c, start, n)]
        shares.append(links.start(done, done, sibling))

    stages = []
    for i, (start, n) in enumerate(sets):
        raw_set(c, i)
        exchanges[i].wait_recv()
        rows = half_rows(c, start, n)
        part[:, rows, :] += swap[:, start : start + n, :]
        for h in range(2):
            stage = whole_sum(i, h)
            next(stage)
            stages.append(stage)

    def raw_rows(start, n):
        rows = pl.ds(pl.multiple_of(start, 8), n)
        return jnp.concatenate([full[0, rows, :], full[1, rows, :]], axis=1)

    def own_gram(start, n):
        raw = raw_rows(base + start, n)
        high = raw.astype(BF16)
        middle, low = split(raw - high.astype(F32))
        cross[...] = bf16_dot(high, middle, TN) + bf16_dot(high, low, TN)
        mirrored = cross[...] + cross[...].T
        return bf16_dot(high, high, TN) + (mirrored + bf16_dot(middle, middle, TN))

    def w_of(cc, start, n):
        start = cc * HALF + start
        rows = pl.ds(pl.multiple_of(start, 16), n)
        high, low = split(raw_rows(start, n))
        b_high = bh[rows, :]
        return bf16_dot(b_high, high, TN) + (
            bf16_dot(b_high, low, TN) + bf16_dot(bl[rows, :], high, TN)
        )

    def first_set():
        gram[0] = own_gram(0, 640)
        w_first[...] = w_of(c, 0, 640)

    together(stages[0:2], stages[2:4], after=first_set)
    def put_w(i, kind, w):
        row = i * 64 + kind * 32
        for k in range(8):
            wpart[k, row : row + 32, :] = w[k * 32 : k * 32 + 32, :]

    chains = []

    def z_chain(i, kind, w):
        put_w(i, kind, w)
        row = i * 64 + kind * 32
        chain = z_reduce_gather(links, wpart, wfull, wland, row, 32, z, zs[0], zs[6])
        next(chain)
        chains.append(chain)

    z_chain(0, 0, w_first[...] + w_of(c, 640, wide_b))
    z_chain(0, 1, w_of(c, WIDE, NARROW))

    gram[0] += own_gram(640, wide_b)
    gram[1] = own_gram(WIDE, NARROW)

    places = (x * 4 + y, y * 4 + x)
    for t in range(8):
        h, m, r = t // 4, (t // 2) % 2, t % 2
        rows = pl.ds(pl.multiple_of(places[h] * 16 + r * 8, 8), 8)
        slices[t] = gram[m, rows, h * 128 : h * 128 + 128]
    gram_sends = [
        links.start(slices.at[(z + d) % 8], zland.at[d - 1], zs[d - 1]) for d in range(1, 8)
    ]

    for copy in shares:
        copy.wait_recv()
    z_chain(1, 0, w_of(1 - c, 0, WIDE))
    z_chain(1, 1, w_of(1 - c, WIDE, NARROW))

    def z_step():
        for chain in chains:
            next(chain, None)

    for copy in gram_sends:
        copy.wait_recv()
    total = slices[z]
    for d in range(7):
        total = total + zland[d]
    place = places[0] + (z // 4) * (places[1] - places[0])
    own = gathered.at[z // 4, pl.ds(pl.multiple_of(place * 32 + (z % 4) * 8, 8), 8)]
    own[...] = total
    gram_sends = [links.start(own, own, zs[d]) for d in range(7)]
    z_step()
    for copy in gram_sends:
        copy.wait_recv()
    def gather_gram(h, first, second):
        yield from direct_gather(links, gathered, h, first["q"] * 128, 32, **second)
        yield from direct_gather(links, gathered, h, 0, 128, **first)

    stages = [gather_gram(0, x_ring, y_ring), gather_gram(1, y_ring, x_ring)]
    for i in range(3):
        for stage in stages:
            next(stage, None)
        if i < 2:
            links.finish(40)
        z_step()
    for h in range(2):
        for p in range(16):
            for m in range(2):
                gram[m, p * 16 : p * 16 + 16, h * 128 : h * 128 + 128] = gathered[
                    h, p * 32 + m * 16 : p * 32 + m * 16 + 16, :
                ]

    exchanges = []

    def after_block(k):
        if k % 2:
            done = inverse.at[c, :, pl.ds(32 * (k - 1), 64)]
            exchanges.append(links.start(done, done, sibling))
        else:
            z_step()

    invert_factor(gram, inverse.at[c], after_block)
    def times_inverse(a, cc, kind):
        i_high, i_low = split(inverse[cc, kind])
        high, low = split(a)
        return bf16_dot(high, i_high, NT) + (
            bf16_dot(high, i_low, NT) + bf16_dot(low, i_high, NT)
        )

    def factor_of(i, cc, kind):
        row = i * 64 + kind * 32
        w = jnp.concatenate([wfull[k, row : row + 32, :] for k in range(8)], axis=0)
        factor = times_inverse(w, cc, kind)
        fac[2 * kind + cc] = factor
        squares = jnp.sum(factor * factor, axis=0, keepdims=True)
        return [squares[:, 0:128], squares[:, 128:256]]

    def ortho_half(cc):
        start = cc * HALF
        ow[cc] = times_inverse(raw_rows(start, WIDE), cc, 0)
        on[cc] = times_inverse(raw_rows(start + WIDE, NARROW), cc, 1)

    for chain in chains[0:2]:
        for _ in chain:
            pass
    for kind in range(2):
        for h, squares in enumerate(factor_of(0, c, kind)):
            row = pl.ds(pl.multiple_of((2 * kind + c) * 2, 2) + h, 1)
            sq[row, :] = squares
    for chain in chains[2:4]:
        for _ in chain:
            pass
    for copy in exchanges:
        copy.wait_recv()
    for kind in range(2):
        for h, squares in enumerate(factor_of(1, 1 - c, kind)):
            row = pl.ds(pl.multiple_of((2 * kind + 1 - c) * 2, 2) + h, 1)
            sq[row, :] = squares
    sq_land[0] = sq[...]
    sends = [links.start(sq_land.at[0], sq_land.at[d], device) for d, device in others]
    ortho_half(c)
    ortho_half(1 - c)
    total = sq_land[0]
    for (d, _), copy in zip(others, sends):
        copy.wait_recv()
        total = total + sq_land[d]
    sq[...] = total
    links.finish()


def last_kernel(
    bw, bn, ow, on, fac, sq, wmo, wbo, wup, nmo, nbo, nup, f_t, b_high, b_low
):
    kinds = ((bw, ow, wmo, wbo, wup, D), (bn, on, nmo, nbo, nup, KVW))

    which, step = pl.program_id(0), pl.program_id(1)

    @pl.when(step == 0)
    def _():
        for kind in range(2):
            factor = fac[kind, which]
            basis = factor * lax.rsqrt(sq[kind, which] + 1e-6)
            kinds[kind][3][0] = basis
            f_t[kind] = factor.astype(BF16).T
            b_high[kind], b_low[kind] = split(basis.T)

    for kind, (buffer, ortho, m_out, _, update, rows) in enumerate(kinds):
        n = m_out.shape[1]
        at = pl.ds(pl.multiple_of(step * n, n), n)
        o_high, o_low = split(ortho[which, at, :])
        m_out[0] = buffer[which, at, :] - 0.05 * bf16_dot(o_high, f_t[kind])
        product = bf16_dot(o_high, b_high[kind]) + (
            bf16_dot(o_high, b_low[kind]) + bf16_dot(o_low, b_high[kind])
        )
        update[0] = ((rows * D / RANK) ** 0.5 * product).astype(BF16)


def local(wide_momentum, wide_grad, wide_basis, narrow_momentum, narrow_grad, narrow_basis):
    vmem = pl.BlockSpec(memory_space=pltpu.VMEM)
    bw = wide_momentum + wide_grad.astype(F32)
    bn = narrow_momentum + narrow_grad.astype(F32)
    copies = 192
    ow, on, fac, sq = pl.pallas_call(
        main_kernel,
        out_shape=(
            jax.ShapeDtypeStruct((2, WIDE, RANK), F32),
            jax.ShapeDtypeStruct((2, NARROW, RANK), F32),
            jax.ShapeDtypeStruct((4, COLS, RANK), F32),
            jax.ShapeDtypeStruct((8, 128), F32),
        ),
        in_specs=[vmem] * 4,
        out_specs=[vmem] * 4,
        scratch_shapes=[
            pltpu.VMEM((2 * HALF, COLS), BF16),
            pltpu.VMEM((2 * HALF, COLS), BF16),
            pltpu.VMEM((2, 2, COLS, RANK), BF16),
            pltpu.VMEM((2, 2, COLS, RANK), BF16),
            pltpu.VMEM((2, 2 * HALF, 128), F32),
            pltpu.VMEM((2, 2 * HALF, 128), F32),
            pltpu.VMEM((2, HALF, 128), F32),
            pltpu.VMEM((2, 2, 2, 4, 160, 128), F32),
            pltpu.VMEM((2, RANK, RANK), F32),
            pltpu.VMEM((RANK, RANK), F32),
            pltpu.VMEM((COLS, RANK), F32),
            pltpu.VMEM((8, 8, 128), F32),
            pltpu.VMEM((7, 8, 128), F32),
            pltpu.VMEM((2, 512, 128), F32),
            pltpu.VMEM((8, 128, RANK), F32),
            pltpu.VMEM((8, 128, RANK), F32),
            pltpu.VMEM((2, 4, 128, RANK), F32),
            pltpu.VMEM((2, 2, RANK, RANK), F32),
            pltpu.VMEM((32, 8, 128), F32),
            pltpu.SemaphoreType.DMA((copies,)),
            pltpu.SemaphoreType.DMA((copies,)),
        ],
        compiler_params=pltpu.CompilerParams(
            collective_id=0, has_side_effects=True, vmem_limit_bytes=36 * 2**20
        ),
    )(bw, bn, wide_basis, narrow_basis)

    def rows(n):
        return pl.BlockSpec((1, n, COLS), lambda m, i: (m, i, 0))

    basis_out = pl.BlockSpec((1, COLS, RANK), lambda m, i: (m, 0, 0))
    steps = 1
    w, n = WIDE // steps, NARROW // steps
    return pl.pallas_call(
        last_kernel,
        grid=(2, steps),
        out_shape=(
            jax.ShapeDtypeStruct((2, WIDE, COLS), F32),
            jax.ShapeDtypeStruct((2, COLS, RANK), F32),
            jax.ShapeDtypeStruct((2, WIDE, COLS), BF16),
            jax.ShapeDtypeStruct((2, NARROW, COLS), F32),
            jax.ShapeDtypeStruct((2, COLS, RANK), F32),
            jax.ShapeDtypeStruct((2, NARROW, COLS), BF16),
        ),
        in_specs=[
            vmem,
        ] * 6,
        out_specs=[rows(w), basis_out, rows(w), rows(n), basis_out, rows(n)],
        scratch_shapes=[pltpu.VMEM((2, RANK, COLS), BF16)] * 3,
        compiler_params=pltpu.CompilerParams(vmem_limit_bytes=24 * 2**20),
    )(
        bw, bn, ow, on,
        fac.reshape(2, 2, COLS, RANK), sq.reshape(2, 2, 1, RANK),
    )


def solution(mesh):
    return jax.shard_map(
        local,
        mesh=mesh,
        in_specs=(
            P(None, "mp", "fsdp"),
            P(None, "mp", "fsdp"),
            P(None, "fsdp", None),
            P(None, "mp", "fsdp"),
            P(None, "mp", "fsdp"),
            P(None, "fsdp", None),
        ),
        out_specs=(
            P(None, "mp", "fsdp"),
            P(None, "fsdp", None),
            P(None, "mp", "fsdp"),
            P(None, "mp", "fsdp"),
            P(None, "fsdp", None),
            P(None, "mp", "fsdp"),
        ),
        check_vma=False,
    )
```
